512 devices in a mesh: gx: 32 (over z_lo, y, core), gy: 16 (over x, z_hi).
Axes of the slice: x: 4, y: 4, z: 16 (z_hi: 4, z_lo: 4; z = z_hi * 4 + z_lo), core: 2. Of those that a mesh axis runs over, the one named last changes fastest.
Arguments:
- fine_now: float32 [3, 8, 512, 4096], P(None, None, 'gx', 'gy'), may hold values from -6 to 6
- fine_before: float32 [3, 8, 512, 4096], P(None, None, 'gx', 'gy'), may hold values from -6 to 6
- fine_density: float32 [8, 512, 4096], P(None, 'gx', 'gy'), may hold values from 1.5 to 3
- fine_shear: float32 [8, 512, 4096], P(None, 'gx', 'gy'), may hold values from 0.3 to 1.5
- fine_lame: float32 [8, 512, 4096], P(None, 'gx', 'gy'), may hold values from 0.3 to 3
- coarse_now: float32 [3, 8, 256, 2048], P(None, None, 'gx', 'gy'), may hold values from -6 to 6
- coarse_before: float32 [3, 8, 256, 2048], P(None, None, 'gx', 'gy'), may hold values from -6 to 6
- coarse_density: float32 [8, 256, 2048], P(None, 'gx', 'gy'), may hold values from 1.5 to 3
- coarse_shear: float32 [8, 256, 2048], P(None, 'gx', 'gy'), may hold values from 0.3 to 1.5
- coarse_lame: float32 [8, 256, 2048], P(None, 'gx', 'gy'), may hold values from 0.3 to 3
Outputs:
- fine_next: float32 [3, 8, 512, 4096], P(None, None, 'gx', 'gy')
- coarse_next: float32 [3, 8, 256, 2048], P(None, None, 'gx', 'gy')
- reduction: float32 [], replicated
The draws below stay inside these ranges and needn't reach their ends.
All inputs are finite; a program needn't handle non-finite values. Where the reference program divides by a largest or mean magnitude, that divisor is 1e-20 or more.
Results may differ from the reference program's by a relative error of at most 0.000023.
Values sent between devices are 32-bit elements; how exact they have to be, the bound alone decides.
No kernel may reach another device: no remote copies, remote signals or barrier semaphores. Data moves between devices by JAX's collectives and lax.ppermute only.
A program may use at most 64 MiB of HBM per device.

```python
import math
import jax
import jax.numpy as jnp
from jax import lax

NZF = 8
NZC = 8
ITERS = 3
NXF = 512
NYF = 4096
NXC = 256
NYC = 2048


def block_scale(key, shape, cuts, low, largest):
    def one(dim, parts):
        draws = jax.random.uniform(jax.random.fold_in(jax.random.fold_in(key, 6), dim), (parts,), jnp.float32, low / len(cuts), largest / len(cuts))
        return jnp.repeat(jnp.exp(draws), shape[dim] // parts).reshape((-1,) + (1,) * (len(shape) - dim - 1))

    level = one(*cuts[0])
    for cut in cuts[1:]:
        level = level * one(*cut)
    return level


def scatter_about(stream_key, extent, width, most, split=(), kind=jnp.bfloat16):
    factor_of = block_scale(stream_key, extent, split, -0.22, 0.18) if split else 1.0
    drawn = jax.random.normal(stream_key, extent, jnp.float32) * width * factor_of
    return jnp.minimum(jnp.maximum(drawn, -most), most).astype(kind)


def setup_inputs(seed: int = 0) -> dict:
    arg_keys = jax.random.split(jax.random.key(seed), 11)
    return {
        "fine_now": scatter_about(arg_keys[0], (3, NZF, NXF, NYF), 1.0, 6.0, ((2, 32), (3, 16)), jnp.float32),
        "fine_before": scatter_about(arg_keys[1], (3, NZF, NXF, NYF), 1.0, 6.0, ((2, 32), (3, 16)), jnp.float32),
        "fine_density": jnp.clip(1.5 + 1.5 * jax.random.uniform(arg_keys[2], (NZF, NXF, NYF), jnp.float32) ** block_scale(arg_keys[2], (NZF, NXF, NYF), ((1, 32), (2, 16)), -0.2, 0.2), 1.5, 3.0),
        "fine_shear": jnp.clip(jnp.exp(math.log(1.5) - 1.60943787 * jax.random.uniform(arg_keys[3], (NZF, NXF, NYF), jnp.float32) ** block_scale(arg_keys[3], (NZF, NXF, NYF), ((1, 32), (2, 16)), -0.2, 0.2)), 0.3, 1.5),
        "fine_lame": jnp.clip(jnp.exp(math.log(3.0) - 2.3025851 * jax.random.uniform(arg_keys[4], (NZF, NXF, NYF), jnp.float32) ** block_scale(arg_keys[4], (NZF, NXF, NYF), ((1, 32), (2, 16)), -0.2, 0.2)), 0.3, 3.0),
        "coarse_now": scatter_about(arg_keys[5], (3, NZC, NXC, NYC), 1.0, 6.0, ((2, 32), (3, 16)), jnp.float32),
        "coarse_before": scatter_about(arg_keys[6], (3, NZC, NXC, NYC), 1.0, 6.0, ((2, 32), (3, 16)), jnp.float32),
        "coarse_density": jnp.clip(1.5 + 1.5 * jax.random.uniform(arg_keys[7], (NZC, NXC, NYC), jnp.float32) ** block_scale(arg_keys[7], (NZC, NXC, NYC), ((1, 32), (2, 16)), -0.2, 0.2), 1.5, 3.0),
        "coarse_shear": jnp.clip(jnp.exp(math.log(1.5) - 1.60943787 * jax.random.uniform(arg_keys[8], (NZC, NXC, NYC), jnp.float32) ** block_scale(arg_keys[8], (NZC, NXC, NYC), ((1, 32), (2, 16)), -0.2, 0.2)), 0.3, 1.5),
        "coarse_lame": jnp.clip(jnp.exp(math.log(3.0) - 2.3025851 * jax.random.uniform(arg_keys[9], (NZC, NXC, NYC), jnp.float32) ** block_scale(arg_keys[9], (NZC, NXC, NYC), ((1, 32), (2, 16)), -0.2, 0.2)), 0.3, 3.0),
    }


def first_diff(field, along, spacing):
    length = field.shape[along] - 4

    def piece(start):
        return lax.slice_in_dim(field, start, start + length, axis=along)
    return (piece(0) - 8.0 * piece(1) + 8.0 * piece(3) - piece(4)) / (12.0 * spacing)

def second_diff(field, along, spacing):
    length = field.shape[along] - 4

    def piece(start):
        return lax.slice_in_dim(field, start, start + length, axis=along)
    return (-piece(0) + 16.0 * piece(1) - 30.0 * piece(2) + 16.0 * piece(3) - piece(4)) / (12.0 * spacing * spacing)

def vertical_first(field, spacing):
    return (field[2:] - field[:-2]) / (2.0 * spacing)

def vertical_second(field, spacing):
    return (field[2:] - 2.0 * field[1:-1] + field[:-2]) / (spacing * spacing)

def laplace(field, spacing):
    return second_diff(field[1:-1, :, 2:-2], 1, spacing) + second_diff(field[1:-1, 2:-2, :], 2, spacing) + vertical_second(field[:, 2:-2, 2:-2], spacing)

def elastic(extended, shear, lame_param, spacing, slope_x, slope_y):
    comp_x, comp_y, comp_z = (extended[0], extended[1], extended[2])
    vert_z = vertical_first(comp_z, spacing)
    div_x = second_diff(comp_x[1:-1, :, 2:-2], 1, spacing) + first_diff(slope_y, 1, spacing) + first_diff(vert_z[:, :, 2:-2], 1, spacing)
    div_y = first_diff(slope_x, 1, spacing) + second_diff(comp_y[1:-1, 2:-2, :], 2, spacing) + first_diff(vert_z[:, 2:-2, :], 2, spacing)
    across_x = first_diff(comp_x[:, :, 2:-2], 1, spacing)
    across_y = first_diff(comp_y[:, 2:-2, :], 2, spacing)
    div_z = vertical_first(across_x, spacing) + vertical_first(across_y, spacing) + vertical_second(comp_z[:, 2:-2, 2:-2], spacing)
    bulk = lame_param + shear
    return jnp.stack([shear * laplace(comp_x, spacing) + bulk * div_x, shear * laplace(comp_y, spacing) + bulk * div_y, shear * laplace(comp_z, spacing) + bulk * div_z])

def wave(lame_param, shear, density):
    return jnp.sqrt((lame_param + 2.0 * shear) / density)

def modulus(shear, lame_param):
    return jnp.stack([shear, shear, lame_param + 2.0 * shear])

def refine(field, along):
    length = field.shape[along]
    even_rows = lax.slice_in_dim(field, 0, length - 1, axis=along)
    next_rows = lax.slice_in_dim(field, 1, length, axis=along)
    odd_rows = 0.5 * (even_rows + next_rows)
    woven = jnp.stack([even_rows, odd_rows], axis=along + 1)
    shape = list(field.shape)
    shape[along] = 2 * (length - 1)
    woven = woven.reshape(shape)
    tail = lax.slice_in_dim(field, length - 1, length, axis=along)
    joined = jnp.concatenate([woven, tail], axis=along)
    return lax.slice_in_dim(joined, 1, 2 * length - 1, axis=along)

def prolong(padded):
    return refine(refine(padded, 1), 2)

def restrict_once(field, along):
    length = field.shape[along]
    left = lax.slice_in_dim(field, 0, length - 2, 2, axis=along)
    centre = lax.slice_in_dim(field, 1, length - 1, 2, axis=along)
    right = lax.slice_in_dim(field, 2, length, 2, axis=along)
    return 0.25 * left + 0.5 * centre + 0.25 * right

def restrict(field):
    return restrict_once(restrict_once(field, 1), 2)

def pad_plane(plane):
    return jnp.pad(plane, ((0, 0), (1, 1), (1, 1)))

def advance(extended, now, before, density, shear, lame_param, spacing, time_step):

    def one_layer(layer):
        slab = lax.dynamic_slice_in_dim(extended, layer, 3, axis=1)
        slope_x = first_diff(slab[0, 1:-1], 2, spacing)
        slope_y = first_diff(slab[1, 1:-1], 2, spacing)
        accel = elastic(slab, lax.dynamic_slice_in_dim(shear, layer, 1, 0), lax.dynamic_slice_in_dim(lame_param, layer, 1, 0), spacing, slope_x, slope_y)
        present = lax.dynamic_slice_in_dim(now, layer, 1, 1)
        earlier = lax.dynamic_slice_in_dim(before, layer, 1, 1)
        weight = lax.dynamic_slice_in_dim(density, layer, 1, 0)
        return 2.0 * present - earlier + time_step * time_step * accel / weight
    layers = jnp.arange(now.shape[1], dtype=jnp.int32)
    stacked = lax.map(one_layer, layers)
    return jnp.moveaxis(stacked[:, :, 0], 0, 1)

def reference(fine_now, fine_before, fine_density, fine_shear, fine_lame, coarse_now, coarse_before, coarse_density, coarse_shear, coarse_lame):
    wave_peak = jnp.maximum(jnp.max(wave(fine_lame, fine_shear, fine_density)), 0.5 * jnp.max(wave(coarse_lame, coarse_shear, coarse_density)))
    time_step = 0.3 / wave_peak
    fine_pad = jnp.pad(fine_now, ((0, 0), (0, 0), (2, 2), (2, 2)))
    fine_ext = jnp.concatenate([fine_pad[:, 1:2], fine_pad], axis=1)
    fine_new = advance(fine_ext, fine_now[:, :-1], fine_before[:, :-1], fine_density[:-1], fine_shear[:-1], fine_lame[:-1], 1.0, time_step)
    coarse_pad = jnp.pad(coarse_now, ((0, 0), (0, 0), (2, 2), (2, 2)))
    coarse_ext = jnp.concatenate([coarse_pad, jnp.zeros_like(coarse_pad[:, :1])], axis=1)
    coarse_new = advance(coarse_ext, coarse_now[:, 1:], coarse_before[:, 1:], coarse_density[1:], coarse_shear[1:], coarse_lame[1:], 2.0, time_step)
    above = fine_new[:, -1]
    below = coarse_new[:, 0]
    fine_modulus = modulus(fine_shear[-1], fine_lame[-1])
    coarse_modulus = modulus(coarse_shear[0], coarse_lame[0])
    modulus_pad = pad_plane(fine_modulus)
    above_pad = pad_plane(above)
    jacobi_diag = 0.5 * coarse_modulus + 0.5625 * restrict(modulus_pad)

    def mismatch_of(interface):
        refined = prolong(pad_plane(interface))
        return (0.5 * coarse_modulus * (interface - below) + restrict(modulus_pad * (refined - above_pad)), refined)
    interface = 2.0 * coarse_now[:, 0] - coarse_before[:, 0]
    mismatch, refined = mismatch_of(interface)
    first_max = jnp.max(jnp.abs(mismatch))
    for sweep in range(ITERS):
        interface = interface - mismatch / jacobi_diag
        mismatch, refined = mismatch_of(interface)
    last_max = jnp.max(jnp.abs(mismatch))
    fine_next = jnp.concatenate([fine_new, refined[:, 1:-1, 1:-1][:, None]], axis=1)
    coarse_next = jnp.concatenate([interface[:, None], coarse_new], axis=1)
    return (fine_next, coarse_next, last_max / (first_max + 1e-06))
```

```python
import jax
import jax.numpy as jnp
import ml_dtypes
import numpy as np
from jax import lax
from jax.experimental import pallas as pl
from jax.experimental.pallas import tpu as pltpu
from jax.sharding import PartitionSpec as P

ITERS = 3
LANES = 128
NAMES = ("fn", "fb", "fd", "fs", "fl", "cn", "cb", "cd", "cs", "cl")

DEEP_NOW = [("fn", (c, k)) for c in range(3) for k in (5, 6, 7)]
THIN_NOW = [("fn", (c, k)) for c in range(3) for k in range(5)]
DEEP_REST = [("fb", (c, 6)) for c in range(3)] + [("fd", (6,)), ("fs", (6,)), ("fl", (6,)), ("fs", (7,)), ("fl", (7,))]
COARSE_NOW = [("cn", (c, k)) for c in range(3) for k in range(3)]
COARSE_REST = [("cb", (c, k)) for c in range(3) for k in range(2)] + [
    ("cd", (1,)),
    ("cs", (0,)),
    ("cl", (0,)),
    ("cs", (1,)),
    ("cl", (1,)),
]
COARSE_THIN = [("cn", (c, k)) for c in range(3) for k in range(3, 8)]

TILE_ROWS = {"A": (0, 16), "B": (16, 16), "C": (32, 8)}
TILE_RIM = {"A": 9, "B": 7, "C": 5}
PACKED_ROWS = 40


def plan():
    entries, lane, row = [], {"A": 0, "B": 0, "C": 0}, 0
    for tile, keys, low, high in (
        ("A", DEEP_NOW, 9, 8),
        ("A", THIN_NOW, 2, 2),
        ("B", DEEP_REST, 7, 6),
        ("C", COARSE_NOW, 5, 5),
        ("C", COARSE_REST, 4, 4),
        ("C", COARSE_THIN, 2, 2),
    ):
        for key in keys:
            own = 1 if tile == "C" else 2
            entries.append((key, low, high, tile, lane[tile], row, own))
            lane[tile] += low
            row += own * low
    corners = []
    for tile in "ABC":
        for side in range(2):
            corners.append((tile, side, row))
            row += TILE_RIM[tile]
    return entries, corners, -(-row // 8) * 8


ENTRIES, CORNERS, RIM_ROWS = plan()

SLOTS = 31
PEAK_LANE = 31
FLAG_LANE = 63
STEP_LOW = 0.02
FAR = -1.0e30


def iota(shape, dim):
    return lax.broadcasted_iota(jnp.int32, shape, dim)


def turned(value, steps, axis):
    size = value.shape[axis]
    steps = steps % size
    return value if steps == 0 else pltpu.roll(value, steps, axis)


def own_tile(refs, key, tile):
    name, index = key
    return refs[name][index + (slice(None), slice(tile * LANES, (tile + 1) * LANES))]


def pack_columns(*refs):
    named = dict(zip(NAMES, refs[:10]))
    low_out, high_out = refs[10:]
    for tile, (base, rows) in TILE_ROWS.items():
        lane = iota((rows, LANES), 1)
        low_sum = jnp.zeros((rows, LANES), jnp.float32)
        high_sum = low_sum
        for key, low, _, where, at, _, own in ENTRIES:
            if where != tile:
                continue
            inside = (lane >= at) & (lane < at + low)
            low_sum = jnp.where(inside, turned(own_tile(named, key, own - 1), at + low, 1), low_sum)
            high_sum = jnp.where(inside, turned(own_tile(named, key, 0), at, 1), high_sum)
        low_out[base : base + rows, :] = low_sum
        high_out[base : base + rows, :] = high_sum


def pack_rows(*refs):
    named = dict(zip(NAMES, refs[:10]))
    sides = refs[10:12]
    low_out, high_out = refs[12:]
    low_out[RIM_ROWS - 8 :, :] = jnp.zeros((8, LANES), jnp.float32)
    high_out[RIM_ROWS - 8 :, :] = jnp.zeros((8, LANES), jnp.float32)
    for (name, index), low, high, _, _, row, own in ENTRIES:
        ref = named[name]
        rows = ref.shape[-2]
        for tile in range(own):
            lanes = slice(tile * LANES, (tile + 1) * LANES)
            start = row + tile * low
            low_out[start : start + low, :] = ref[index + (slice(rows - low, rows), lanes)]
            high_out[start : start + high, :] = ref[index + (slice(0, high), lanes)]
            if high < low:
                high_out[start + high : start + low, :] = jnp.zeros((low - high, LANES), jnp.float32)
    for tile, side, row in CORNERS:
        base, rows = TILE_ROWS[tile]
        rim = TILE_RIM[tile]
        low_out[row : row + rim, :] = sides[side][base + rows - rim : base + rows, :]
        high_out[row : row + rim, :] = sides[side][base : base + rim, :]


def across(tiles, steps, wanted):
    count = len(tiles)
    lane = iota(tiles[0].shape, 1)
    rolled = [turned(tile, -steps, 1) for tile in tiles]
    if steps > 0:
        return [jnp.where(lane < LANES - steps, rolled[t], rolled[(t + 1) % count]) for t in range(wanted)]
    return [jnp.where(lane >= -steps, rolled[t], rolled[(t - 1) % count]) for t in range(wanted)]


def first_of(down2, down1, up1, up2, spacing):
    return (8.0 * (up1 - down1) - (up2 - down2)) * (1.0 / (12.0 * spacing))


def second_of(down2, down1, here, up1, up2, spacing):
    return (16.0 * (up1 + down1) - (up2 + down2) - 30.0 * here) * (1.0 / (12.0 * spacing * spacing))


def across_all(tiles, wanted):
    return [across(tiles, steps, wanted) for steps in (-2, -1, 1, 2)]


def slopes(field, along_x, along_y, plane, start, rows, wanted, spacing):
    count = field.shape[2]
    for t in range(count):
        down2, down1, up1, up2 = (field[0, plane, t, pl.ds(start + d, rows), :] for d in (-2, -1, 1, 2))
        along_x[plane, t, start : start + rows, :] = first_of(down2, down1, up1, up2, spacing)
    span = slice(start - 4, start + rows + 4)
    shifted = across_all([field[1, plane, t, span, :] for t in range(count)], wanted)
    for t in range(wanted):
        along_y[plane, t, span, :] = first_of(*(s[t] for s in shifted), spacing)


def acceleration(field, along_x, along_y, mixed, planes, start, rows, wanted, spacing, shear, lame):
    above, plane, under = planes
    count = field.shape[2]
    half = 1.0 / (2.0 * spacing)
    square = 1.0 / (spacing * spacing)
    span = slice(start, start + rows)
    wide = slice(start - 4, start + rows + 4)
    for t in range(wanted):
        mixed[t, wide, :] = along_y[plane, t, wide, :] + half * (
            field[2, under, t, wide, :] - field[2, above, t, wide, :]
        )
    twist = [
        along_x[plane, t, span, :] + half * (field[2, under, t, span, :] - field[2, above, t, span, :])
        for t in range(count)
    ]
    twist = across_all(twist, wanted)
    laps, seconds = [], []
    for c in range(3):
        shifted = across_all([field[c, plane, t, span, :] for t in range(count)], wanted)
        lap, second = [], []
        for t in range(wanted):
            here = field[c, plane, t, span, :]
            down2, down1, up1, up2 = (field[c, plane, t, pl.ds(start + d, rows), :] for d in (-2, -1, 1, 2))
            in_x = second_of(down2, down1, here, up1, up2, spacing)
            in_y = second_of(shifted[0][t], shifted[1][t], here, shifted[2][t], shifted[3][t], spacing)
            in_z = square * (field[c, under, t, span, :] - 2.0 * here + field[c, above, t, span, :])
            lap.append(in_x + in_y + in_z)
            second.append((in_x, in_y, in_z)[c])
        laps.append(lap)
        seconds.append(second)
    out = [[], [], []]
    for t in range(wanted):
        ends = (mixed[t, pl.ds(start + d, rows), :] for d in (-2, -1, 1, 2))
        div_x = seconds[0][t] + first_of(*ends, spacing)
        div_y = seconds[1][t] + first_of(*(s[t] for s in twist), spacing)
        lower = along_x[under, t, span, :] + along_y[under, t, span, :]
        upper = along_x[above, t, span, :] + along_y[above, t, span, :]
        div_z = seconds[2][t] + half * (lower - upper)
        bulk = lame[t] + shear[t]
        for c, div in enumerate((div_x, div_y, div_z)):
            out[c].append(shear[t] * laps[c][t] + bulk * div)
    return out


def exact_dot(value, pick):
    high = value.astype(jnp.bfloat16)
    rest = value - high.astype(jnp.float32)
    middle = rest.astype(jnp.bfloat16)
    low = (rest - middle.astype(jnp.float32)).astype(jnp.bfloat16)
    dot = lambda part: jnp.dot(part, pick, preferred_element_type=jnp.float32)
    return dot(high) + (dot(middle) + dot(low))


def prolonged(tiles):
    odd_x = [0.5 * (tile + turned(tile, -1, 0)) for tile in tiles]
    next_y = across(tiles, 1, 2)
    next_odd = across(odd_x, 1, 2)
    return (
        tiles,
        [0.5 * (a + b) for a, b in zip(tiles, next_y)],
        odd_x,
        [0.5 * (a + b) for a, b in zip(odd_x, next_odd)],
    )


def restricted(parts):
    even_even, even_odd, odd_even, odd_odd = parts
    even = [0.5 * a + 0.25 * (b + turned(b, 1, 0)) for a, b in zip(even_even, odd_even)]
    odd = [0.5 * a + 0.25 * (b + turned(b, 1, 0)) for a, b in zip(even_odd, odd_odd)]
    return [0.5 * a + 0.25 * (b + c) for a, b, c in zip(even, odd, across(odd, -1, 2))]


def largest(values):
    total = values[0]
    for value in values[1:]:
        total = jnp.maximum(total, value)
    return jnp.max(total)


def start_line(lines):
    ends = [a + STEP_LOW * b for a, b in lines]
    top = largest(ends)
    slope = largest([jnp.where(e == top, b, FAR) for e, (_, b) in zip(ends, lines)])
    begin = largest([jnp.where((e == top) & (b == slope), a, FAR) for e, (a, b) in zip(ends, lines)])
    return begin, slope


def next_line(lines, begin, slope, limit):
    crossings = []
    for a, b in lines:
        steeper = b - slope
        crossings.append(jnp.where(steeper > 0.0, (begin - a) / steeper, -FAR))
    nearest = -largest([-s for s in crossings])
    found = nearest <= limit
    new_slope = largest([jnp.where(s == nearest, b, FAR) for s, (_, b) in zip(crossings, lines)])
    new_begin = largest(
        [jnp.where((s == nearest) & (b == new_slope), a, FAR) for s, (a, b) in zip(crossings, lines)]
    )
    return jnp.where(found, new_begin, begin), jnp.where(found, new_slope, slope), found


def envelopes(first, last, peak):
    lane = iota((1, LANES), 1)
    bound = 0.3 / jnp.full((8, LANES), peak, jnp.float32)
    limit = jnp.max(bound * bound) * 1.00001
    first_begin, first_slope = start_line(first)
    last_begin, last_slope = start_line(last)
    message = jnp.where(
        lane < 32,
        first_begin,
        jnp.where(lane < 64, first_slope, jnp.where(lane < 96, last_begin, last_slope)),
    )

    def more(state):
        return (state[0] < SLOTS) & (state[1] > 0)

    def step(state):
        n, _, fa, fb, la, lb, message = state
        message = jnp.where(lane == n, fa, message)
        message = jnp.where(lane == n + 32, fb, message)
        message = jnp.where(lane == n + 64, la, message)
        message = jnp.where(lane == n + 96, lb, message)
        fa, fb, found_first = next_line(first, fa, fb, limit)
        la, lb, found_last = next_line(last, la, lb, limit)
        found = (found_first | found_last).astype(jnp.int32)
        return n + 1, found, fa, fb, la, lb, message

    start = (jnp.int32(0), jnp.int32(1), first_begin, first_slope, last_begin, last_slope, message)
    _, left, _, _, _, _, message = lax.while_loop(more, step, start)
    return message, left.astype(jnp.float32)


def sealed(message, peak, flag):
    lane = iota((1, LANES), 1)
    return jnp.where(lane == PEAK_LANE, peak, jnp.where(lane == FLAG_LANE, flag, message))


def opened(received):
    first, last = [], []
    rows = received.shape[0]
    lane = iota((8, LANES), 1)
    peak, flag = [], []
    for r in range(0, rows, 8):
        begin = received[r : r + 8, :]
        slope = turned(begin, -32, 1)
        in_first = lane < SLOTS
        in_last = (lane >= 64) & (lane < 64 + SLOTS)
        first.append((jnp.where(in_first, begin, FAR), jnp.where(in_first, slope, 0.0)))
        last.append((jnp.where(in_last, begin, FAR), jnp.where(in_last, slope, 0.0)))
        peak.append(jnp.where(lane == PEAK_LANE, begin, 0.0))
        flag.append(jnp.where(lane == FLAG_LANE, begin, 0.0))
    return first, last, largest(peak), largest(flag)


def main_kernel(*refs):
    named = dict(zip(NAMES, refs[:10]))
    place, side_low, side_high, row_low, row_high, split_pick, weave_pick = refs[10:17]
    fine_rate, coarse_rate, plane_out, iterate_out, lines_out, message_out = refs[17:23]
    fine, fine_x, fine_y, rest, coarse, coarse_x, coarse_y, coarse_rest = refs[23:31]
    mixed, planes, parted, woven, ends = refs[31:36]
    packed = dict(zip("ABC", zip(refs[36:39], refs[39:42])))

    for tile in "ABC":
        base, rows = TILE_ROWS[tile]
        rim = TILE_RIM[tile]
        for side, source in enumerate((side_low, side_high)):
            target = packed[tile][side]
            target[...] = jnp.zeros(target.shape, jnp.float32)
            target[rows : 2 * rows, :] = source[base : base + rows, :]
            row = [r for t, s, r in CORNERS if t == tile and s == side][0]
            target[rows - rim : rows, :] = row_low[row : row + rim, :]
            high = min(rim, 8)
            target[2 * rows : 2 * rows + high, :] = row_high[row : row + high, :]

    slot = {key: i for i, key in enumerate(DEEP_REST)}
    coarse_slot = {key: i for i, key in enumerate(COARSE_REST)}

    def home(key):
        if key in slot:
            return rest.at[slot[key]]
        if key in coarse_slot:
            return coarse_rest.at[coarse_slot[key]]
        return (fine if key[0] == "fn" else coarse).at[key[1]]

    for key, low, high, tile, at, row, own in ENTRIES:
        target = home(key)
        rows = TILE_ROWS[tile][1]
        total = target.shape[1]
        if low > 2:
            for t in range(own):
                target[t, 0:rows, :] = jnp.zeros((rows, LANES), jnp.float32)
                target[t, 2 * rows : total, :] = jnp.zeros((total - 2 * rows, LANES), jnp.float32)
        for t in range(own):
            target[t, rows : 2 * rows, :] = own_tile(named, key, t)
            begin = row + t * low
            target[t, rows - low : rows, :] = row_low[begin : begin + low, :]
            target[t, 2 * rows : 2 * rows + high, :] = row_high[begin : begin + high, :]
        low_side, high_side = packed[tile][0][...], packed[tile][1][...]
        lane = iota(low_side.shape, 1)
        target[own, :, :] = jnp.where(
            lane < high,
            turned(high_side, -at, 1),
            jnp.where(lane >= LANES - low, turned(low_side, -(at + low), 1), 0.0),
        )
    coarse[:, 8] = jnp.zeros(coarse.shape[:1] + coarse.shape[2:], jnp.float32)

    def fine_slopes(k, carry):
        slopes(fine, fine_x, fine_y, k, 16, 16, 2, 1.0)
        return carry

    lax.fori_loop(0, 5, fine_slopes, 0)
    for k in (5, 6, 7):
        slopes(fine, fine_x, fine_y, k, 8, 32, 3, 1.0)

    def fine_plane(k, carry):
        above = jnp.where(k == 0, 1, k - 1)
        own = [slice(t * LANES, (t + 1) * LANES) for t in range(2)]
        shear = [named["fs"][k, :, lanes] for lanes in own]
        lame = [named["fl"][k, :, lanes] for lanes in own]
        accel = acceleration(fine, fine_x, fine_y, mixed, (above, k, k + 1), 16, 16, 2, 1.0, shear, lame)
        for c in range(3):
            for t in range(2):
                fine_rate[c, k, :, own[t]] = accel[c][t] / named["fd"][k, :, own[t]]
        return carry

    lax.fori_loop(0, 6, fine_plane, 0)

    window = slice(8, 40)
    shear = [rest[slot[("fs", (6,))], t, window, :] for t in range(3)]
    lame = [rest[slot[("fl", (6,))], t, window, :] for t in range(3)]
    accel = acceleration(fine, fine_x, fine_y, mixed, (5, 6, 7), 8, 32, 3, 1.0, shear, lame)
    for t in range(3):
        density = rest[slot[("fd", (6,))], t, window, :]
        filled = density > 0.0
        density = jnp.where(filled, density, 1.0)
        for c in range(3):
            rate = jnp.where(filled, accel[c][t] / density, 0.0)
            planes[3 + c, t, :, :] = rate
            planes[c, t, :, :] = 2.0 * fine[c, 6, t, window, :] - rest[c, t, window, :]
            if t < 2:
                fine_rate[c, 6, :, t * LANES : (t + 1) * LANES] = rate[8:24, :]
        fine_shear = rest[slot[("fs", (7,))], t, window, :]
        planes[6, t, :, :] = fine_shear
        planes[7, t, :, :] = rest[slot[("fl", (7,))], t, window, :] + 2.0 * fine_shear

    stacked = jnp.concatenate(
        [
            jnp.concatenate([planes[p, t, pl.ds(odd, 16, stride=2), :] for t in range(3)], axis=1)
            for p in range(8)
            for odd in range(2)
        ],
        axis=0,
    )
    parted[...] = exact_dot(stacked, split_pick[...])

    def four(p):
        return tuple(
            [
                parted[p * 32 + odd_x * 16 : p * 32 + odd_x * 16 + 16, (odd_y * 2 + t) * LANES : (odd_y * 2 + t + 1) * LANES]
                for t in range(2)
            ]
            for odd_x in range(2)
            for odd_y in range(2)
        )

    for k in range(8):
        slopes(coarse, coarse_x, coarse_y, k, 4, 16, 2, 2.0)
    coarse_x[8] = jnp.zeros(coarse_x.shape[1:], jnp.float32)
    coarse_y[8] = jnp.zeros(coarse_y.shape[1:], jnp.float32)

    def coarse_plane(k, carry):
        shear = [named["cs"][k]]
        lame = [named["cl"][k]]
        accel = acceleration(coarse, coarse_x, coarse_y, mixed, (k - 1, k, k + 1), 8, 8, 1, 2.0, shear, lame)
        for c in range(3):
            coarse_rate[c, k - 1] = accel[c][0] / named["cd"][k]
        return carry

    lax.fori_loop(2, 8, coarse_plane, 0)
    band = slice(4, 20)

    def coarse_pair(name, k):
        return [coarse_rest[coarse_slot[(name, (k,))], t, band, :] for t in range(2)]

    shear, lame, density = coarse_pair("cs", 1), coarse_pair("cl", 1), coarse_pair("cd", 1)
    accel = acceleration(coarse, coarse_x, coarse_y, mixed, (0, 1, 2), 4, 16, 2, 2.0, shear, lame)
    below_rate = [[], [], []]
    for c in range(3):
        for t in range(2):
            filled = density[t] > 0.0
            rate = jnp.where(filled, accel[c][t] / jnp.where(filled, density[t], 1.0), 0.0)
            below_rate[c].append(rate)
        coarse_rate[c, 0] = below_rate[c][0][4:12, :]

    shear, lame = coarse_pair("cs", 0), coarse_pair("cl", 0)
    row = iota((16, LANES), 0) + (place[0] * 8 - 4)
    lane = iota((16, LANES), 1)
    column = [lane, jnp.where(lane < 64, lane + LANES, lane - LANES)]
    fine_moduli = (four(6), four(6), four(7))
    coarse_moduli = (shear, shear, [l + 2.0 * s for l, s in zip(lame, shear)])
    for c in range(3):
        moduli = fine_moduli[c]
        half = [0.5 * m for m in coarse_moduli[c]]
        spread = restricted(moduli)
        inverse = []
        for t in range(2):
            diagonal = half[t] + 0.5625 * spread[t]
            x, y = row, column[t] + place[1] * LANES
            inside = (x >= 0) & (x < place[2]) & (y >= 0) & (y < place[3]) & (diagonal > 0.0)
            inverse.append(jnp.where(inside, 1.0 / jnp.where(inside, diagonal, 1.0), 0.0))
        for part in range(2):
            if part == 0:
                now = [coarse[c, 0, t, band, :] for t in range(2)]
                before = [coarse_rest[coarse_slot[("cb", (c, 0))], t, band, :] for t in range(2)]
                iterate = [2.0 * a - b for a, b in zip(now, before)]
                now = [coarse[c, 1, t, band, :] for t in range(2)]
                before = [coarse_rest[coarse_slot[("cb", (c, 1))], t, band, :] for t in range(2)]
                below = [2.0 * a - b for a, b in zip(now, before)]
            else:
                iterate = [jnp.zeros((16, LANES), jnp.float32)] * 2
                below = below_rate[c]
            above = four(3 * part + c)
            fixed = restricted([[m * a for m, a in zip(ms, as_)] for ms, as_ in zip(moduli, above)])
            fixed = [h * b + f for h, b, f in zip(half, below, fixed)]

            def mismatch_of(iterate):
                stress = [[m * a for m, a in zip(ms, ps)] for ms, ps in zip(moduli, prolonged(iterate))]
                return [h * i + (s - f) for h, i, s, f in zip(half, iterate, restricted(stress), fixed)]

            mismatch = mismatch_of(iterate)
            ends[part, c] = mismatch[0]
            for _ in range(ITERS):
                iterate = [i - m * v for i, m, v in zip(iterate, mismatch, inverse)]
                mismatch = mismatch_of(iterate)
            ends[2 + part, c] = mismatch[0]
            ends[4 + part, c] = iterate[0]
            even_even, even_odd, odd_even, odd_odd = prolonged(iterate)
            at = (part * 3 + c) * 32
            woven[at : at + 16, 0:LANES] = even_even[0]
            woven[at : at + 16, LANES : 2 * LANES] = even_odd[0]
            woven[at + 16 : at + 32, 0:LANES] = odd_even[0]
            woven[at + 16 : at + 32, LANES : 2 * LANES] = odd_odd[0]

    woven[...] = exact_dot(woven[...], weave_pick[...])
    for part in range(2):
        for c in range(3):
            iterate_out[part, c] = ends[4 + part, c, 4:12, :]
            for odd in range(2):
                at = (part * 3 + c) * 32 + odd * 16 + 4
                for t in range(2):
                    plane_out[part, c, t, pl.ds(odd, 8, stride=2), :] = woven[
                        at : at + 8, t * LANES : (t + 1) * LANES
                    ]

    lines = []
    for which in range(2):
        found = []
        for c in range(3):
            begin, slope = ends[2 * which, c, 4:12, :], ends[2 * which + 1, c, 4:12, :]
            lines_out[2 * which, c] = begin
            lines_out[2 * which + 1, c] = slope
            found += [(begin, slope), (-begin, -slope)]
        lines.append(found)
    ratio = (named["fl"][...] + 2.0 * named["fs"][...]) / named["fd"][...]
    coarse_ratio = (named["cl"][...] + 2.0 * named["cs"][...]) / named["cd"][...]
    fine_peak = jnp.sqrt(jnp.full((8, LANES), jnp.max(ratio), jnp.float32))
    coarse_peak = jnp.sqrt(jnp.full((8, LANES), jnp.max(coarse_ratio), jnp.float32))
    peak = jnp.max(jnp.maximum(fine_peak, 0.5 * coarse_peak))
    message, flag = envelopes(lines[0], lines[1], peak)
    message_out[...] = jnp.broadcast_to(sealed(message, peak, flag), message_out.shape)


def merge_kernel(received, message_out):
    first, last, peak, flag = opened(received)
    message, full = envelopes(first, last, peak)
    message_out[...] = jnp.broadcast_to(sealed(message, peak, jnp.maximum(flag, full)), message_out.shape)


def final_kernel(received, fn, fb, cn, cb, fine_rate, coarse_rate, plane, iterate, fine_out, coarse_out, scalars):
    first, last, peak, flag = opened(received)
    step = 0.3 / jnp.full((8, LANES), peak, jnp.float32)
    square = step * step
    first_max = largest([a + square * b for a, b in first])
    last_max = largest([a + square * b for a, b in last])
    reduction = last_max / (jnp.full((8, LANES), first_max, jnp.float32) + 1e-06)
    flag = jnp.where(square < STEP_LOW, 1.0, flag)
    row = iota((8, LANES), 0)
    scalars[...] = jnp.where(row == 0, reduction, jnp.where(row == 1, square, flag))
    square = square[0:1, 0:1]
    for c in range(3):
        fine_out[c, 0:7] = 2.0 * fn[c, 0:7] - fb[c, 0:7] + square * fine_rate[c]
        coarse_out[c, 1:8] = 2.0 * cn[c, 1:8] - cb[c, 1:8] + square * coarse_rate[c]
        coarse_out[c, 0] = iterate[0, c] + square * iterate[1, c]
        for t in range(2):
            fine_out[c, 7, :, t * LANES : (t + 1) * LANES] = plane[0, c, t] + square * plane[1, c, t]


def shifts(count, up):
    return [(i, i + 1) if up else (i + 1, i) for i in range(count - 1)]


def gather_groups(columns, rows):
    near, ring = {}, {}
    for i in range(columns):
        for j in range(rows):
            near.setdefault((i // 8, j % 4), []).append(i * rows + j)
            ring.setdefault((i % 8, j // 4), []).append(i * rows + j)
    return list(near.values()), list(ring.values())


def split_matrix():
    lane = np.arange(3 * LANES)
    fine_column = np.where(lane < 320, lane, lane - 384)[:, None]
    circle = np.arange(2 * LANES)
    coarse_column = np.where(circle < 192, circle, circle - 256)[None, :]
    return np.concatenate(
        [fine_column == 2 * coarse_column, fine_column == 2 * coarse_column + 1], axis=1
    ).astype(ml_dtypes.bfloat16)


def weave_matrix():
    lane = np.arange(2 * LANES)
    target = np.where(lane < LANES, 2 * lane, 2 * (lane - LANES) + 1)[:, None]
    return (target == lane[None, :]).astype(ml_dtypes.bfloat16)


def f32(*shape):
    return jax.ShapeDtypeStruct(shape, jnp.float32)


def vm(*shape):
    return pltpu.VMEM(shape, jnp.float32)


PARAMS = pltpu.CompilerParams(vmem_limit_bytes=48 * 1024 * 1024)


def make_shards(columns, rows):
    near, ring = gather_groups(columns, rows)
    axes = ("gx", "gy")

    def shards(*args):
        fn, fb, fd, fs, fl, cn, cb, cd, cs, cl = args
        in_vmem = pl.BlockSpec(memory_space=pltpu.VMEM)
        call = lambda kernel, n_in, outs, scratch=(), specs=None: pl.pallas_call(
            kernel,
            out_shape=outs,
            in_specs=specs or [in_vmem] * n_in,
            out_specs=[in_vmem] * len(outs) if isinstance(outs, tuple) else in_vmem,
            scratch_shapes=list(scratch),
            compiler_params=PARAMS,
        )
        low, high = call(pack_columns, 10, (f32(PACKED_ROWS, LANES),) * 2)(*args)
        side_low = lax.ppermute(low, "gy", shifts(rows, True))
        side_high = lax.ppermute(high, "gy", shifts(rows, False))
        low, high = call(pack_rows, 12, (f32(RIM_ROWS, LANES),) * 2)(*args, side_low, side_high)
        row_low = lax.ppermute(low, "gx", shifts(columns, True))
        row_high = lax.ppermute(high, "gx", shifts(columns, False))
        place = jnp.stack(
            [
                lax.axis_index("gx"),
                lax.axis_index("gy"),
                jnp.int32(columns * 8),
                jnp.int32(rows * LANES),
            ]
        ).astype(jnp.int32)
        near_size, ring_size = len(near[0]), len(ring[0])
        outs = (
            f32(3, 7, 16, 256),
            f32(3, 7, 8, 128),
            f32(2, 3, 2, 16, 128),
            f32(2, 3, 8, 128),
            f32(4, 3, 8, 128),
            f32(near_size, LANES),
        )
        scratch = (
            vm(3, 8, 3, 48, LANES),
            vm(8, 3, 48, LANES),
            vm(8, 3, 48, LANES),
            vm(8, 3, 48, LANES),
            vm(3, 9, 2, 24, LANES),
            vm(9, 2, 24, LANES),
            vm(9, 2, 24, LANES),
            vm(11, 2, 24, LANES),
            vm(3, 48, LANES),
            vm(8, 3, 32, LANES),
            vm(256, 512),
            vm(192, 256),
            vm(6, 3, 16, LANES),
        ) + (vm(48, LANES), vm(48, LANES), vm(24, LANES)) * 2
        specs = [in_vmem] * 10 + [pl.BlockSpec(memory_space=pltpu.SMEM)] + [in_vmem] * 6
        fine_rate, coarse_rate, plane, iterate, lines, message = call(main_kernel, 17, outs, scratch, specs)(
            *args,
            place,
            side_low,
            side_high,
            row_low,
            row_high,
            jnp.asarray(split_matrix()),
            jnp.asarray(weave_matrix()),
        )
        received = lax.all_to_all(message, axes, 0, 0, tiled=True, axis_index_groups=near)
        message = call(merge_kernel, 1, f32(ring_size, LANES))(received)
        received = lax.all_to_all(message, axes, 0, 0, tiled=True, axis_index_groups=ring)
        fine_next, coarse_next, scalars = call(final_kernel, 9, (f32(*fn.shape), f32(*cn.shape), f32(8, LANES)))(
            received, fn, fb, cn, cb, fine_rate, coarse_rate, plane, iterate
        )

        def plain():
            square = scalars[1, 0]
            values = jnp.abs(lines[0::2] + square * lines[1::2])
            tops = lax.pmax(jnp.max(values, axis=(1, 2, 3)), axes)
            return tops[1] / (tops[0] + 1e-06)

        reduction = lax.cond(scalars[2, 0] > 0.0, plain, lambda: scalars[0, 0])
        return fine_next, coarse_next, reduction

    return shards


def solution(mesh):
    placed = (
        P(None, None, "gx", "gy"),
        P(None, None, "gx", "gy"),
        P(None, "gx", "gy"),
        P(None, "gx", "gy"),
        P(None, "gx", "gy"),
        P(None, None, "gx", "gy"),
        P(None, None, "gx", "gy"),
        P(None, "gx", "gy"),
        P(None, "gx", "gy"),
        P(None, "gx", "gy"),
    )
    return jax.shard_map(
        make_shards(mesh.shape["gx"], mesh.shape["gy"]),
        mesh=mesh,
        in_specs=placed,
        out_specs=(P(None, None, "gx", "gy"), P(None, None, "gx", "gy"), P()),
        check_vma=False,
    )
```

```python
import jax
import jax.numpy as jnp
import ml_dtypes
import numpy as np
from jax import lax
from jax.experimental import pallas as pl
from jax.experimental.pallas import tpu as pltpu
from jax.sharding import PartitionSpec as P

ITERS = 3
LANES = 128
NAMES = ("fn", "fb", "fd", "fs", "fl", "cn", "cb", "cd", "cs", "cl")

DEEP_NOW = [("fn", (c, k)) for c in range(3) for k in (5, 6, 7)]
THIN_NOW = [("fn", (c, k)) for c in range(3) for k in range(5)]
DEEP_REST = [("fb", (c, 6)) for c in range(3)] + [("fd", (6,)), ("fs", (6,)), ("fl", (6,)), ("fs", (7,)), ("fl", (7,))]
COARSE_NOW = [("cn", (c, k)) for c in range(3) for k in range(3)]
COARSE_REST = [("cb", (c, k)) for c in range(3) for k in range(2)] + [
    ("cd", (1,)),
    ("cs", (0,)),
    ("cl", (0,)),
    ("cs", (1,)),
    ("cl", (1,)),
]
COARSE_THIN = [("cn", (c, k)) for c in range(3) for k in range(3, 8)]

TILE_ROWS = {"A": (0, 16), "B": (16, 16), "C": (32, 8)}
TILE_RIM = {"A": 9, "B": 7, "C": 5}
PACKED_ROWS = 40


def plan():
    entries, lane, row = [], {"A": 0, "B": 0, "C": 0}, 0
    for tile, keys, low, high in (
        ("A", DEEP_NOW, 9, 8),
        ("A", THIN_NOW, 2, 2),
        ("B", DEEP_REST, 7, 6),
        ("C", COARSE_NOW, 5, 5),
        ("C", COARSE_REST, 4, 4),
        ("C", COARSE_THIN, 2, 2),
    ):
        for key in keys:
            own = 1 if tile == "C" else 2
            entries.append((key, low, high, tile, lane[tile], row, own))
            lane[tile] += low
            row += own * low
    corners, corner_row = {}, 0
    for tile in "ABC":
        for side in range(2):
            corners[tile, side] = corner_row
            corner_row += TILE_RIM[tile]
    return entries, corners, -(-row // 8) * 8, -(-corner_row // 8) * 8


ENTRIES, CORNERS, RIM_ROWS, CORNER_ROWS = plan()

PACK_SOURCES = (
    ("fn", ()),
    ("fb", (slice(None), slice(6, 7))),
    ("fd", (slice(6, 7),)),
    ("fs", (slice(6, 8),)),
    ("fl", (slice(6, 8),)),
    ("cn", ()),
    ("cb", (slice(None), slice(0, 2))),
    ("cd", (slice(1, 2),)),
    ("cs", (slice(0, 2),)),
    ("cl", (slice(0, 2),)),
)

SLOTS = 31
PEAK_LANE = 31
FLAG_LANE = 63
STEP_LOW = 0.02
FAR = -1.0e30


def iota(shape, dim):
    return lax.broadcasted_iota(jnp.int32, shape, dim)


def turned(value, steps, axis):
    size = value.shape[axis]
    steps = steps % size
    return value if steps == 0 else pltpu.roll(value, steps, axis)


def own_tile(refs, key, tile):
    name, index = key
    return refs[name][index + (slice(None), slice(tile * LANES, (tile + 1) * LANES))]


def is_even(axis):
    return lax.axis_index(axis) % 2 == 0


def pair(axis, low, high):
    even = is_even(axis)
    return jnp.where(even, low, high), jnp.where(even, high, low)


def pack(*refs):
    sources = dict(zip(NAMES, refs[:10]))
    column_outs, row_outs = refs[10:12], refs[12:14]
    named = dict(zip(NAMES, refs[14:24]))
    sems = refs[24]
    copies = []
    for i, (name, part) in enumerate(PACK_SOURCES):
        source, target = sources[name], named[name]
        if part:
            source, target = source.at[part], target.at[part]
        copies.append(pltpu.make_async_copy(source, target, sems.at[i]))
    for copy in copies:
        copy.start()
    for copy in copies:
        copy.wait()
    for tile, (base, rows) in TILE_ROWS.items():
        lane = iota((rows, LANES), 1)
        low_sum = jnp.zeros((rows, LANES), jnp.float32)
        high_sum = low_sum
        for key, low, _, where, at, _, own in ENTRIES:
            if where != tile:
                continue
            inside = (lane >= at) & (lane < at + low)
            low_sum = jnp.where(inside, turned(own_tile(named, key, own - 1), at + low, 1), low_sum)
            high_sum = jnp.where(inside, turned(own_tile(named, key, 0), at, 1), high_sum)
        span = slice(base, base + rows)
        column_outs[0][span, :], column_outs[1][span, :] = pair("gy", low_sum, high_sum)
    row_outs[0][RIM_ROWS - 8 :, :] = jnp.zeros((8, LANES), jnp.float32)
    row_outs[1][RIM_ROWS - 8 :, :] = jnp.zeros((8, LANES), jnp.float32)
    for (name, index), low, _, _, _, row, own in ENTRIES:
        ref = named[name]
        rows = ref.shape[-2]
        for tile in range(own):
            lanes = slice(tile * LANES, (tile + 1) * LANES)
            span = slice(row + tile * low, row + tile * low + low)
            row_outs[0][span, :], row_outs[1][span, :] = pair(
                "gx", ref[index + (slice(rows - low, rows), lanes)], ref[index + (slice(0, low), lanes)]
            )


def pack_corners(first, second, first_out, second_out):
    first_out[CORNER_ROWS - 8 :, :] = jnp.zeros((8, LANES), jnp.float32)
    second_out[CORNER_ROWS - 8 :, :] = jnp.zeros((8, LANES), jnp.float32)
    for tile, (base, rows) in TILE_ROWS.items():
        rim = TILE_RIM[tile]
        end, begin = slice(base + rows - rim, base + rows), slice(base, base + rim)
        ends = pair("gy", second[end, :], first[end, :])
        begins = pair("gy", second[begin, :], first[begin, :])
        for side in range(2):
            row = CORNERS[tile, side]
            first_out[row : row + rim, :], second_out[row : row + rim, :] = pair("gx", ends[side], begins[side])


def across(tiles, steps, wanted):
    count = len(tiles)
    lane = iota(tiles[0].shape, 1)
    rolled = [turned(tile, -steps, 1) for tile in tiles]
    if steps > 0:
        return [jnp.where(lane < LANES - steps, rolled[t], rolled[(t + 1) % count]) for t in range(wanted)]
    return [jnp.where(lane >= -steps, rolled[t], rolled[(t - 1) % count]) for t in range(wanted)]


def first_of(down2, down1, up1, up2, spacing):
    return (8.0 * (up1 - down1) - (up2 - down2)) * (1.0 / (12.0 * spacing))


def second_of(down2, down1, here, up1, up2, spacing):
    return (16.0 * (up1 + down1) - (up2 + down2) - 30.0 * here) * (1.0 / (12.0 * spacing * spacing))


def across_all(tiles, wanted):
    return [across(tiles, steps, wanted) for steps in (-2, -1, 1, 2)]


def slopes(field, along_x, along_y, plane, start, rows, wanted, spacing):
    count = field.shape[2]
    for t in range(count):
        down2, down1, up1, up2 = (field[0, plane, t, pl.ds(start + d, rows), :] for d in (-2, -1, 1, 2))
        along_x[plane, t, start : start + rows, :] = first_of(down2, down1, up1, up2, spacing)
    span = slice(start - 4, start + rows + 4)
    shifted = across_all([field[1, plane, t, span, :] for t in range(count)], wanted)
    for t in range(wanted):
        along_y[plane, t, span, :] = first_of(*(s[t] for s in shifted), spacing)


def acceleration(field, along_x, along_y, mixed, planes, start, rows, wanted, spacing, shear, lame):
    above, plane, under = planes
    count = field.shape[2]
    half = 1.0 / (2.0 * spacing)
    square = 1.0 / (spacing * spacing)
    span = slice(start, start + rows)
    wide = slice(start - 4, start + rows + 4)
    for t in range(wanted):
        mixed[t, wide, :] = along_y[plane, t, wide, :] + half * (
            field[2, under, t, wide, :] - field[2, above, t, wide, :]
        )
    twist = [
        along_x[plane, t, span, :] + half * (field[2, under, t, span, :] - field[2, above, t, span, :])
        for t in range(count)
    ]
    twist = across_all(twist, wanted)
    laps, seconds = [], []
    for c in range(3):
        shifted = across_all([field[c, plane, t, span, :] for t in range(count)], wanted)
        lap, second = [], []
        for t in range(wanted):
            here = field[c, plane, t, span, :]
            down2, down1, up1, up2 = (field[c, plane, t, pl.ds(start + d, rows), :] for d in (-2, -1, 1, 2))
            in_x = second_of(down2, down1, here, up1, up2, spacing)
            in_y = second_of(shifted[0][t], shifted[1][t], here, shifted[2][t], shifted[3][t], spacing)
            in_z = square * (field[c, under, t, span, :] - 2.0 * here + field[c, above, t, span, :])
            lap.append(in_x + in_y + in_z)
            second.append((in_x, in_y, in_z)[c])
        laps.append(lap)
        seconds.append(second)
    out = [[], [], []]
    for t in range(wanted):
        ends = (mixed[t, pl.ds(start + d, rows), :] for d in (-2, -1, 1, 2))
        div_x = seconds[0][t] + first_of(*ends, spacing)
        div_y = seconds[1][t] + first_of(*(s[t] for s in twist), spacing)
        lower = along_x[under, t, span, :] + along_y[under, t, span, :]
        upper = along_x[above, t, span, :] + along_y[above, t, span, :]
        div_z = seconds[2][t] + half * (lower - upper)
        bulk = lame[t] + shear[t]
        for c, div in enumerate((div_x, div_y, div_z)):
            out[c].append(shear[t] * laps[c][t] + bulk * div)
    return out


def exact_dot(value, pick):
    high = value.astype(jnp.bfloat16)
    rest = value - high.astype(jnp.float32)
    middle = rest.astype(jnp.bfloat16)
    low = (rest - middle.astype(jnp.float32)).astype(jnp.bfloat16)
    dot = lambda part: jnp.dot(part, pick, preferred_element_type=jnp.float32)
    return dot(high) + (dot(middle) + dot(low))


def prolonged(tiles):
    odd_x = [0.5 * (tile + turned(tile, -1, 0)) for tile in tiles]
    next_y = across(tiles, 1, 2)
    next_odd = across(odd_x, 1, 2)
    return (
        tiles,
        [0.5 * (a + b) for a, b in zip(tiles, next_y)],
        odd_x,
        [0.5 * (a + b) for a, b in zip(odd_x, next_odd)],
    )


def restricted(parts):
    even_even, even_odd, odd_even, odd_odd = parts
    even = [0.5 * a + 0.25 * (b + turned(b, 1, 0)) for a, b in zip(even_even, odd_even)]
    odd = [0.5 * a + 0.25 * (b + turned(b, 1, 0)) for a, b in zip(even_odd, odd_odd)]
    return [0.5 * a + 0.25 * (b + c) for a, b, c in zip(even, odd, across(odd, -1, 2))]


def largest(values):
    total = values[0]
    for value in values[1:]:
        total = jnp.maximum(total, value)
    return jnp.max(total)


def start_line(lines):
    ends = [a + STEP_LOW * b for a, b in lines]
    top = largest(ends)
    slope = largest([jnp.where(e == top, b, FAR) for e, (_, b) in zip(ends, lines)])
    begin = largest([jnp.where((e == top) & (b == slope), a, FAR) for e, (a, b) in zip(ends, lines)])
    return begin, slope


def next_line(lines, begin, slope, limit):
    crossings = []
    for a, b in lines:
        steeper = b - slope
        crossings.append(jnp.where(steeper > 0.0, (begin - a) / steeper, -FAR))
    nearest = -largest([-s for s in crossings])
    found = nearest <= limit
    new_slope = largest([jnp.where(s == nearest, b, FAR) for s, (_, b) in zip(crossings, lines)])
    new_begin = largest(
        [jnp.where((s == nearest) & (b == new_slope), a, FAR) for s, (a, b) in zip(crossings, lines)]
    )
    return jnp.where(found, new_begin, begin), jnp.where(found, new_slope, slope), found


def envelopes(first, last, peak):
    lane = iota((1, LANES), 1)
    bound = 0.3 / jnp.full((8, LANES), peak, jnp.float32)
    limit = jnp.max(bound * bound) * 1.00001
    first_begin, first_slope = start_line(first)
    last_begin, last_slope = start_line(last)
    message = jnp.where(
        lane < 32,
        first_begin,
        jnp.where(lane < 64, first_slope, jnp.where(lane < 96, last_begin, last_slope)),
    )

    def more(state):
        return (state[0] < SLOTS) & (state[1] > 0)

    def step(state):
        n, _, fa, fb, la, lb, message = state
        message = jnp.where(lane == n, fa, message)
        message = jnp.where(lane == n + 32, fb, message)
        message = jnp.where(lane == n + 64, la, message)
        message = jnp.where(lane == n + 96, lb, message)
        fa, fb, found_first = next_line(first, fa, fb, limit)
        la, lb, found_last = next_line(last, la, lb, limit)
        found = (found_first | found_last).astype(jnp.int32)
        return n + 1, found, fa, fb, la, lb, message

    start = (jnp.int32(0), jnp.int32(1), first_begin, first_slope, last_begin, last_slope, message)
    _, left, _, _, _, _, message = lax.while_loop(more, step, start)
    return message, left.astype(jnp.float32)


def sealed(message, peak, flag):
    lane = iota((1, LANES), 1)
    return jnp.where(lane == PEAK_LANE, peak, jnp.where(lane == FLAG_LANE, flag, message))


def opened(received):
    first, last = [], []
    rows = received.shape[0]
    lane = iota((8, LANES), 1)
    peak, flag = [], []
    for r in range(0, rows, 8):
        begin = received[r : r + 8, :]
        slope = turned(begin, -32, 1)
        in_first = lane < SLOTS
        in_last = (lane >= 64) & (lane < 64 + SLOTS)
        first.append((jnp.where(in_first, begin, FAR), jnp.where(in_first, slope, 0.0)))
        last.append((jnp.where(in_last, begin, FAR), jnp.where(in_last, slope, 0.0)))
        peak.append(jnp.where(lane == PEAK_LANE, begin, 0.0))
        flag.append(jnp.where(lane == FLAG_LANE, begin, 0.0))
    return first, last, largest(peak), largest(flag)


def main_kernel(*refs):
    named = dict(zip(NAMES, refs[:10]))
    sides, rims, corners = refs[10:12], refs[12:14], refs[14:16]
    split_pick, weave_pick = refs[16:18]
    fine_rate, coarse_rate, plane_out, iterate_out, lines_out, message_out = refs[18:24]
    fine, fine_x, fine_y, rest, coarse, coarse_x, coarse_y, coarse_rest = refs[24:32]
    mixed, planes, parted, woven, ends = refs[32:37]
    packed = dict(zip("ABC", zip(refs[37:40], refs[40:43])))

    def received(axis, pieces, span):
        return pair(axis, pieces[1][span, :], pieces[0][span, :])

    for tile, (base, rows) in TILE_ROWS.items():
        rim = TILE_RIM[tile]
        own = received("gy", sides, slice(base, base + rows))
        for side in range(2):
            target = packed[tile][side]
            target[...] = jnp.zeros(target.shape, jnp.float32)
            target[rows : 2 * rows, :] = own[side]
            row = CORNERS[tile, side]
            low, high = received("gx", corners, slice(row, row + rim))
            target[rows - rim : rows, :] = low
            target[2 * rows : 2 * rows + rim, :] = high

    slot = {key: i for i, key in enumerate(DEEP_REST)}
    coarse_slot = {key: i for i, key in enumerate(COARSE_REST)}

    def home(key):
        if key in slot:
            return rest.at[slot[key]]
        if key in coarse_slot:
            return coarse_rest.at[coarse_slot[key]]
        return (fine if key[0] == "fn" else coarse).at[key[1]]

    for key, low, high, tile, at, row, own in ENTRIES:
        target = home(key)
        rows = TILE_ROWS[tile][1]
        total = target.shape[1]
        if low > 2:
            for t in range(own):
                target[t, 0:rows, :] = jnp.zeros((rows, LANES), jnp.float32)
                target[t, 2 * rows : total, :] = jnp.zeros((total - 2 * rows, LANES), jnp.float32)
        for t in range(own):
            target[t, rows : 2 * rows, :] = own_tile(named, key, t)
            below, beyond = received("gx", rims, slice(row + t * low, row + t * low + low))
            target[t, rows - low : rows, :] = below
            target[t, 2 * rows : 2 * rows + low, :] = beyond
        low_side, high_side = packed[tile][0][...], packed[tile][1][...]
        lane = iota(low_side.shape, 1)
        target[own, :, :] = jnp.where(
            lane < high,
            turned(high_side, -at, 1),
            jnp.where(lane >= LANES - low, turned(low_side, -(at + low), 1), 0.0),
        )
    coarse[:, 8] = jnp.zeros(coarse.shape[:1] + coarse.shape[2:], jnp.float32)

    def fine_slopes(k, carry):
        slopes(fine, fine_x, fine_y, k, 16, 16, 2, 1.0)
        return carry

    lax.fori_loop(0, 5, fine_slopes, 0)
    for k in (5, 6, 7):
        slopes(fine, fine_x, fine_y, k, 8, 32, 3, 1.0)

    def fine_plane(k, carry):
        above = jnp.where(k == 0, 1, k - 1)
        own = [slice(t * LANES, (t + 1) * LANES) for t in range(2)]
        shear = [named["fs"][k, :, lanes] for lanes in own]
        lame = [named["fl"][k, :, lanes] for lanes in own]
        accel = acceleration(fine, fine_x, fine_y, mixed, (above, k, k + 1), 16, 16, 2, 1.0, shear, lame)
        for c in range(3):
            for t in range(2):
                fine_rate[c, k, :, own[t]] = accel[c][t] / named["fd"][k, :, own[t]]
        return carry

    lax.fori_loop(0, 6, fine_plane, 0)

    window = slice(8, 40)
    shear = [rest[slot[("fs", (6,))], t, window, :] for t in range(3)]
    lame = [rest[slot[("fl", (6,))], t, window, :] for t in range(3)]
    accel = acceleration(fine, fine_x, fine_y, mixed, (5, 6, 7), 8, 32, 3, 1.0, shear, lame)
    for t in range(3):
        density = rest[slot[("fd", (6,))], t, window, :]
        filled = density > 0.0
        density = jnp.where(filled, density, 1.0)
        for c in range(3):
            rate = jnp.where(filled, accel[c][t] / density, 0.0)
            planes[3 + c, t, :, :] = rate
            planes[c, t, :, :] = 2.0 * fine[c, 6, t, window, :] - rest[c, t, window, :]
            if t < 2:
                fine_rate[c, 6, :, t * LANES : (t + 1) * LANES] = rate[8:24, :]
        fine_shear = rest[slot[("fs", (7,))], t, window, :]
        planes[6, t, :, :] = fine_shear
        planes[7, t, :, :] = rest[slot[("fl", (7,))], t, window, :] + 2.0 * fine_shear

    stacked = jnp.concatenate(
        [
            jnp.concatenate([planes[p, t, pl.ds(odd, 16, stride=2), :] for t in range(3)], axis=1)
            for p in range(8)
            for odd in range(2)
        ],
        axis=0,
    )
    parted[...] = exact_dot(stacked, split_pick[...])

    def four(p):
        return tuple(
            [
                parted[p * 32 + odd_x * 16 : p * 32 + odd_x * 16 + 16, (odd_y * 2 + t) * LANES : (odd_y * 2 + t + 1) * LANES]
                for t in range(2)
            ]
            for odd_x in range(2)
            for odd_y in range(2)
        )

    for k in range(8):
        slopes(coarse, coarse_x, coarse_y, k, 4, 16, 2, 2.0)
    coarse_x[8] = jnp.zeros(coarse_x.shape[1:], jnp.float32)
    coarse_y[8] = jnp.zeros(coarse_y.shape[1:], jnp.float32)

    def coarse_plane(k, carry):
        shear = [named["cs"][k]]
        lame = [named["cl"][k]]
        accel = acceleration(coarse, coarse_x, coarse_y, mixed, (k - 1, k, k + 1), 8, 8, 1, 2.0, shear, lame)
        for c in range(3):
            coarse_rate[c, k - 1] = accel[c][0] / named["cd"][k]
        return carry

    lax.fori_loop(2, 8, coarse_plane, 0)
    band = slice(4, 20)

    def coarse_pair(name, k):
        return [coarse_rest[coarse_slot[(name, (k,))], t, band, :] for t in range(2)]

    shear, lame, density = coarse_pair("cs", 1), coarse_pair("cl", 1), coarse_pair("cd", 1)
    accel = acceleration(coarse, coarse_x, coarse_y, mixed, (0, 1, 2), 4, 16, 2, 2.0, shear, lame)
    below_rate = [[], [], []]
    for c in range(3):
        for t in range(2):
            filled = density[t] > 0.0
            rate = jnp.where(filled, accel[c][t] / jnp.where(filled, density[t], 1.0), 0.0)
            below_rate[c].append(rate)
        coarse_rate[c, 0] = below_rate[c][0][4:12, :]

    shear, lame = coarse_pair("cs", 0), coarse_pair("cl", 0)
    row = iota((16, LANES), 0) + (lax.axis_index("gx") * 8 - 4)
    lane = iota((16, LANES), 1) + lax.axis_index("gy") * LANES
    column = [lane, jnp.where(iota((16, LANES), 1) < 64, lane + LANES, lane - LANES)]
    extent = (lax.axis_size("gx") * 8, lax.axis_size("gy") * LANES)
    fine_moduli = (four(6), four(6), four(7))
    coarse_moduli = (shear, shear, [l + 2.0 * s for l, s in zip(lame, shear)])
    for c in range(3):
        moduli = fine_moduli[c]
        half = [0.5 * m for m in coarse_moduli[c]]
        spread = restricted(moduli)
        inverse = []
        for t in range(2):
            diagonal = half[t] + 0.5625 * spread[t]
            x, y = row, column[t]
            inside = (x >= 0) & (x < extent[0]) & (y >= 0) & (y < extent[1]) & (diagonal > 0.0)
            inverse.append(jnp.where(inside, 1.0 / jnp.where(inside, diagonal, 1.0), 0.0))
        for part in range(2):
            if part == 0:
                now = [coarse[c, 0, t, band, :] for t in range(2)]
                before = [coarse_rest[coarse_slot[("cb", (c, 0))], t, band, :] for t in range(2)]
                iterate = [2.0 * a - b for a, b in zip(now, before)]
                now = [coarse[c, 1, t, band, :] for t in range(2)]
                before = [coarse_rest[coarse_slot[("cb", (c, 1))], t, band, :] for t in range(2)]
                below = [2.0 * a - b for a, b in zip(now, before)]
            else:
                iterate = [jnp.zeros((16, LANES), jnp.float32)] * 2
                below = below_rate[c]
            above = four(3 * part + c)
            fixed = restricted([[m * a for m, a in zip(ms, as_)] for ms, as_ in zip(moduli, above)])
            fixed = [h * b + f for h, b, f in zip(half, below, fixed)]

            def mismatch_of(iterate):
                stress = [[m * a for m, a in zip(ms, ps)] for ms, ps in zip(moduli, prolonged(iterate))]
                return [h * i + (s - f) for h, i, s, f in zip(half, iterate, restricted(stress), fixed)]

            mismatch = mismatch_of(iterate)
            ends[part, c] = mismatch[0]
            for _ in range(ITERS):
                iterate = [i - m * v for i, m, v in zip(iterate, mismatch, inverse)]
                mismatch = mismatch_of(iterate)
            ends[2 + part, c] = mismatch[0]
            ends[4 + part, c] = iterate[0]
            even_even, even_odd, odd_even, odd_odd = prolonged(iterate)
            at = (part * 3 + c) * 32
            woven[at : at + 16, 0:LANES] = even_even[0]
            woven[at : at + 16, LANES : 2 * LANES] = even_odd[0]
            woven[at + 16 : at + 32, 0:LANES] = odd_even[0]
            woven[at + 16 : at + 32, LANES : 2 * LANES] = odd_odd[0]

    woven[...] = exact_dot(woven[...], weave_pick[...])
    for part in range(2):
        for c in range(3):
            iterate_out[part, c] = ends[4 + part, c, 4:12, :]
            for odd in range(2):
                at = (part * 3 + c) * 32 + odd * 16 + 4
                for t in range(2):
                    plane_out[part, c, t, pl.ds(odd, 8, stride=2), :] = woven[
                        at : at + 8, t * LANES : (t + 1) * LANES
                    ]

    lines = []
    for which in range(2):
        found = []
        for c in range(3):
            begin, slope = ends[2 * which, c, 4:12, :], ends[2 * which + 1, c, 4:12, :]
            lines_out[2 * which, c] = begin
            lines_out[2 * which + 1, c] = slope
            found += [(begin, slope), (-begin, -slope)]
        lines.append(found)
    ratio = (named["fl"][...] + 2.0 * named["fs"][...]) / named["fd"][...]
    coarse_ratio = (named["cl"][...] + 2.0 * named["cs"][...]) / named["cd"][...]
    fine_peak = jnp.sqrt(jnp.full((8, LANES), jnp.max(ratio), jnp.float32))
    coarse_peak = jnp.sqrt(jnp.full((8, LANES), jnp.max(coarse_ratio), jnp.float32))
    peak = jnp.max(jnp.maximum(fine_peak, 0.5 * coarse_peak))
    message, flag = envelopes(lines[0], lines[1], peak)
    message_out[...] = jnp.broadcast_to(sealed(message, peak, flag), message_out.shape)


def merge_kernel(received, message_out):
    first, last, peak, flag = opened(received)
    message, full = envelopes(first, last, peak)
    message_out[...] = jnp.broadcast_to(sealed(message, peak, jnp.maximum(flag, full)), message_out.shape)


def final_kernel(
    received, fn, fb, cn, cb, fine_rate, coarse_rate, plane, iterate, fine_out, coarse_out, ratio_out, square_out, flag_out
):
    first, last, peak, flag = opened(received)
    step = 0.3 / jnp.full((8, LANES), peak, jnp.float32)
    square = step * step
    first_max = largest([a + square * b for a, b in first])
    last_max = largest([a + square * b for a, b in last])
    ratio = last_max / (jnp.full((8, LANES), first_max, jnp.float32) + 1e-06)
    ratio_out[0] = jnp.max(ratio)
    square_out[0] = jnp.max(square)
    flag_out[0] = jnp.where((flag > 0.0) | (jnp.max(square) < STEP_LOW), 1, 0)
    square = square[0:1, 0:1]
    for c in range(3):
        fine_out[c, 0:7] = 2.0 * fn[c, 0:7] - fb[c, 0:7] + square * fine_rate[c]
        coarse_out[c, 1:8] = 2.0 * cn[c, 1:8] - cb[c, 1:8] + square * coarse_rate[c]
        coarse_out[c, 0] = iterate[0, c] + square * iterate[1, c]
        for t in range(2):
            fine_out[c, 7, :, t * LANES : (t + 1) * LANES] = plane[0, c, t] + square * plane[1, c, t]


def exchange(first, second, axis, count):
    near = [(i, i ^ 1) for i in range(count) if i ^ 1 < count]
    far = [(i, i + 1) for i in range(1, count - 1, 2)] + [(i + 1, i) for i in range(1, count - 1, 2)]
    return lax.ppermute(first, axis, near), lax.ppermute(second, axis, far)


def gather_groups(columns, rows):
    near, ring = {}, {}
    for i in range(columns):
        for j in range(rows):
            near.setdefault((i // 8, j % 4), []).append(i * rows + j)
            ring.setdefault((i % 8, j // 4), []).append(i * rows + j)
    return list(near.values()), list(ring.values())


def split_matrix():
    lane = np.arange(3 * LANES)
    fine_column = np.where(lane < 320, lane, lane - 384)[:, None]
    circle = np.arange(2 * LANES)
    coarse_column = np.where(circle < 192, circle, circle - 256)[None, :]
    return np.concatenate(
        [fine_column == 2 * coarse_column, fine_column == 2 * coarse_column + 1], axis=1
    ).astype(ml_dtypes.bfloat16)


def weave_matrix():
    lane = np.arange(2 * LANES)
    target = np.where(lane < LANES, 2 * lane, 2 * (lane - LANES) + 1)[:, None]
    return (target == lane[None, :]).astype(ml_dtypes.bfloat16)


def f32(*shape):
    return jax.ShapeDtypeStruct(shape, jnp.float32)


def vm(*shape):
    return pltpu.VMEM(shape, jnp.float32)


def make_shards(columns, rows):
    near, ring = gather_groups(columns, rows)
    axes = ("gx", "gy")

    def shards(*args):
        in_vmem = pl.BlockSpec(memory_space=pltpu.VMEM)
        in_smem = pl.BlockSpec(memory_space=pltpu.SMEM)
        in_hbm = pl.BlockSpec(memory_space=pltpu.HBM)

        def call(kernel, ins, outs, scratch=(), out_specs=None, cost=None, limit=48):
            return pl.pallas_call(
                kernel,
                out_shape=outs,
                in_specs=ins,
                out_specs=out_specs or ([in_vmem] * len(outs) if isinstance(outs, tuple) else in_vmem),
                scratch_shapes=list(scratch),
                compiler_params=pltpu.CompilerParams(vmem_limit_bytes=limit * 1024 * 1024),
                cost_estimate=cost,
            )

        fn, fb, _, _, _, cn, cb, _, _, _ = args
        first_side, second_side, first_rim, second_rim = call(
            pack,
            [in_hbm] * 10,
            (f32(PACKED_ROWS, LANES),) * 2 + (f32(RIM_ROWS, LANES),) * 2,
            [vm(*a.shape) for a in args] + [pltpu.SemaphoreType.DMA((len(PACK_SOURCES),))],
            limit=63,
        )(*args)
        sides = exchange(first_side, second_side, "gy", rows)
        rims = exchange(first_rim, second_rim, "gx", columns)
        first, second = call(
            pack_corners,
            [in_vmem] * 2,
            (f32(CORNER_ROWS, LANES),) * 2,
            cost=pl.CostEstimate(flops=10**12, bytes_accessed=10**9, transcendentals=0),
        )(*sides)
        corners = exchange(first, second, "gx", columns)
        near_size, ring_size = len(near[0]), len(ring[0])
        outs = (
            f32(3, 7, 16, 256),
            f32(3, 7, 8, 128),
            f32(2, 3, 2, 16, 128),
            f32(2, 3, 8, 128),
            f32(4, 3, 8, 128),
            f32(near_size, LANES),
        )
        scratch = (
            vm(3, 8, 3, 48, LANES),
            vm(8, 3, 48, LANES),
            vm(8, 3, 48, LANES),
            vm(8, 3, 48, LANES),
            vm(3, 9, 2, 24, LANES),
            vm(9, 2, 24, LANES),
            vm(9, 2, 24, LANES),
            vm(11, 2, 24, LANES),
            vm(3, 48, LANES),
            vm(8, 3, 32, LANES),
            vm(256, 512),
            vm(192, 256),
            vm(6, 3, 16, LANES),
        ) + (vm(48, LANES), vm(48, LANES), vm(24, LANES)) * 2
        fine_rate, coarse_rate, plane, iterate, lines, message = call(main_kernel, [in_vmem] * 18, outs, scratch)(
            *args,
            *sides,
            *rims,
            *corners,
            jnp.asarray(split_matrix()),
            jnp.asarray(weave_matrix()),
        )
        received = lax.all_to_all(message, axes, 0, 0, tiled=True, axis_index_groups=near)
        message = call(merge_kernel, [in_vmem], f32(ring_size, LANES))(received)
        received = lax.all_to_all(message, axes, 0, 0, tiled=True, axis_index_groups=ring)
        fine_next, coarse_next, ratio, square, flag = call(
            final_kernel,
            [in_vmem] * 9,
            (f32(*fn.shape), f32(*cn.shape), f32(1), f32(1), jax.ShapeDtypeStruct((1,), jnp.int32)),
            out_specs=[in_vmem] * 2 + [in_smem] * 3,
        )(received, fn, fb, cn, cb, fine_rate, coarse_rate, plane, iterate)

        def plain():
            values = jnp.abs(lines[0::2] + square[0] * lines[1::2])
            tops = lax.pmax(jnp.max(values, axis=(1, 2, 3)), axes)
            return tops[1] / (tops[0] + 1e-06)

        reduction = lax.cond(flag[0] > 0, plain, lambda: ratio[0])
        return fine_next, coarse_next, reduction

    return shards


def solution(mesh):
    placed = (
        P(None, None, "gx", "gy"),
        P(None, None, "gx", "gy"),
        P(None, "gx", "gy"),
        P(None, "gx", "gy"),
        P(None, "gx", "gy"),
        P(None, None, "gx", "gy"),
        P(None, None, "gx", "gy"),
        P(None, "gx", "gy"),
        P(None, "gx", "gy"),
        P(None, "gx", "gy"),
    )
    return jax.shard_map(
        make_shards(mesh.shape["gx"], mesh.shape["gy"]),
        mesh=mesh,
        in_specs=placed,
        out_specs=(P(None, None, "gx", "gy"), P(None, None, "gx", "gy"), P()),
        check_vma=False,
    )
```

```python
import jax
import jax.numpy as jnp
import ml_dtypes
import numpy as np
from jax import lax
from jax.experimental import pallas as pl
from jax.experimental.pallas import tpu as pltpu
from jax.sharding import PartitionSpec as P

ITERS = 3
LANES = 128
NAMES = ("fn", "fb", "fd", "fs", "fl", "cn", "cb", "cd", "cs", "cl")

DEEP_NOW = [("fn", (c, k)) for c in range(3) for k in (5, 6, 7)]
THIN_NOW = [("fn", (c, k)) for c in range(3) for k in range(5)]
DEEP_REST = [("fb", (c, 6)) for c in range(3)] + [("fd", (6,)), ("fs", (6,)), ("fl", (6,)), ("fs", (7,)), ("fl", (7,))]
COARSE_NOW = [("cn", (c, k)) for c in range(3) for k in range(3)]
COARSE_REST = [("cb", (c, k)) for c in range(3) for k in range(2)] + [
    ("cd", (1,)),
    ("cs", (0,)),
    ("cl", (0,)),
    ("cs", (1,)),
    ("cl", (1,)),
]
COARSE_THIN = [("cn", (c, k)) for c in range(3) for k in range(3, 8)]

TILE_ROWS = {"A": (0, 16), "B": (16, 16), "C": (32, 8)}
TILE_RIM = {"A": 9, "B": 7, "C": 5}
PACKED_ROWS = 40


def plan():
    entries, lane, row = [], {"A": 0, "B": 0, "C": 0}, 0
    for tile, keys, low, high in (
        ("A", DEEP_NOW, 9, 8),
        ("A", THIN_NOW, 2, 2),
        ("B", DEEP_REST, 7, 6),
        ("C", COARSE_NOW, 5, 5),
        ("C", COARSE_REST, 4, 4),
        ("C", COARSE_THIN, 2, 2),
    ):
        for key in keys:
            own = 1 if tile == "C" else 2
            entries.append((key, low, high, tile, lane[tile], row, own))
            lane[tile] += low
            row += own * low
    corners, corner_row = {}, 0
    for tile in "ABC":
        for side in range(2):
            corners[tile, side] = corner_row
            corner_row += TILE_RIM[tile]
    return entries, corners, -(-row // 8) * 8, -(-corner_row // 8) * 8


ENTRIES, CORNERS, RIM_ROWS, CORNER_ROWS = plan()

PACK_SOURCES = (
    ("fn", ()),
    ("fb", (slice(None), slice(6, 7))),
    ("fd", (slice(6, 7),)),
    ("fs", (slice(6, 8),)),
    ("fl", (slice(6, 8),)),
    ("cn", ()),
    ("cb", (slice(None), slice(0, 2))),
    ("cd", (slice(1, 2),)),
    ("cs", (slice(0, 2),)),
    ("cl", (slice(0, 2),)),
)

SLOTS = 31
PEAK_LANE = 31
FLAG_LANE = 63
STEP_LOW = 0.02
FAR = -1.0e30


def iota(shape, dim):
    return lax.broadcasted_iota(jnp.int32, shape, dim)


def turned(value, steps, axis):
    size = value.shape[axis]
    steps = steps % size
    return value if steps == 0 else pltpu.roll(value, steps, axis)


def own_tile(refs, key, tile):
    name, index = key
    return refs[name][index + (slice(None), slice(tile * LANES, (tile + 1) * LANES))]


def is_even(axis):
    return lax.axis_index(axis) % 2 == 0


def pair(axis, low, high):
    even = is_even(axis)
    return jnp.where(even, low, high), jnp.where(even, high, low)


def pack(*refs):
    sources = dict(zip(NAMES, refs[:10]))
    targets, packs = refs[10:14], refs[14:18]
    column_outs, row_outs = packs[:2], packs[2:]
    named = dict(zip(NAMES, refs[18:28]))
    sems, out_sems = refs[28:30]
    sends = [pltpu.make_async_copy(source, target, out_sems.at[i]) for i, (source, target) in enumerate(zip(packs, targets))]
    copies = []
    for i, (name, part) in enumerate(PACK_SOURCES):
        source, target = sources[name], named[name]
        if part:
            source, target = source.at[part], target.at[part]
        copies.append(pltpu.make_async_copy(source, target, sems.at[i]))
    for copy in copies:
        copy.start()
    for copy in copies:
        copy.wait()
    for tile, (base, rows) in TILE_ROWS.items():
        lane = iota((rows, LANES), 1)
        low_sum = jnp.zeros((rows, LANES), jnp.float32)
        high_sum = low_sum
        for key, low, _, where, at, _, own in ENTRIES:
            if where != tile:
                continue
            inside = (lane >= at) & (lane < at + low)
            low_sum = jnp.where(inside, turned(own_tile(named, key, own - 1), at + low, 1), low_sum)
            high_sum = jnp.where(inside, turned(own_tile(named, key, 0), at, 1), high_sum)
        span = slice(base, base + rows)
        column_outs[0][span, :], column_outs[1][span, :] = pair("gy", low_sum, high_sum)
    for send in sends[:2]:
        send.start()
    row_outs[0][RIM_ROWS - 8 :, :] = jnp.zeros((8, LANES), jnp.float32)
    row_outs[1][RIM_ROWS - 8 :, :] = jnp.zeros((8, LANES), jnp.float32)
    for (name, index), low, _, _, _, row, own in ENTRIES:
        ref = named[name]
        rows = ref.shape[-2]
        for tile in range(own):
            lanes = slice(tile * LANES, (tile + 1) * LANES)
            span = slice(row + tile * low, row + tile * low + low)
            row_outs[0][span, :], row_outs[1][span, :] = pair(
                "gx", ref[index + (slice(rows - low, rows), lanes)], ref[index + (slice(0, low), lanes)]
            )
    for send in sends[2:]:
        send.start()
    for send in sends:
        send.wait()


def pack_corners(first, second, first_out, second_out):
    first_out[CORNER_ROWS - 8 :, :] = jnp.zeros((8, LANES), jnp.float32)
    second_out[CORNER_ROWS - 8 :, :] = jnp.zeros((8, LANES), jnp.float32)
    for tile, (base, rows) in TILE_ROWS.items():
        rim = TILE_RIM[tile]
        end, begin = slice(base + rows - rim, base + rows), slice(base, base + rim)
        ends = pair("gy", second[end, :], first[end, :])
        begins = pair("gy", second[begin, :], first[begin, :])
        for side in range(2):
            row = CORNERS[tile, side]
            first_out[row : row + rim, :], second_out[row : row + rim, :] = pair("gx", ends[side], begins[side])


def across(tiles, steps, wanted):
    count = len(tiles)
    lane = iota(tiles[0].shape, 1)
    rolled = [turned(tile, -steps, 1) for tile in tiles]
    if steps > 0:
        return [jnp.where(lane < LANES - steps, rolled[t], rolled[(t + 1) % count]) for t in range(wanted)]
    return [jnp.where(lane >= -steps, rolled[t], rolled[(t - 1) % count]) for t in range(wanted)]


def first_of(down2, down1, up1, up2, spacing):
    return (8.0 * (up1 - down1) - (up2 - down2)) * (1.0 / (12.0 * spacing))


def second_of(down2, down1, here, up1, up2, spacing):
    return (16.0 * (up1 + down1) - (up2 + down2) - 30.0 * here) * (1.0 / (12.0 * spacing * spacing))


def across_all(tiles, wanted):
    return [across(tiles, steps, wanted) for steps in (-2, -1, 1, 2)]


def slopes(field, along_x, along_y, plane, start, rows, wanted, spacing):
    count = field.shape[2]
    for t in range(count):
        down2, down1, up1, up2 = (field[0, plane, t, pl.ds(start + d, rows), :] for d in (-2, -1, 1, 2))
        along_x[plane, t, start : start + rows, :] = first_of(down2, down1, up1, up2, spacing)
    span = slice(start - 4, start + rows + 4)
    shifted = across_all([field[1, plane, t, span, :] for t in range(count)], wanted)
    for t in range(wanted):
        along_y[plane, t, span, :] = first_of(*(s[t] for s in shifted), spacing)


def acceleration(field, along_x, along_y, mixed, planes, start, rows, wanted, spacing, shear, lame):
    above, plane, under = planes
    count = field.shape[2]
    half = 1.0 / (2.0 * spacing)
    square = 1.0 / (spacing * spacing)
    span = slice(start, start + rows)
    wide = slice(start - 4, start + rows + 4)
    for t in range(wanted):
        mixed[t, wide, :] = along_y[plane, t, wide, :] + half * (
            field[2, under, t, wide, :] - field[2, above, t, wide, :]
        )
    twist = [
        along_x[plane, t, span, :] + half * (field[2, under, t, span, :] - field[2, above, t, span, :])
        for t in range(count)
    ]
    twist = across_all(twist, wanted)
    laps, seconds = [], []
    for c in range(3):
        shifted = across_all([field[c, plane, t, span, :] for t in range(count)], wanted)
        lap, second = [], []
        for t in range(wanted):
            here = field[c, plane, t, span, :]
            down2, down1, up1, up2 = (field[c, plane, t, pl.ds(start + d, rows), :] for d in (-2, -1, 1, 2))
            in_x = second_of(down2, down1, here, up1, up2, spacing)
            in_y = second_of(shifted[0][t], shifted[1][t], here, shifted[2][t], shifted[3][t], spacing)
            in_z = square * (field[c, under, t, span, :] - 2.0 * here + field[c, above, t, span, :])
            lap.append(in_x + in_y + in_z)
            second.append((in_x, in_y, in_z)[c])
        laps.append(lap)
        seconds.append(second)
    out = [[], [], []]
    for t in range(wanted):
        ends = (mixed[t, pl.ds(start + d, rows), :] for d in (-2, -1, 1, 2))
        div_x = seconds[0][t] + first_of(*ends, spacing)
        div_y = seconds[1][t] + first_of(*(s[t] for s in twist), spacing)
        lower = along_x[under, t, span, :] + along_y[under, t, span, :]
        upper = along_x[above, t, span, :] + along_y[above, t, span, :]
        div_z = seconds[2][t] + half * (lower - upper)
        bulk = lame[t] + shear[t]
        for c, div in enumerate((div_x, div_y, div_z)):
            out[c].append(shear[t] * laps[c][t] + bulk * div)
    return out


def exact_dot(value, pick):
    high = value.astype(jnp.bfloat16)
    rest = value - high.astype(jnp.float32)
    middle = rest.astype(jnp.bfloat16)
    low = (rest - middle.astype(jnp.float32)).astype(jnp.bfloat16)
    dot = lambda part: jnp.dot(part, pick, preferred_element_type=jnp.float32)
    return dot(high) + (dot(middle) + dot(low))


def prolonged(tiles):
    odd_x = [0.5 * (tile + turned(tile, -1, 0)) for tile in tiles]
    next_y = across(tiles, 1, 2)
    next_odd = across(odd_x, 1, 2)
    return (
        tiles,
        [0.5 * (a + b) for a, b in zip(tiles, next_y)],
        odd_x,
        [0.5 * (a + b) for a, b in zip(odd_x, next_odd)],
    )


def restricted(parts):
    even_even, even_odd, odd_even, odd_odd = parts
    even = [0.5 * a + 0.25 * (b + turned(b, 1, 0)) for a, b in zip(even_even, odd_even)]
    odd = [0.5 * a + 0.25 * (b + turned(b, 1, 0)) for a, b in zip(even_odd, odd_odd)]
    return [0.5 * a + 0.25 * (b + c) for a, b, c in zip(even, odd, across(odd, -1, 2))]


def largest(values):
    total = values[0]
    for value in values[1:]:
        total = jnp.maximum(total, value)
    return jnp.max(total)


def smallest(values):
    total = values[0]
    for value in values[1:]:
        total = jnp.minimum(total, value)
    return jnp.min(total)


def pick(lines, marks, wanted):
    begin = smallest([jnp.where(m == wanted, a, -FAR) for m, (a, _) in zip(marks, lines)])
    slope = largest([jnp.where(m == wanted, b, FAR) for m, (_, b) in zip(marks, lines)])
    return begin, slope


def top_line(lines, step):
    values = [a + step * b for a, b in lines]
    top = largest(values)
    return pick(lines, values, top)


def next_line(lines, begin, slope, limit):
    crossings = []
    for a, b in lines:
        steeper = b - slope
        crossings.append(jnp.where(steeper > 0.0, (begin - a) / steeper, -FAR))
    nearest = smallest(crossings)
    found = nearest <= limit
    new_begin, new_slope = pick(lines, crossings, nearest)
    return jnp.where(found, new_begin, begin), jnp.where(found, new_slope, slope), found


def envelopes(first, last, peak):
    lane = iota((1, LANES), 1)
    bound = 0.3 / jnp.full((8, LANES), peak, jnp.float32)
    bound = bound * bound * 1.00001
    limit = jnp.max(bound)
    first_begin, first_slope = top_line(first, STEP_LOW)
    last_begin, last_slope = top_line(last, STEP_LOW)
    first_top = largest([a + bound * b for a, b in first])
    last_top = largest([a + bound * b for a, b in last])
    single = (jnp.max(first_begin + bound * first_slope) >= first_top) & (
        jnp.max(last_begin + bound * last_slope) >= last_top
    )
    message = jnp.where(
        lane < 32,
        first_begin,
        jnp.where(lane < 64, first_slope, jnp.where(lane < 96, last_begin, last_slope)),
    )

    def more(state):
        return (state[0] < SLOTS) & (state[1] > 0)

    def step(state):
        n, _, fa, fb, la, lb, message = state
        fa, fb, found_first = next_line(first, fa, fb, limit)
        la, lb, found_last = next_line(last, la, lb, limit)
        message = jnp.where(lane == n, fa, message)
        message = jnp.where(lane == n + 32, fb, message)
        message = jnp.where(lane == n + 64, la, message)
        message = jnp.where(lane == n + 96, lb, message)
        found = (found_first | found_last).astype(jnp.int32)
        return n + 1, found, fa, fb, la, lb, message

    left = jnp.where(single, 0, 1).astype(jnp.int32)
    start = (jnp.int32(1), left, first_begin, first_slope, last_begin, last_slope, message)
    _, left, _, _, _, _, message = lax.while_loop(more, step, start)
    return message, left.astype(jnp.float32)


def sealed(message, peak, flag):
    lane = iota((1, LANES), 1)
    return jnp.where(lane == PEAK_LANE, peak, jnp.where(lane == FLAG_LANE, flag, message))


def opened(received):
    first, last = [], []
    rows = received.shape[0]
    lane = iota((8, LANES), 1)
    peak, flag = [], []
    for r in range(0, rows, 8):
        begin = received[r : r + 8, :]
        slope = turned(begin, -32, 1)
        in_first = lane < SLOTS
        in_last = (lane >= 64) & (lane < 64 + SLOTS)
        first.append((jnp.where(in_first, begin, FAR), jnp.where(in_first, slope, 0.0)))
        last.append((jnp.where(in_last, begin, FAR), jnp.where(in_last, slope, 0.0)))
        peak.append(jnp.where(lane == PEAK_LANE, begin, 0.0))
        flag.append(jnp.where(lane == FLAG_LANE, begin, 0.0))
    return first, last, largest(peak), largest(flag)


def main_kernel(*refs):
    named = dict(zip(NAMES, refs[:10]))
    sides, rim_sources, corners = refs[10:12], refs[12:14], refs[14:16]
    split_pick, weave_pick = refs[16:18]
    fine_rate, coarse_rate, plane_out, iterate_out, lines_out, message_out = refs[18:24]
    fine, fine_x, fine_y, rest, coarse, coarse_x, coarse_y, coarse_rest = refs[24:32]
    mixed, planes, parted, woven, ends = refs[32:37]
    packed = dict(zip("ABC", zip(refs[37:40], refs[40:43])))
    rims, sems = refs[43:45], refs[45]
    copies = [pltpu.make_async_copy(source, rims[i], sems.at[i]) for i, source in enumerate(rim_sources)]
    for copy in copies:
        copy.start()

    def received(axis, pieces, span):
        return pair(axis, pieces[1][span, :], pieces[0][span, :])

    for tile, (base, rows) in TILE_ROWS.items():
        rim = TILE_RIM[tile]
        own = received("gy", sides, slice(base, base + rows))
        for side in range(2):
            target = packed[tile][side]
            target[...] = jnp.zeros(target.shape, jnp.float32)
            target[rows : 2 * rows, :] = own[side]
            row = CORNERS[tile, side]
            low, high = received("gx", corners, slice(row, row + rim))
            target[rows - rim : rows, :] = low
            target[2 * rows : 2 * rows + rim, :] = high

    slot = {key: i for i, key in enumerate(DEEP_REST)}
    coarse_slot = {key: i for i, key in enumerate(COARSE_REST)}

    def home(key):
        if key in slot:
            return rest.at[slot[key]]
        if key in coarse_slot:
            return coarse_rest.at[coarse_slot[key]]
        return (fine if key[0] == "fn" else coarse).at[key[1]]

    for key, low, high, tile, at, row, own in ENTRIES:
        target = home(key)
        rows = TILE_ROWS[tile][1]
        total = target.shape[1]
        for t in range(own):
            if low > 2:
                target[t, 0:rows, :] = jnp.zeros((rows, LANES), jnp.float32)
                target[t, 2 * rows : total, :] = jnp.zeros((total - 2 * rows, LANES), jnp.float32)
            target[t, rows : 2 * rows, :] = own_tile(named, key, t)
        low_side, high_side = packed[tile][0][...], packed[tile][1][...]
        lane = iota(low_side.shape, 1)
        target[own, :, :] = jnp.where(
            lane < high,
            turned(high_side, -at, 1),
            jnp.where(lane >= LANES - low, turned(low_side, -(at + low), 1), 0.0),
        )
    for copy in copies:
        copy.wait()
    for key, low, high, tile, at, row, own in ENTRIES:
        target = home(key)
        rows = TILE_ROWS[tile][1]
        for t in range(own):
            below, beyond = received("gx", rims, slice(row + t * low, row + t * low + low))
            target[t, rows - low : rows, :] = below
            target[t, 2 * rows : 2 * rows + low, :] = beyond
    coarse[:, 8] = jnp.zeros(coarse.shape[:1] + coarse.shape[2:], jnp.float32)

    for k in range(5):
        slopes(fine, fine_x, fine_y, k, 16, 16, 2, 1.0)
    for k in (5, 6, 7):
        slopes(fine, fine_x, fine_y, k, 8, 32, 3, 1.0)

    def fine_plane(k):
        above = 1 if k == 0 else k - 1
        own = [slice(t * LANES, (t + 1) * LANES) for t in range(2)]
        shear = [named["fs"][k, :, lanes] for lanes in own]
        lame = [named["fl"][k, :, lanes] for lanes in own]
        accel = acceleration(fine, fine_x, fine_y, mixed, (above, k, k + 1), 16, 16, 2, 1.0, shear, lame)
        for c in range(3):
            for t in range(2):
                fine_rate[c, k, :, own[t]] = accel[c][t] / named["fd"][k, :, own[t]]

    for k in range(6):
        fine_plane(k)

    window = slice(8, 40)
    shear = [rest[slot[("fs", (6,))], t, window, :] for t in range(3)]
    lame = [rest[slot[("fl", (6,))], t, window, :] for t in range(3)]
    accel = acceleration(fine, fine_x, fine_y, mixed, (5, 6, 7), 8, 32, 3, 1.0, shear, lame)
    for t in range(3):
        density = rest[slot[("fd", (6,))], t, window, :]
        filled = density > 0.0
        density = jnp.where(filled, density, 1.0)
        for c in range(3):
            rate = jnp.where(filled, accel[c][t] / density, 0.0)
            planes[3 + c, t, :, :] = rate
            planes[c, t, :, :] = 2.0 * fine[c, 6, t, window, :] - rest[c, t, window, :]
            if t < 2:
                fine_rate[c, 6, :, t * LANES : (t + 1) * LANES] = rate[8:24, :]
        fine_shear = rest[slot[("fs", (7,))], t, window, :]
        planes[6, t, :, :] = fine_shear
        planes[7, t, :, :] = rest[slot[("fl", (7,))], t, window, :] + 2.0 * fine_shear

    stacked = jnp.concatenate(
        [
            jnp.concatenate([planes[p, t, pl.ds(odd, 16, stride=2), :] for t in range(3)], axis=1)
            for p in range(8)
            for odd in range(2)
        ],
        axis=0,
    )
    parted[...] = exact_dot(stacked, split_pick[...])

    def four(p):
        return tuple(
            [
                parted[p * 32 + odd_x * 16 : p * 32 + odd_x * 16 + 16, (odd_y * 2 + t) * LANES : (odd_y * 2 + t + 1) * LANES]
                for t in range(2)
            ]
            for odd_x in range(2)
            for odd_y in range(2)
        )

    for k in range(8):
        slopes(coarse, coarse_x, coarse_y, k, 4, 16, 2, 2.0)
    coarse_x[8] = jnp.zeros(coarse_x.shape[1:], jnp.float32)
    coarse_y[8] = jnp.zeros(coarse_y.shape[1:], jnp.float32)

    def coarse_plane(k):
        shear = [named["cs"][k]]
        lame = [named["cl"][k]]
        accel = acceleration(coarse, coarse_x, coarse_y, mixed, (k - 1, k, k + 1), 8, 8, 1, 2.0, shear, lame)
        for c in range(3):
            coarse_rate[c, k - 1] = accel[c][0] / named["cd"][k]

    for k in range(2, 8):
        coarse_plane(k)
    band = slice(4, 20)

    def coarse_pair(name, k):
        return [coarse_rest[coarse_slot[(name, (k,))], t, band, :] for t in range(2)]

    shear, lame, density = coarse_pair("cs", 1), coarse_pair("cl", 1), coarse_pair("cd", 1)
    accel = acceleration(coarse, coarse_x, coarse_y, mixed, (0, 1, 2), 4, 16, 2, 2.0, shear, lame)
    below_rate = [[], [], []]
    for c in range(3):
        for t in range(2):
            filled = density[t] > 0.0
            rate = jnp.where(filled, accel[c][t] / jnp.where(filled, density[t], 1.0), 0.0)
            below_rate[c].append(rate)
        coarse_rate[c, 0] = below_rate[c][0][4:12, :]

    shear, lame = coarse_pair("cs", 0), coarse_pair("cl", 0)
    row = iota((16, LANES), 0) + (lax.axis_index("gx") * 8 - 4)
    lane = iota((16, LANES), 1) + lax.axis_index("gy") * LANES
    column = [lane, jnp.where(iota((16, LANES), 1) < 64, lane + LANES, lane - LANES)]
    extent = (lax.axis_size("gx") * 8, lax.axis_size("gy") * LANES)
    fine_moduli = (four(6), four(6), four(7))
    coarse_moduli = (shear, shear, [l + 2.0 * s for l, s in zip(lame, shear)])
    for c in range(3):
        moduli = fine_moduli[c]
        half = [0.5 * m for m in coarse_moduli[c]]
        spread = restricted(moduli)
        inverse = []
        for t in range(2):
            diagonal = half[t] + 0.5625 * spread[t]
            x, y = row, column[t]
            inside = (x >= 0) & (x < extent[0]) & (y >= 0) & (y < extent[1]) & (diagonal > 0.0)
            inverse.append(jnp.where(inside, 1.0 / jnp.where(inside, diagonal, 1.0), 0.0))
        for part in range(2):
            if part == 0:
                now = [coarse[c, 0, t, band, :] for t in range(2)]
                before = [coarse_rest[coarse_slot[("cb", (c, 0))], t, band, :] for t in range(2)]
                iterate = [2.0 * a - b for a, b in zip(now, before)]
                now = [coarse[c, 1, t, band, :] for t in range(2)]
                before = [coarse_rest[coarse_slot[("cb", (c, 1))], t, band, :] for t in range(2)]
                below = [2.0 * a - b for a, b in zip(now, before)]
            else:
                iterate = [jnp.zeros((16, LANES), jnp.float32)] * 2
                below = below_rate[c]
            above = four(3 * part + c)
            fixed = restricted([[m * a for m, a in zip(ms, as_)] for ms, as_ in zip(moduli, above)])
            fixed = [h * b + f for h, b, f in zip(half, below, fixed)]

            def mismatch_of(iterate):
                stress = [[m * a for m, a in zip(ms, ps)] for ms, ps in zip(moduli, prolonged(iterate))]
                return [h * i + (s - f) for h, i, s, f in zip(half, iterate, restricted(stress), fixed)]

            mismatch = mismatch_of(iterate)
            ends[part, c] = mismatch[0]
            for _ in range(ITERS):
                iterate = [i - m * v for i, m, v in zip(iterate, mismatch, inverse)]
                mismatch = mismatch_of(iterate)
            ends[2 + part, c] = mismatch[0]
            ends[4 + part, c] = iterate[0]
            even_even, even_odd, odd_even, odd_odd = prolonged(iterate)
            at = (part * 3 + c) * 32
            woven[at : at + 16, 0:LANES] = even_even[0]
            woven[at : at + 16, LANES : 2 * LANES] = even_odd[0]
            woven[at + 16 : at + 32, 0:LANES] = odd_even[0]
            woven[at + 16 : at + 32, LANES : 2 * LANES] = odd_odd[0]

    woven[...] = exact_dot(woven[...], weave_pick[...])
    for part in range(2):
        for c in range(3):
            iterate_out[part, c] = ends[4 + part, c, 4:12, :]
            for odd in range(2):
                at = (part * 3 + c) * 32 + odd * 16 + 4
                for t in range(2):
                    plane_out[part, c, t, pl.ds(odd, 8, stride=2), :] = woven[
                        at : at + 8, t * LANES : (t + 1) * LANES
                    ]

    lines = []
    for which in range(2):
        found = []
        for c in range(3):
            begin, slope = ends[2 * which, c, 4:12, :], ends[2 * which + 1, c, 4:12, :]
            lines_out[2 * which, c] = begin
            lines_out[2 * which + 1, c] = slope
            found += [(begin, slope), (-begin, -slope)]
        lines.append(found)
    ratio = (named["fl"][...] + 2.0 * named["fs"][...]) / named["fd"][...]
    coarse_ratio = (named["cl"][...] + 2.0 * named["cs"][...]) / named["cd"][...]
    fine_peak = jnp.sqrt(jnp.full((8, LANES), jnp.max(ratio), jnp.float32))
    coarse_peak = jnp.sqrt(jnp.full((8, LANES), jnp.max(coarse_ratio), jnp.float32))
    peak = jnp.max(jnp.maximum(fine_peak, 0.5 * coarse_peak))
    message, flag = envelopes(lines[0], lines[1], peak)
    message_out[...] = jnp.broadcast_to(sealed(message, peak, flag), message_out.shape)


def merge_kernel(received, message_out):
    first, last, peak, flag = opened(received)
    message, full = envelopes(first, last, peak)
    message_out[...] = jnp.broadcast_to(sealed(message, peak, jnp.maximum(flag, full)), message_out.shape)


def final_kernel(
    received, fn, fb, cn, cb, fine_rate, coarse_rate, plane, iterate, fine_out, coarse_out, ratio_out, square_out, flag_out
):
    first, last, peak, flag = opened(received)
    step = 0.3 / jnp.full((8, LANES), peak, jnp.float32)
    square = step * step
    first_max = largest([a + square * b for a, b in first])
    last_max = largest([a + square * b for a, b in last])
    ratio = last_max / (jnp.full((8, LANES), first_max, jnp.float32) + 1e-06)
    ratio_out[0] = jnp.max(ratio)
    square_out[0] = jnp.max(square)
    flag_out[0] = jnp.where((flag > 0.0) | (jnp.max(square) < STEP_LOW), 1, 0)
    square = square[0:1, 0:1]
    for c in range(3):
        fine_out[c, 0:7] = 2.0 * fn[c, 0:7] - fb[c, 0:7] + square * fine_rate[c]
        coarse_out[c, 1:8] = 2.0 * cn[c, 1:8] - cb[c, 1:8] + square * coarse_rate[c]
        coarse_out[c, 0] = iterate[0, c] + square * iterate[1, c]
        for t in range(2):
            fine_out[c, 7, :, t * LANES : (t + 1) * LANES] = plane[0, c, t] + square * plane[1, c, t]


def exchange(first, second, axis, count):
    near = [(i, i ^ 1) for i in range(count) if i ^ 1 < count]
    far = [(i, i + 1) for i in range(1, count - 1, 2)] + [(i + 1, i) for i in range(1, count - 1, 2)]
    return lax.ppermute(first, axis, near), lax.ppermute(second, axis, far)


def gather_groups(columns, rows):
    ring, plane = {}, {}
    for i in range(columns):
        for j in range(rows):
            chip_y, core, z, x = i // 2 % 4, i % 2, (i // 8, j % 4), j // 4
            ring.setdefault((x, chip_y), []).append(i * rows + j)
            plane.setdefault((z, core), []).append(i * rows + j)
    return list(ring.values()), list(plane.values())


def split_matrix():
    lane = np.arange(3 * LANES)
    fine_column = np.where(lane < 320, lane, lane - 384)[:, None]
    circle = np.arange(2 * LANES)
    coarse_column = np.where(circle < 192, circle, circle - 256)[None, :]
    return np.concatenate(
        [fine_column == 2 * coarse_column, fine_column == 2 * coarse_column + 1], axis=1
    ).astype(ml_dtypes.bfloat16)


def weave_matrix():
    lane = np.arange(2 * LANES)
    target = np.where(lane < LANES, 2 * lane, 2 * (lane - LANES) + 1)[:, None]
    return (target == lane[None, :]).astype(ml_dtypes.bfloat16)


def f32(*shape):
    return jax.ShapeDtypeStruct(shape, jnp.float32)


def vm(*shape):
    return pltpu.VMEM(shape, jnp.float32)


def make_shards(columns, rows):
    ring, plane_groups = gather_groups(columns, rows)
    axes = ("gx", "gy")

    def shards(*args):
        in_vmem = pl.BlockSpec(memory_space=pltpu.VMEM)
        in_smem = pl.BlockSpec(memory_space=pltpu.SMEM)
        in_hbm = pl.BlockSpec(memory_space=pltpu.HBM)

        def call(kernel, ins, outs, scratch=(), out_specs=None, cost=None, limit=48):
            return pl.pallas_call(
                kernel,
                out_shape=outs,
                in_specs=ins,
                out_specs=out_specs or ([in_vmem] * len(outs) if isinstance(outs, tuple) else in_vmem),
                scratch_shapes=list(scratch),
                compiler_params=pltpu.CompilerParams(vmem_limit_bytes=limit * 1024 * 1024),
                cost_estimate=cost,
            )

        fn, fb, _, _, _, cn, cb, _, _, _ = args
        first_side, second_side, first_rim, second_rim = call(
            pack,
            [in_hbm] * 10,
            (f32(PACKED_ROWS, LANES),) * 2 + (f32(RIM_ROWS, LANES),) * 2,
            [vm(PACKED_ROWS, LANES)] * 2
            + [vm(RIM_ROWS, LANES)] * 2
            + [vm(*a.shape) for a in args]
            + [pltpu.SemaphoreType.DMA((len(PACK_SOURCES),)), pltpu.SemaphoreType.DMA((4,))],
            out_specs=[in_hbm] * 4,
            limit=63,
        )(*args)
        sides = exchange(first_side, second_side, "gy", rows)
        rims = exchange(first_rim, second_rim, "gx", columns)
        first, second = call(
            pack_corners,
            [in_vmem] * 2,
            (f32(CORNER_ROWS, LANES),) * 2,
            cost=pl.CostEstimate(flops=10**12, bytes_accessed=10**9, transcendentals=0),
        )(*sides)
        corners = exchange(first, second, "gx", columns)
        ring_size, plane_size = len(ring[0]), len(plane_groups[0])
        outs = (
            f32(3, 7, 16, 256),
            f32(3, 7, 8, 128),
            f32(2, 3, 2, 16, 128),
            f32(2, 3, 8, 128),
            f32(4, 3, 8, 128),
            f32(ring_size, LANES),
        )
        scratch = (
            vm(3, 8, 3, 48, LANES),
            vm(8, 3, 48, LANES),
            vm(8, 3, 48, LANES),
            vm(8, 3, 48, LANES),
            vm(3, 9, 2, 24, LANES),
            vm(9, 2, 24, LANES),
            vm(9, 2, 24, LANES),
            vm(11, 2, 24, LANES),
            vm(3, 48, LANES),
            vm(8, 3, 32, LANES),
            vm(256, 512),
            vm(192, 256),
            vm(6, 3, 16, LANES),
        ) + (vm(48, LANES), vm(48, LANES), vm(24, LANES)) * 2
        scratch += (vm(RIM_ROWS, LANES), vm(RIM_ROWS, LANES), pltpu.SemaphoreType.DMA((2,)))
        ins = [in_vmem] * 12 + [in_hbm] * 2 + [in_vmem] * 4
        fine_rate, coarse_rate, plane, iterate, lines, message = call(main_kernel, ins, outs, scratch)(
            *args,
            *sides,
            *rims,
            *corners,
            jnp.asarray(split_matrix()),
            jnp.asarray(weave_matrix()),
        )
        received = lax.all_to_all(message, axes, 0, 0, tiled=True, axis_index_groups=ring)
        message = call(merge_kernel, [in_vmem], f32(plane_size, LANES))(received)
        received = lax.all_to_all(message, axes, 0, 0, tiled=True, axis_index_groups=plane_groups)
        fine_next, coarse_next, ratio, square, flag = call(
            final_kernel,
            [in_vmem] * 9,
            (f32(*fn.shape), f32(*cn.shape), f32(1), f32(1), jax.ShapeDtypeStruct((1,), jnp.int32)),
            out_specs=[in_vmem] * 2 + [in_smem] * 3,
        )(received, fn, fb, cn, cb, fine_rate, coarse_rate, plane, iterate)

        def plain():
            values = jnp.abs(lines[0::2] + square[0] * lines[1::2])
            tops = lax.pmax(jnp.max(values, axis=(1, 2, 3)), axes)
            return tops[1] / (tops[0] + 1e-06)

        reduction = lax.cond(flag[0] > 0, plain, lambda: ratio[0])
        return fine_next, coarse_next, reduction

    return shards


def solution(mesh):
    placed = (
        P(None, None, "gx", "gy"),
        P(None, None, "gx", "gy"),
        P(None, "gx", "gy"),
        P(None, "gx", "gy"),
        P(None, "gx", "gy"),
        P(None, None, "gx", "gy"),
        P(None, None, "gx", "gy"),
        P(None, "gx", "gy"),
        P(None, "gx", "gy"),
        P(None, "gx", "gy"),
    )
    return jax.shard_map(
        make_shards(mesh.shape["gx"], mesh.shape["gy"]),
        mesh=mesh,
        in_specs=placed,
        out_specs=(P(None, None, "gx", "gy"), P(None, None, "gx", "gy"), P()),
        check_vma=False,
    )
```

```python
import jax
import jax.numpy as jnp
import ml_dtypes
import numpy as np
from jax import lax
from jax.experimental import pallas as pl
from jax.experimental.pallas import tpu as pltpu
from jax.sharding import PartitionSpec as P

ITERS = 3
LANES = 128
NAMES = ("fn", "fb", "fd", "fs", "fl", "cn", "cb", "cd", "cs", "cl")

DEEP_NOW = [("fn", (c, k)) for c in range(3) for k in (5, 6, 7)]
THIN_NOW = [("fn", (c, k)) for c in range(3) for k in range(5)]
DEEP_REST = [("fb", (c, 6)) for c in range(3)] + [("fd", (6,)), ("fs", (6,)), ("fl", (6,)), ("fs", (7,)), ("fl", (7,))]
COARSE_NOW = [("cn", (c, k)) for c in range(3) for k in range(3)]
COARSE_REST = [("cb", (c, k)) for c in range(3) for k in range(2)] + [
    ("cd", (1,)),
    ("cs", (0,)),
    ("cl", (0,)),
    ("cs", (1,)),
    ("cl", (1,)),
]
COARSE_THIN = [("cn", (c, k)) for c in range(3) for k in range(3, 8)]

TILE_ROWS = {"A": (0, 16), "B": (16, 16), "C": (32, 8)}
TILE_RIM = {"A": 9, "B": 7, "C": 5}
PACKED_ROWS = 40


def plan():
    entries, lane, row = [], {"A": 0, "B": 0, "C": 0}, 0
    for tile, keys, low, high in (
        ("A", DEEP_NOW, 9, 8),
        ("A", THIN_NOW, 2, 2),
        ("B", DEEP_REST, 7, 6),
        ("C", COARSE_NOW, 5, 5),
        ("C", COARSE_REST, 4, 4),
        ("C", COARSE_THIN, 2, 2),
    ):
        for key in keys:
            own = 1 if tile == "C" else 2
            entries.append((key, low, high, tile, lane[tile], row, own))
            lane[tile] += low
            row += own * low
    corners, corner_row = {}, 0
    for tile in "ABC":
        for side in range(2):
            corners[tile, side] = corner_row
            corner_row += TILE_RIM[tile]
    return entries, corners, -(-row // 8) * 8, -(-corner_row // 8) * 8


ENTRIES, CORNERS, RIM_ROWS, CORNER_ROWS = plan()

PACK_SOURCES = (
    ("fn", ()),
    ("fb", (slice(None), slice(6, 7))),
    ("fd", (slice(6, 7),)),
    ("fs", (slice(6, 8),)),
    ("fl", (slice(6, 8),)),
    ("cn", ()),
    ("cb", (slice(None), slice(0, 2))),
    ("cd", (slice(1, 2),)),
    ("cs", (slice(0, 2),)),
    ("cl", (slice(0, 2),)),
)

SLOTS = 31
PEAK_LANE = 31
FLAG_LANE = 63
STEP_LOW = 0.02
FAR = -1.0e30


def iota(shape, dim):
    return lax.broadcasted_iota(jnp.int32, shape, dim)


def turned(value, steps, axis):
    size = value.shape[axis]
    steps = steps % size
    return value if steps == 0 else pltpu.roll(value, steps, axis)


def own_tile(refs, key, tile):
    name, index = key
    return refs[name][index + (slice(None), slice(tile * LANES, (tile + 1) * LANES))]


def is_even(axis):
    return lax.axis_index(axis) % 2 == 0


def pair(axis, low, high):
    even = is_even(axis)
    return jnp.where(even, low, high), jnp.where(even, high, low)


def pack(*refs):
    sources = dict(zip(NAMES, refs[:10]))
    targets, packs = refs[10:14], refs[14:18]
    column_outs, row_outs = packs[:2], packs[2:]
    named = dict(zip(NAMES, refs[18:28]))
    sems, out_sems = refs[28:30]
    sends = [pltpu.make_async_copy(source, target, out_sems.at[i]) for i, (source, target) in enumerate(zip(packs, targets))]
    copies = []
    for i, (name, part) in enumerate(PACK_SOURCES):
        source, target = sources[name], named[name]
        if part:
            source, target = source.at[part], target.at[part]
        copies.append(pltpu.make_async_copy(source, target, sems.at[i]))
    for copy in copies:
        copy.start()
    for copy in copies:
        copy.wait()
    for tile, (base, rows) in TILE_ROWS.items():
        lane = iota((rows, LANES), 1)
        low_sum = jnp.zeros((rows, LANES), jnp.float32)
        high_sum = low_sum
        for key, low, _, where, at, _, own in ENTRIES:
            if where != tile:
                continue
            inside = (lane >= at) & (lane < at + low)
            low_sum = jnp.where(inside, turned(own_tile(named, key, own - 1), at + low, 1), low_sum)
            high_sum = jnp.where(inside, turned(own_tile(named, key, 0), at, 1), high_sum)
        span = slice(base, base + rows)
        column_outs[0][span, :], column_outs[1][span, :] = pair("gy", low_sum, high_sum)
    for send in sends[:2]:
        send.start()
    row_outs[0][RIM_ROWS - 8 :, :] = jnp.zeros((8, LANES), jnp.float32)
    row_outs[1][RIM_ROWS - 8 :, :] = jnp.zeros((8, LANES), jnp.float32)
    for (name, index), low, _, _, _, row, own in ENTRIES:
        ref = named[name]
        rows = ref.shape[-2]
        for tile in range(own):
            lanes = slice(tile * LANES, (tile + 1) * LANES)
            span = slice(row + tile * low, row + tile * low + low)
            row_outs[0][span, :], row_outs[1][span, :] = pair(
                "gx", ref[index + (slice(rows - low, rows), lanes)], ref[index + (slice(0, low), lanes)]
            )
    for send in sends[2:]:
        send.start()
    for send in sends:
        send.wait()


def pack_corners(first, second, first_out, second_out):
    first_out[CORNER_ROWS - 8 :, :] = jnp.zeros((8, LANES), jnp.float32)
    second_out[CORNER_ROWS - 8 :, :] = jnp.zeros((8, LANES), jnp.float32)
    for tile, (base, rows) in TILE_ROWS.items():
        rim = TILE_RIM[tile]
        end, begin = slice(base + rows - rim, base + rows), slice(base, base + rim)
        ends = pair("gy", second[end, :], first[end, :])
        begins = pair("gy", second[begin, :], first[begin, :])
        for side in range(2):
            row = CORNERS[tile, side]
            first_out[row : row + rim, :], second_out[row : row + rim, :] = pair("gx", ends[side], begins[side])


def across(tiles, steps, wanted):
    count = len(tiles)
    lane = iota(tiles[0].shape, 1)
    rolled = [turned(tile, -steps, 1) for tile in tiles]
    if steps > 0:
        return [jnp.where(lane < LANES - steps, rolled[t], rolled[(t + 1) % count]) for t in range(wanted)]
    return [jnp.where(lane >= -steps, rolled[t], rolled[(t - 1) % count]) for t in range(wanted)]


def first_of(down2, down1, up1, up2, spacing):
    return (8.0 * (up1 - down1) - (up2 - down2)) * (1.0 / (12.0 * spacing))


def second_of(down2, down1, here, up1, up2, spacing):
    return (16.0 * (up1 + down1) - (up2 + down2) - 30.0 * here) * (1.0 / (12.0 * spacing * spacing))


def across_all(tiles, wanted):
    return [across(tiles, steps, wanted) for steps in (-2, -1, 1, 2)]


def slopes(field, along_x, along_y, plane, start, rows, wanted, spacing):
    count = field.count
    for t in range(count):
        down2, down1, up1, up2 = (field[0, plane, t, pl.ds(start + d, rows), :] for d in (-2, -1, 1, 2))
        along_x[plane, t, start : start + rows, :] = first_of(down2, down1, up1, up2, spacing)
    span = slice(start - 4, start + rows + 4)
    shifted = across_all([field[1, plane, t, span, :] for t in range(count)], wanted)
    for t in range(wanted):
        along_y[plane, t, span, :] = first_of(*(s[t] for s in shifted), spacing)


def acceleration(field, along_x, along_y, mixed, planes, start, rows, wanted, spacing, shear, lame):
    above, plane, under = planes
    count = field.count
    half = 1.0 / (2.0 * spacing)
    square = 1.0 / (spacing * spacing)
    span = slice(start, start + rows)
    wide = slice(start - 4, start + rows + 4)
    for t in range(wanted):
        mixed[t, wide, :] = along_y[plane, t, wide, :] + half * (
            field[2, under, t, wide, :] - field[2, above, t, wide, :]
        )
    twist = [
        along_x[plane, t, span, :] + half * (field[2, under, t, span, :] - field[2, above, t, span, :])
        for t in range(count)
    ]
    twist = across_all(twist, wanted)
    laps, seconds = [], []
    for c in range(3):
        shifted = across_all([field[c, plane, t, span, :] for t in range(count)], wanted)
        lap, second = [], []
        for t in range(wanted):
            here = field[c, plane, t, span, :]
            down2, down1, up1, up2 = (field[c, plane, t, pl.ds(start + d, rows), :] for d in (-2, -1, 1, 2))
            in_x = second_of(down2, down1, here, up1, up2, spacing)
            in_y = second_of(shifted[0][t], shifted[1][t], here, shifted[2][t], shifted[3][t], spacing)
            in_z = square * (field[c, under, t, span, :] - 2.0 * here + field[c, above, t, span, :])
            lap.append(in_x + in_y + in_z)
            second.append((in_x, in_y, in_z)[c])
        laps.append(lap)
        seconds.append(second)
    out = [[], [], []]
    for t in range(wanted):
        ends = (mixed[t, pl.ds(start + d, rows), :] for d in (-2, -1, 1, 2))
        div_x = seconds[0][t] + first_of(*ends, spacing)
        div_y = seconds[1][t] + first_of(*(s[t] for s in twist), spacing)
        lower = along_x[under, t, span, :] + along_y[under, t, span, :]
        upper = along_x[above, t, span, :] + along_y[above, t, span, :]
        div_z = seconds[2][t] + half * (lower - upper)
        bulk = lame[t] + shear[t]
        for c, div in enumerate((div_x, div_y, div_z)):
            out[c].append(shear[t] * laps[c][t] + bulk * div)
    return out


def exact_dot(value, pick):
    high = value.astype(jnp.bfloat16)
    rest = value - high.astype(jnp.float32)
    middle = rest.astype(jnp.bfloat16)
    low = (rest - middle.astype(jnp.float32)).astype(jnp.bfloat16)
    dot = lambda part: jnp.dot(part, pick, preferred_element_type=jnp.float32)
    return dot(high) + (dot(middle) + dot(low))


def prolonged(tiles):
    odd_x = [0.5 * (tile + turned(tile, -1, 0)) for tile in tiles]
    next_y = across(tiles, 1, 2)
    next_odd = across(odd_x, 1, 2)
    return (
        tiles,
        [0.5 * (a + b) for a, b in zip(tiles, next_y)],
        odd_x,
        [0.5 * (a + b) for a, b in zip(odd_x, next_odd)],
    )


def restricted(parts):
    even_even, even_odd, odd_even, odd_odd = parts
    even = [0.5 * a + 0.25 * (b + turned(b, 1, 0)) for a, b in zip(even_even, odd_even)]
    odd = [0.5 * a + 0.25 * (b + turned(b, 1, 0)) for a, b in zip(even_odd, odd_odd)]
    return [0.5 * a + 0.25 * (b + c) for a, b, c in zip(even, odd, across(odd, -1, 2))]


def largest(values):
    total = values[0]
    for value in values[1:]:
        total = jnp.maximum(total, value)
    return jnp.max(total)


def smallest(values):
    total = values[0]
    for value in values[1:]:
        total = jnp.minimum(total, value)
    return jnp.min(total)


def pick(lines, marks, wanted):
    begin = smallest([jnp.where(m == wanted, a, -FAR) for m, (a, _) in zip(marks, lines)])
    slope = largest([jnp.where(m == wanted, b, FAR) for m, (_, b) in zip(marks, lines)])
    return begin, slope


def top_line(lines, step):
    values = [a + step * b for a, b in lines]
    top = largest(values)
    return pick(lines, values, top)


def next_line(lines, begin, slope, limit):
    crossings = []
    for a, b in lines:
        steeper = b - slope
        crossings.append(jnp.where(steeper > 0.0, (begin - a) / steeper, -FAR))
    nearest = smallest(crossings)
    found = nearest <= limit
    new_begin, new_slope = pick(lines, crossings, nearest)
    return jnp.where(found, new_begin, begin), jnp.where(found, new_slope, slope), found


def envelopes(first, last, peak):
    lane = iota((1, LANES), 1)
    bound = 0.3 / jnp.full((8, LANES), peak, jnp.float32)
    bound = bound * bound * 1.00001
    limit = jnp.max(bound)
    first_begin, first_slope = top_line(first, STEP_LOW)
    last_begin, last_slope = top_line(last, STEP_LOW)
    first_top = largest([a + bound * b for a, b in first])
    last_top = largest([a + bound * b for a, b in last])
    single = (jnp.max(first_begin + bound * first_slope) >= first_top) & (
        jnp.max(last_begin + bound * last_slope) >= last_top
    )
    message = jnp.where(
        lane < 32,
        first_begin,
        jnp.where(lane < 64, first_slope, jnp.where(lane < 96, last_begin, last_slope)),
    )

    def more(state):
        return (state[0] < SLOTS) & (state[1] > 0)

    def step(state):
        n, _, fa, fb, la, lb, message = state
        fa, fb, found_first = next_line(first, fa, fb, limit)
        la, lb, found_last = next_line(last, la, lb, limit)
        message = jnp.where(lane == n, fa, message)
        message = jnp.where(lane == n + 32, fb, message)
        message = jnp.where(lane == n + 64, la, message)
        message = jnp.where(lane == n + 96, lb, message)
        found = (found_first | found_last).astype(jnp.int32)
        return n + 1, found, fa, fb, la, lb, message

    left = jnp.where(single, 0, 1).astype(jnp.int32)
    start = (jnp.int32(1), left, first_begin, first_slope, last_begin, last_slope, message)
    _, left, _, _, _, _, message = lax.while_loop(more, step, start)
    return message, left.astype(jnp.float32)


def sealed(message, peak, flag):
    lane = iota((1, LANES), 1)
    return jnp.where(lane == PEAK_LANE, peak, jnp.where(lane == FLAG_LANE, flag, message))


def opened(received):
    first, last = [], []
    rows = received.shape[0]
    lane = iota((8, LANES), 1)
    peak, flag = [], []
    for r in range(0, rows, 8):
        begin = received[r : r + 8, :]
        slope = turned(begin, -32, 1)
        in_first = lane < SLOTS
        in_last = (lane >= 64) & (lane < 64 + SLOTS)
        first.append((jnp.where(in_first, begin, FAR), jnp.where(in_first, slope, 0.0)))
        last.append((jnp.where(in_last, begin, FAR), jnp.where(in_last, slope, 0.0)))
        peak.append(jnp.where(lane == PEAK_LANE, begin, 0.0))
        flag.append(jnp.where(lane == FLAG_LANE, begin, 0.0))
    return first, last, largest(peak), largest(flag)


class Tiles:
    def __init__(self, own, rim):
        self.own, self.rim = own, rim
        self.count = own.shape[-3] + 1

    def __getitem__(self, index):
        *plane, tile, rows, lanes = index
        if tile < self.count - 1:
            return self.own[(*plane, tile, rows, lanes)]
        return self.rim[(*plane, rows, lanes)]


def home(key, fine, rest, coarse, coarse_rest):
    if key in DEEP_REST:
        return rest.at[DEEP_REST.index(key)]
    if key in COARSE_REST:
        return coarse_rest.at[COARSE_REST.index(key)]
    return (fine if key[0] == "fn" else coarse).at[key[1]]


def received(axis, pieces, span):
    return pair(axis, pieces[1][span, :], pieces[0][span, :])


def place_kernel(*refs):
    named = dict(zip(NAMES, refs[:10]))
    rims, targets = refs[10:12], refs[12:16]
    for key, low, _, tile, _, row, own in ENTRIES:
        target = home(key, *targets)
        rows = TILE_ROWS[tile][1]
        total = target.shape[1]
        for t in range(own):
            if low > 2:
                target[t, 0:rows, :] = jnp.zeros((rows, LANES), jnp.float32)
                target[t, 2 * rows : total, :] = jnp.zeros((total - 2 * rows, LANES), jnp.float32)
            target[t, rows : 2 * rows, :] = own_tile(named, key, t)
            below, beyond = received("gx", rims, slice(row + t * low, row + t * low + low))
            target[t, rows - low : rows, :] = below
            target[t, 2 * rows : 2 * rows + low, :] = beyond
    coarse = targets[2]
    coarse[:, 8] = jnp.zeros(coarse.shape[:1] + coarse.shape[2:], jnp.float32)


def main_kernel(*refs):
    named = dict(zip(("fd", "fs", "fl", "cd", "cs", "cl"), refs[:6]))
    sides, corners = refs[6:8], refs[8:10]
    split_pick, weave_pick = refs[10:12]
    owns = refs[12:16]
    fine_rate, coarse_rate, plane_out, iterate_out, lines_out, message_out = refs[16:22]
    rims = refs[22:26]
    fine_x, fine_y, coarse_x, coarse_y = refs[26:30]
    mixed, planes, parted, woven, ends = refs[30:35]
    packed = dict(zip("ABC", zip(refs[35:38], refs[38:41])))
    fine, rest, coarse, coarse_rest = (Tiles(own, rim) for own, rim in zip(owns, rims))
    slot = {key: i for i, key in enumerate(DEEP_REST)}
    coarse_slot = {key: i for i, key in enumerate(COARSE_REST)}

    for tile, (base, rows) in TILE_ROWS.items():
        rim = TILE_RIM[tile]
        own = received("gy", sides, slice(base, base + rows))
        for side in range(2):
            target = packed[tile][side]
            target[...] = jnp.zeros(target.shape, jnp.float32)
            target[rows : 2 * rows, :] = own[side]
            row = CORNERS[tile, side]
            low, high = received("gx", corners, slice(row, row + rim))
            target[rows - rim : rows, :] = low
            target[2 * rows : 2 * rows + rim, :] = high
    for key, low, high, tile, at, _, _ in ENTRIES:
        low_side, high_side = packed[tile][0][...], packed[tile][1][...]
        lane = iota(low_side.shape, 1)
        home(key, *rims)[...] = jnp.where(
            lane < high,
            turned(high_side, -at, 1),
            jnp.where(lane >= LANES - low, turned(low_side, -(at + low), 1), 0.0),
        )
    rims[2][:, 8] = jnp.zeros(rims[2].shape[:1] + rims[2].shape[2:], jnp.float32)

    for k in range(5):
        slopes(fine, fine_x, fine_y, k, 16, 16, 2, 1.0)
    for k in (5, 6, 7):
        slopes(fine, fine_x, fine_y, k, 8, 32, 3, 1.0)

    def fine_plane(k):
        above = 1 if k == 0 else k - 1
        own = [slice(t * LANES, (t + 1) * LANES) for t in range(2)]
        shear = [named["fs"][k, :, lanes] for lanes in own]
        lame = [named["fl"][k, :, lanes] for lanes in own]
        accel = acceleration(fine, fine_x, fine_y, mixed, (above, k, k + 1), 16, 16, 2, 1.0, shear, lame)
        for c in range(3):
            for t in range(2):
                fine_rate[c, k, :, own[t]] = accel[c][t] / named["fd"][k, :, own[t]]

    for k in range(6):
        fine_plane(k)

    window = slice(8, 40)
    shear = [rest[slot[("fs", (6,))], t, window, :] for t in range(3)]
    lame = [rest[slot[("fl", (6,))], t, window, :] for t in range(3)]
    accel = acceleration(fine, fine_x, fine_y, mixed, (5, 6, 7), 8, 32, 3, 1.0, shear, lame)
    for t in range(3):
        density = rest[slot[("fd", (6,))], t, window, :]
        filled = density > 0.0
        density = jnp.where(filled, density, 1.0)
        for c in range(3):
            rate = jnp.where(filled, accel[c][t] / density, 0.0)
            planes[3 + c, t, :, :] = rate
            planes[c, t, :, :] = 2.0 * fine[c, 6, t, window, :] - rest[c, t, window, :]
            if t < 2:
                fine_rate[c, 6, :, t * LANES : (t + 1) * LANES] = rate[8:24, :]
        fine_shear = rest[slot[("fs", (7,))], t, window, :]
        planes[6, t, :, :] = fine_shear
        planes[7, t, :, :] = rest[slot[("fl", (7,))], t, window, :] + 2.0 * fine_shear

    stacked = jnp.concatenate(
        [
            jnp.concatenate([planes[p, t, pl.ds(odd, 16, stride=2), :] for t in range(3)], axis=1)
            for p in range(8)
            for odd in range(2)
        ],
        axis=0,
    )
    parted[...] = exact_dot(stacked, split_pick[...])

    def four(p):
        return tuple(
            [
                parted[p * 32 + odd_x * 16 : p * 32 + odd_x * 16 + 16, (odd_y * 2 + t) * LANES : (odd_y * 2 + t + 1) * LANES]
                for t in range(2)
            ]
            for odd_x in range(2)
            for odd_y in range(2)
        )

    for k in range(8):
        slopes(coarse, coarse_x, coarse_y, k, 4, 16, 2, 2.0)
    coarse_x[8] = jnp.zeros(coarse_x.shape[1:], jnp.float32)
    coarse_y[8] = jnp.zeros(coarse_y.shape[1:], jnp.float32)

    def coarse_plane(k):
        shear = [named["cs"][k]]
        lame = [named["cl"][k]]
        accel = acceleration(coarse, coarse_x, coarse_y, mixed, (k - 1, k, k + 1), 8, 8, 1, 2.0, shear, lame)
        for c in range(3):
            coarse_rate[c, k - 1] = accel[c][0] / named["cd"][k]

    for k in range(2, 8):
        coarse_plane(k)
    band = slice(4, 20)

    def coarse_pair(name, k):
        return [coarse_rest[coarse_slot[(name, (k,))], t, band, :] for t in range(2)]

    shear, lame, density = coarse_pair("cs", 1), coarse_pair("cl", 1), coarse_pair("cd", 1)
    accel = acceleration(coarse, coarse_x, coarse_y, mixed, (0, 1, 2), 4, 16, 2, 2.0, shear, lame)
    below_rate = [[], [], []]
    for c in range(3):
        for t in range(2):
            filled = density[t] > 0.0
            rate = jnp.where(filled, accel[c][t] / jnp.where(filled, density[t], 1.0), 0.0)
            below_rate[c].append(rate)
        coarse_rate[c, 0] = below_rate[c][0][4:12, :]

    shear, lame = coarse_pair("cs", 0), coarse_pair("cl", 0)
    row = iota((16, LANES), 0) + (lax.axis_index("gx") * 8 - 4)
    lane = iota((16, LANES), 1) + lax.axis_index("gy") * LANES
    column = [lane, jnp.where(iota((16, LANES), 1) < 64, lane + LANES, lane - LANES)]
    extent = (lax.axis_size("gx") * 8, lax.axis_size("gy") * LANES)
    fine_moduli = (four(6), four(6), four(7))
    coarse_moduli = (shear, shear, [l + 2.0 * s for l, s in zip(lame, shear)])
    for c in range(3):
        moduli = fine_moduli[c]
        half = [0.5 * m for m in coarse_moduli[c]]
        spread = restricted(moduli)
        inverse = []
        for t in range(2):
            diagonal = half[t] + 0.5625 * spread[t]
            x, y = row, column[t]
            inside = (x >= 0) & (x < extent[0]) & (y >= 0) & (y < extent[1]) & (diagonal > 0.0)
            inverse.append(jnp.where(inside, 1.0 / jnp.where(inside, diagonal, 1.0), 0.0))
        for part in range(2):
            if part == 0:
                now = [coarse[c, 0, t, band, :] for t in range(2)]
                before = [coarse_rest[coarse_slot[("cb", (c, 0))], t, band, :] for t in range(2)]
                iterate = [2.0 * a - b for a, b in zip(now, before)]
                now = [coarse[c, 1, t, band, :] for t in range(2)]
                before = [coarse_rest[coarse_slot[("cb", (c, 1))], t, band, :] for t in range(2)]
                below = [2.0 * a - b for a, b in zip(now, before)]
            else:
                iterate = [jnp.zeros((16, LANES), jnp.float32)] * 2
                below = below_rate[c]
            above = four(3 * part + c)
            fixed = restricted([[m * a for m, a in zip(ms, as_)] for ms, as_ in zip(moduli, above)])
            fixed = [h * b + f for h, b, f in zip(half, below, fixed)]

            def mismatch_of(iterate):
                stress = [[m * a for m, a in zip(ms, ps)] for ms, ps in zip(moduli, prolonged(iterate))]
                return [h * i + (s - f) for h, i, s, f in zip(half, iterate, restricted(stress), fixed)]

            mismatch = mismatch_of(iterate)
            ends[part, c] = mismatch[0]
            for _ in range(ITERS):
                iterate = [i - m * v for i, m, v in zip(iterate, mismatch, inverse)]
                mismatch = mismatch_of(iterate)
            ends[2 + part, c] = mismatch[0]
            ends[4 + part, c] = iterate[0]
            even_even, even_odd, odd_even, odd_odd = prolonged(iterate)
            at = (part * 3 + c) * 32
            woven[at : at + 16, 0:LANES] = even_even[0]
            woven[at : at + 16, LANES : 2 * LANES] = even_odd[0]
            woven[at + 16 : at + 32, 0:LANES] = odd_even[0]
            woven[at + 16 : at + 32, LANES : 2 * LANES] = odd_odd[0]

    woven[...] = exact_dot(woven[...], weave_pick[...])
    for part in range(2):
        for c in range(3):
            iterate_out[part, c] = ends[4 + part, c, 4:12, :]
            for odd in range(2):
                at = (part * 3 + c) * 32 + odd * 16 + 4
                for t in range(2):
                    plane_out[part, c, t, pl.ds(odd, 8, stride=2), :] = woven[
                        at : at + 8, t * LANES : (t + 1) * LANES
                    ]

    lines = []
    for which in range(2):
        found = []
        for c in range(3):
            begin, slope = ends[2 * which, c, 4:12, :], ends[2 * which + 1, c, 4:12, :]
            lines_out[2 * which, c] = begin
            lines_out[2 * which + 1, c] = slope
            found += [(begin, slope), (-begin, -slope)]
        lines.append(found)
    ratio = (named["fl"][...] + 2.0 * named["fs"][...]) / named["fd"][...]
    coarse_ratio = (named["cl"][...] + 2.0 * named["cs"][...]) / named["cd"][...]
    fine_peak = jnp.sqrt(jnp.full((8, LANES), jnp.max(ratio), jnp.float32))
    coarse_peak = jnp.sqrt(jnp.full((8, LANES), jnp.max(coarse_ratio), jnp.float32))
    peak = jnp.max(jnp.maximum(fine_peak, 0.5 * coarse_peak))
    message, flag = envelopes(lines[0], lines[1], peak)
    message_out[...] = jnp.broadcast_to(sealed(message, peak, flag), message_out.shape)


def merge_kernel(received, message_out):
    first, last, peak, flag = opened(received)
    message, full = envelopes(first, last, peak)
    message_out[...] = jnp.broadcast_to(sealed(message, peak, jnp.maximum(flag, full)), message_out.shape)


def final_kernel(
    received, fn, fb, cn, cb, fine_rate, coarse_rate, plane, iterate, fine_out, coarse_out, ratio_out, square_out, flag_out
):
    first, last, peak, flag = opened(received)
    step = 0.3 / jnp.full((8, LANES), peak, jnp.float32)
    square = step * step
    first_max = largest([a + square * b for a, b in first])
    last_max = largest([a + square * b for a, b in last])
    ratio = last_max / (jnp.full((8, LANES), first_max, jnp.float32) + 1e-06)
    ratio_out[0] = jnp.max(ratio)
    square_out[0] = jnp.max(square)
    flag_out[0] = jnp.where((flag > 0.0) | (jnp.max(square) < STEP_LOW), 1, 0)
    square = square[0:1, 0:1]
    for c in range(3):
        fine_out[c, 0:7] = 2.0 * fn[c, 0:7] - fb[c, 0:7] + square * fine_rate[c]
        coarse_out[c, 1:8] = 2.0 * cn[c, 1:8] - cb[c, 1:8] + square * coarse_rate[c]
        coarse_out[c, 0] = iterate[0, c] + square * iterate[1, c]
        for t in range(2):
            fine_out[c, 7, :, t * LANES : (t + 1) * LANES] = plane[0, c, t] + square * plane[1, c, t]


def exchange(first, second, axis, count):
    near = [(i, i ^ 1) for i in range(count) if i ^ 1 < count]
    far = [(i, i + 1) for i in range(1, count - 1, 2)] + [(i + 1, i) for i in range(1, count - 1, 2)]
    return lax.ppermute(first, axis, near), lax.ppermute(second, axis, far)


def gather_groups(columns, rows):
    ring, plane = {}, {}
    for i in range(columns):
        for j in range(rows):
            chip_y, core, z, x = i // 2 % 4, i % 2, (i // 8, j % 4), j // 4
            ring.setdefault((x, chip_y), []).append(i * rows + j)
            plane.setdefault((z, core), []).append(i * rows + j)
    return list(ring.values()), list(plane.values())


def split_matrix():
    lane = np.arange(3 * LANES)
    fine_column = np.where(lane < 320, lane, lane - 384)[:, None]
    circle = np.arange(2 * LANES)
    coarse_column = np.where(circle < 192, circle, circle - 256)[None, :]
    return np.concatenate(
        [fine_column == 2 * coarse_column, fine_column == 2 * coarse_column + 1], axis=1
    ).astype(ml_dtypes.bfloat16)


def weave_matrix():
    lane = np.arange(2 * LANES)
    target = np.where(lane < LANES, 2 * lane, 2 * (lane - LANES) + 1)[:, None]
    return (target == lane[None, :]).astype(ml_dtypes.bfloat16)


def f32(*shape):
    return jax.ShapeDtypeStruct(shape, jnp.float32)


def vm(*shape):
    return pltpu.VMEM(shape, jnp.float32)


def make_shards(columns, rows):
    ring, plane_groups = gather_groups(columns, rows)
    axes = ("gx", "gy")

    def shards(*args):
        in_vmem = pl.BlockSpec(memory_space=pltpu.VMEM)
        in_smem = pl.BlockSpec(memory_space=pltpu.SMEM)
        in_hbm = pl.BlockSpec(memory_space=pltpu.HBM)

        def call(kernel, ins, outs, scratch=(), out_specs=None, cost=None, limit=16):
            return pl.pallas_call(
                kernel,
                out_shape=outs,
                in_specs=ins,
                out_specs=out_specs or ([in_vmem] * len(outs) if isinstance(outs, tuple) else in_vmem),
                scratch_shapes=list(scratch),
                compiler_params=pltpu.CompilerParams(vmem_limit_bytes=limit * 1024 * 1024),
                cost_estimate=cost,
            )

        fn, fb, _, _, _, cn, cb, _, _, _ = args
        first_side, second_side, first_rim, second_rim = call(
            pack,
            [in_hbm] * 10,
            (f32(PACKED_ROWS, LANES),) * 2 + (f32(RIM_ROWS, LANES),) * 2,
            [vm(PACKED_ROWS, LANES)] * 2
            + [vm(RIM_ROWS, LANES)] * 2
            + [vm(*a.shape) for a in args]
            + [pltpu.SemaphoreType.DMA((len(PACK_SOURCES),)), pltpu.SemaphoreType.DMA((4,))],
            out_specs=[in_hbm] * 4,
            limit=63,
        )(*args)
        sides = exchange(first_side, second_side, "gy", rows)
        rims = exchange(first_rim, second_rim, "gx", columns)
        first, second = call(
            pack_corners,
            [in_vmem] * 2,
            (f32(CORNER_ROWS, LANES),) * 2,
            cost=pl.CostEstimate(flops=10**12, bytes_accessed=10**9, transcendentals=0),
        )(*sides)
        corners = exchange(first, second, "gx", columns)
        ring_size, plane_size = len(ring[0]), len(plane_groups[0])
        own_shapes = ((3, 8, 2, 48, LANES), (8, 2, 48, LANES), (3, 9, 1, 24, LANES), (11, 1, 24, LANES))
        owns = call(place_kernel, [in_vmem] * 12, tuple(f32(*shape) for shape in own_shapes))(*args, *rims)
        outs = (
            f32(3, 7, 16, 256),
            f32(3, 7, 8, 128),
            f32(2, 3, 2, 16, 128),
            f32(2, 3, 8, 128),
            f32(4, 3, 8, 128),
            f32(ring_size, LANES),
        )
        scratch = [vm(*shape[:-3], *shape[-2:]) for shape in own_shapes] + [
            vm(8, 3, 48, LANES),
            vm(8, 3, 48, LANES),
            vm(9, 2, 24, LANES),
            vm(9, 2, 24, LANES),
            vm(3, 48, LANES),
            vm(8, 3, 32, LANES),
            vm(256, 512),
            vm(192, 256),
            vm(6, 3, 16, LANES),
        ]
        scratch += [vm(48, LANES), vm(48, LANES), vm(24, LANES)] * 2
        fine_rate, coarse_rate, plane, iterate, lines, message = call(main_kernel, [in_vmem] * 16, outs, scratch)(
            *args[2:5],
            *args[7:],
            *sides,
            *corners,
            jnp.asarray(split_matrix()),
            jnp.asarray(weave_matrix()),
            *owns,
        )
        received = lax.all_to_all(message, axes, 0, 0, tiled=True, axis_index_groups=ring)
        message = call(merge_kernel, [in_vmem], f32(plane_size, LANES))(received)
        received = lax.all_to_all(message, axes, 0, 0, tiled=True, axis_index_groups=plane_groups)
        fine_next, coarse_next, ratio, square, flag = call(
            final_kernel,
            [in_vmem] * 9,
            (f32(*fn.shape), f32(*cn.shape), f32(1), f32(1), jax.ShapeDtypeStruct((1,), jnp.int32)),
            out_specs=[in_vmem] * 2 + [in_smem] * 3,
        )(received, fn, fb, cn, cb, fine_rate, coarse_rate, plane, iterate)

        def plain():
            values = jnp.abs(lines[0::2] + square[0] * lines[1::2])
            tops = lax.pmax(jnp.max(values, axis=(1, 2, 3)), axes)
            return tops[1] / (tops[0] + 1e-06)

        reduction = lax.cond(flag[0] > 0, plain, lambda: ratio[0])
        return fine_next, coarse_next, reduction

    return shards


def solution(mesh):
    placed = (
        P(None, None, "gx", "gy"),
        P(None, None, "gx", "gy"),
        P(None, "gx", "gy"),
        P(None, "gx", "gy"),
        P(None, "gx", "gy"),
        P(None, None, "gx", "gy"),
        P(None, None, "gx", "gy"),
        P(None, "gx", "gy"),
        P(None, "gx", "gy"),
        P(None, "gx", "gy"),
    )
    return jax.shard_map(
        make_shards(mesh.shape["gx"], mesh.shape["gy"]),
        mesh=mesh,
        in_specs=placed,
        out_specs=(P(None, None, "gx", "gy"), P(None, None, "gx", "gy"), P()),
        check_vma=False,
    )
```

```python
import jax
import jax.numpy as jnp
import ml_dtypes
import numpy as np
from jax import lax
from jax.experimental import pallas as pl
from jax.experimental.pallas import tpu as pltpu
from jax.sharding import PartitionSpec as P

ITERS = 3
LANES = 128
NAMES = ("fn", "fb", "fd", "fs", "fl", "cn", "cb", "cd", "cs", "cl")

DEEP_NOW = [("fn", (c, k)) for c in range(3) for k in (5, 6, 7)]
THIN_NOW = [("fn", (c, k)) for c in range(3) for k in range(5)]
DEEP_REST = [("fb", (c, 6)) for c in range(3)] + [("fd", (6,)), ("fs", (6,)), ("fl", (6,)), ("fs", (7,)), ("fl", (7,))]
COARSE_NOW = [("cn", (c, k)) for c in range(3) for k in range(3)]
COARSE_REST = [("cb", (c, k)) for c in range(3) for k in range(2)] + [
    ("cd", (1,)),
    ("cs", (0,)),
    ("cl", (0,)),
    ("cs", (1,)),
    ("cl", (1,)),
]
COARSE_THIN = [("cn", (c, k)) for c in range(3) for k in range(3, 8)]

TILE_ROWS = {"A": (0, 16), "B": (16, 16), "C": (16, 8), "D": (24, 8)}
TILE_RIM = {"A": 9, "B": 7, "C": 5, "D": 5}
PACKED_ROWS = 32


def plan():
    entries, lane, row = [], {"A": 0, "B": 0, "C": 7 * len(DEEP_REST), "D": 7 * len(DEEP_REST)}, 0
    for tile, keys, low, high in (
        ("A", DEEP_NOW, 9, 8),
        ("A", THIN_NOW, 2, 2),
        ("B", DEEP_REST, 7, 6),
        ("C", COARSE_NOW, 5, 5),
        ("D", COARSE_REST, 4, 4),
        ("C", COARSE_THIN[:13], 2, 2),
        ("D", COARSE_THIN[13:], 2, 2),
    ):
        for key in keys:
            own = 1 if tile in "CD" else 2
            entries.append((key, low, high, tile, lane[tile], row, own))
            lane[tile] += low
            row += own * low
    corners, corner_row = {}, 0
    for tile in TILE_ROWS:
        for side in range(2):
            corners[tile, side] = corner_row
            corner_row += TILE_RIM[tile]
    return entries, corners, -(-row // 8) * 8, -(-corner_row // 8) * 8


ENTRIES, CORNERS, RIM_ROWS, CORNER_ROWS = plan()

PACK_SOURCES = (
    ("fn", ()),
    ("fb", (slice(None), slice(6, 7))),
    ("fd", (slice(6, 7),)),
    ("fs", (slice(6, 8),)),
    ("fl", (slice(6, 8),)),
    ("cn", ()),
    ("cb", (slice(None), slice(0, 2))),
    ("cd", (slice(1, 2),)),
    ("cs", (slice(0, 2),)),
    ("cl", (slice(0, 2),)),
)

SLOTS = 31
PEAK_LANE = 31
FLAG_LANE = 63
STEP_LOW = 0.02
FAR = -1.0e30


def iota(shape, dim):
    return lax.broadcasted_iota(jnp.int32, shape, dim)


def turned(value, steps, axis):
    size = value.shape[axis]
    steps = steps % size
    return value if steps == 0 else pltpu.roll(value, steps, axis)


def own_tile(refs, key, tile):
    name, index = key
    return refs[name][index + (slice(None), slice(tile * LANES, (tile + 1) * LANES))]


FIRST_PAIRS = {"columns": ("gy", 1), "rows": ("gx", 1), "corners": ("gx", 1)}


def pair(what, low, high):
    axis, begin = FIRST_PAIRS[what]
    upward = lax.axis_index(axis) % 2 == begin
    return jnp.where(upward, low, high), jnp.where(upward, high, low)


def pack(*refs):
    sources = dict(zip(NAMES, refs[:10]))
    targets, packs = refs[10:14], refs[14:18]
    column_outs, row_outs = packs[:2], packs[2:]
    named = dict(zip(NAMES, refs[18:28]))
    sems, out_sems = refs[28:30]
    sends = [pltpu.make_async_copy(source, target, out_sems.at[i]) for i, (source, target) in enumerate(zip(packs, targets))]
    copies = []
    for i, (name, part) in enumerate(PACK_SOURCES):
        source, target = sources[name], named[name]
        if part:
            source, target = source.at[part], target.at[part]
        copies.append(pltpu.make_async_copy(source, target, sems.at[i]))
    for copy in copies:
        copy.start()
    for copy in copies:
        copy.wait()
    for tile, (base, rows) in TILE_ROWS.items():
        lane = iota((rows, LANES), 1)
        low_sum = jnp.zeros((rows, LANES), jnp.float32)
        high_sum = low_sum
        for key, low, _, where, at, _, own in ENTRIES:
            if where != tile:
                continue
            inside = (lane >= at) & (lane < at + low)
            low_sum = jnp.where(inside, turned(own_tile(named, key, own - 1), at + low, 1), low_sum)
            high_sum = jnp.where(inside, turned(own_tile(named, key, 0), at, 1), high_sum)
        span = slice(base, base + rows)
        sums = pair("columns", low_sum, high_sum)
        for out, value in zip(column_outs, sums):
            out[span, :] = out[span, :] + value if tile in "CD" else value
    for send in sends[:2]:
        send.start()
    row_outs[0][RIM_ROWS - 8 :, :] = jnp.zeros((8, LANES), jnp.float32)
    row_outs[1][RIM_ROWS - 8 :, :] = jnp.zeros((8, LANES), jnp.float32)
    for (name, index), low, _, _, _, row, own in ENTRIES:
        ref = named[name]
        rows = ref.shape[-2]
        for tile in range(own):
            lanes = slice(tile * LANES, (tile + 1) * LANES)
            span = slice(row + tile * low, row + tile * low + low)
            row_outs[0][span, :], row_outs[1][span, :] = pair(
                "rows", ref[index + (slice(rows - low, rows), lanes)], ref[index + (slice(0, low), lanes)]
            )
    for send in sends[2:]:
        send.start()
    for send in sends:
        send.wait()


def pack_corners(first, second, first_out, second_out):
    first_out[CORNER_ROWS - 8 :, :] = jnp.zeros((8, LANES), jnp.float32)
    second_out[CORNER_ROWS - 8 :, :] = jnp.zeros((8, LANES), jnp.float32)
    for tile, (base, rows) in TILE_ROWS.items():
        rim = TILE_RIM[tile]
        end, begin = slice(base + rows - rim, base + rows), slice(base, base + rim)
        ends = pair("columns", second[end, :], first[end, :])
        begins = pair("columns", second[begin, :], first[begin, :])
        for side in range(2):
            row = CORNERS[tile, side]
            first_out[row : row + rim, :], second_out[row : row + rim, :] = pair("corners", ends[side], begins[side])


def across(tiles, steps, wanted):
    count = len(tiles)
    lane = iota(tiles[0].shape, 1)
    rolled = [turned(tile, -steps, 1) for tile in tiles]
    if steps > 0:
        return [jnp.where(lane < LANES - steps, rolled[t], rolled[(t + 1) % count]) for t in range(wanted)]
    return [jnp.where(lane >= -steps, rolled[t], rolled[(t - 1) % count]) for t in range(wanted)]


def first_of(down2, down1, up1, up2, spacing):
    return (8.0 * (up1 - down1) - (up2 - down2)) * (1.0 / (12.0 * spacing))


def second_of(down2, down1, here, up1, up2, spacing):
    return (16.0 * (up1 + down1) - (up2 + down2) - 30.0 * here) * (1.0 / (12.0 * spacing * spacing))


def across_all(tiles, wanted):
    return [across(tiles, steps, wanted) for steps in (-2, -1, 1, 2)]


def slopes(field, along_x, along_y, plane, start, rows, wanted, spacing):
    count = field.count
    for t in range(count):
        down2, down1, up1, up2 = (field[0, plane, t, pl.ds(start + d, rows), :] for d in (-2, -1, 1, 2))
        along_x[plane, t, start : start + rows, :] = first_of(down2, down1, up1, up2, spacing)
    span = slice(start - 4, start + rows + 4)
    shifted = across_all([field[1, plane, t, span, :] for t in range(count)], wanted)
    for t in range(wanted):
        along_y[plane, t, span, :] = first_of(*(s[t] for s in shifted), spacing)


def acceleration(field, along_x, along_y, mixed, planes, start, rows, wanted, spacing, shear, lame):
    above, plane, under = planes
    count = field.count
    half = 1.0 / (2.0 * spacing)
    square = 1.0 / (spacing * spacing)
    span = slice(start, start + rows)
    wide = slice(start - 4, start + rows + 4)
    for t in range(wanted):
        mixed[t, wide, :] = along_y[plane, t, wide, :] + half * (
            field[2, under, t, wide, :] - field[2, above, t, wide, :]
        )
    twist = [
        along_x[plane, t, span, :] + half * (field[2, under, t, span, :] - field[2, above, t, span, :])
        for t in range(count)
    ]
    twist = across_all(twist, wanted)
    laps, seconds = [], []
    for c in range(3):
        shifted = across_all([field[c, plane, t, span, :] for t in range(count)], wanted)
        lap, second = [], []
        for t in range(wanted):
            here = field[c, plane, t, span, :]
            down2, down1, up1, up2 = (field[c, plane, t, pl.ds(start + d, rows), :] for d in (-2, -1, 1, 2))
            in_x = second_of(down2, down1, here, up1, up2, spacing)
            in_y = second_of(shifted[0][t], shifted[1][t], here, shifted[2][t], shifted[3][t], spacing)
            in_z = square * (field[c, under, t, span, :] - 2.0 * here + field[c, above, t, span, :])
            lap.append(in_x + in_y + in_z)
            second.append((in_x, in_y, in_z)[c])
        laps.append(lap)
        seconds.append(second)
    out = [[], [], []]
    for t in range(wanted):
        ends = (mixed[t, pl.ds(start + d, rows), :] for d in (-2, -1, 1, 2))
        div_x = seconds[0][t] + first_of(*ends, spacing)
        div_y = seconds[1][t] + first_of(*(s[t] for s in twist), spacing)
        lower = along_x[under, t, span, :] + along_y[under, t, span, :]
        upper = along_x[above, t, span, :] + along_y[above, t, span, :]
        div_z = seconds[2][t] + half * (lower - upper)
        bulk = lame[t] + shear[t]
        for c, div in enumerate((div_x, div_y, div_z)):
            out[c].append(shear[t] * laps[c][t] + bulk * div)
    return out


def exact_dot(value, pick):
    high = value.astype(jnp.bfloat16)
    rest = value - high.astype(jnp.float32)
    middle = rest.astype(jnp.bfloat16)
    low = (rest - middle.astype(jnp.float32)).astype(jnp.bfloat16)
    dot = lambda part: jnp.dot(part, pick, preferred_element_type=jnp.float32)
    return dot(high) + (dot(middle) + dot(low))


def prolonged(tiles):
    odd_x = [0.5 * (tile + turned(tile, -1, 0)) for tile in tiles]
    next_y = across(tiles, 1, 2)
    next_odd = across(odd_x, 1, 2)
    return (
        tiles,
        [0.5 * (a + b) for a, b in zip(tiles, next_y)],
        odd_x,
        [0.5 * (a + b) for a, b in zip(odd_x, next_odd)],
    )


def restricted(parts):
    even_even, even_odd, odd_even, odd_odd = parts
    even = [0.5 * a + 0.25 * (b + turned(b, 1, 0)) for a, b in zip(even_even, odd_even)]
    odd = [0.5 * a + 0.25 * (b + turned(b, 1, 0)) for a, b in zip(even_odd, odd_odd)]
    return [0.5 * a + 0.25 * (b + c) for a, b, c in zip(even, odd, across(odd, -1, 2))]


def largest(values):
    total = values[0]
    for value in values[1:]:
        total = jnp.maximum(total, value)
    return jnp.max(total)


def smallest(values):
    total = values[0]
    for value in values[1:]:
        total = jnp.minimum(total, value)
    return jnp.min(total)


def pick(lines, marks, wanted):
    begin = smallest([jnp.where(m == wanted, a, -FAR) for m, (a, _) in zip(marks, lines)])
    slope = largest([jnp.where(m == wanted, b, FAR) for m, (_, b) in zip(marks, lines)])
    return begin, slope


def top_line(lines, step):
    values = [a + step * b for a, b in lines]
    top = largest(values)
    return pick(lines, values, top)


def next_line(lines, begin, slope, limit):
    crossings = []
    for a, b in lines:
        steeper = b - slope
        crossings.append(jnp.where(steeper > 0.0, (begin - a) / steeper, -FAR))
    nearest = smallest(crossings)
    found = nearest <= limit
    new_begin, new_slope = pick(lines, crossings, nearest)
    return jnp.where(found, new_begin, begin), jnp.where(found, new_slope, slope), found


def envelopes(first, last, peak):
    lane = iota((1, LANES), 1)
    bound = 0.3 / jnp.full((8, LANES), peak, jnp.float32)
    bound = bound * bound * 1.00001
    limit = jnp.max(bound)
    first_begin, first_slope = top_line(first, STEP_LOW)
    last_begin, last_slope = top_line(last, STEP_LOW)
    first_top = largest([a + bound * b for a, b in first])
    last_top = largest([a + bound * b for a, b in last])
    single = (jnp.max(first_begin + bound * first_slope) >= first_top) & (
        jnp.max(last_begin + bound * last_slope) >= last_top
    )
    message = jnp.where(
        lane < 32,
        first_begin,
        jnp.where(lane < 64, first_slope, jnp.where(lane < 96, last_begin, last_slope)),
    )

    def more(state):
        return (state[0] < SLOTS) & (state[1] > 0)

    def step(state):
        n, _, fa, fb, la, lb, message = state
        fa, fb, found_first = next_line(first, fa, fb, limit)
        la, lb, found_last = next_line(last, la, lb, limit)
        message = jnp.where(lane == n, fa, message)
        message = jnp.where(lane == n + 32, fb, message)
        message = jnp.where(lane == n + 64, la, message)
        message = jnp.where(lane == n + 96, lb, message)
        found = (found_first | found_last).astype(jnp.int32)
        return n + 1, found, fa, fb, la, lb, message

    left = jnp.where(single, 0, 1).astype(jnp.int32)
    start = (jnp.int32(1), left, first_begin, first_slope, last_begin, last_slope, message)
    _, left, _, _, _, _, message = lax.while_loop(more, step, start)
    return message, left.astype(jnp.float32)


def sealed(message, peak, flag):
    lane = iota((1, LANES), 1)
    return jnp.where(lane == PEAK_LANE, peak, jnp.where(lane == FLAG_LANE, flag, message))


def opened(received):
    first, last = [], []
    rows = received.shape[0]
    lane = iota((8, LANES), 1)
    peak, flag = [], []
    for r in range(0, rows, 8):
        begin = received[r : r + 8, :]
        slope = turned(begin, -32, 1)
        in_first = lane < SLOTS
        in_last = (lane >= 64) & (lane < 64 + SLOTS)
        first.append((jnp.where(in_first, begin, FAR), jnp.where(in_first, slope, 0.0)))
        last.append((jnp.where(in_last, begin, FAR), jnp.where(in_last, slope, 0.0)))
        peak.append(jnp.where(lane == PEAK_LANE, begin, 0.0))
        flag.append(jnp.where(lane == FLAG_LANE, begin, 0.0))
    return first, last, largest(peak), largest(flag)


class Tiles:
    def __init__(self, own, rim):
        self.own, self.rim = own, rim
        self.count = own.shape[-3] + 1

    def __getitem__(self, index):
        *plane, tile, rows, lanes = index
        if tile < self.count - 1:
            return self.own[(*plane, tile, rows, lanes)]
        return self.rim[(*plane, rows, lanes)]


def home(key, fine, rest, coarse, coarse_rest):
    if key in DEEP_REST:
        return rest.at[DEEP_REST.index(key)]
    if key in COARSE_REST:
        return coarse_rest.at[COARSE_REST.index(key)]
    return (fine if key[0] == "fn" else coarse).at[key[1]]


def received(what, pieces, span):
    return pair(what, pieces[1][span, :], pieces[0][span, :])


def place_kernel(*refs):
    named = dict(zip(NAMES, refs[:10]))
    rims, targets = refs[10:12], refs[12:16]
    for key, low, _, tile, _, row, own in ENTRIES:
        target = home(key, *targets)
        rows = TILE_ROWS[tile][1]
        total = target.shape[1]
        for t in range(own):
            if low > 2:
                target[t, 0:rows, :] = jnp.zeros((rows, LANES), jnp.float32)
                target[t, 2 * rows : total, :] = jnp.zeros((total - 2 * rows, LANES), jnp.float32)
            target[t, rows : 2 * rows, :] = own_tile(named, key, t)
            below, beyond = received("rows", rims, slice(row + t * low, row + t * low + low))
            target[t, rows - low : rows, :] = below
            target[t, 2 * rows : 2 * rows + low, :] = beyond
    coarse = targets[2]
    coarse[:, 8] = jnp.zeros(coarse.shape[:1] + coarse.shape[2:], jnp.float32)


def main_kernel(*refs):
    named = dict(zip(("fd", "fs", "fl", "cd", "cs", "cl"), refs[:6]))
    sides, corners = refs[6:8], refs[8:10]
    split_pick, weave_pick = refs[10:12]
    owns = refs[12:16]
    fine_rate, coarse_rate, plane_out, iterate_out, lines_out, message_out = refs[16:22]
    rims = refs[22:26]
    fine_x, fine_y, coarse_x, coarse_y = refs[26:30]
    mixed, planes, parted, woven, ends = refs[30:35]
    packed = dict(zip(TILE_ROWS, zip(refs[35:39], refs[39:43])))
    fine, rest, coarse, coarse_rest = (Tiles(own, rim) for own, rim in zip(owns, rims))
    slot = {key: i for i, key in enumerate(DEEP_REST)}
    coarse_slot = {key: i for i, key in enumerate(COARSE_REST)}

    for tile, (base, rows) in TILE_ROWS.items():
        rim = TILE_RIM[tile]
        own = received("columns", sides, slice(base, base + rows))
        for side in range(2):
            target = packed[tile][side]
            target[...] = jnp.zeros(target.shape, jnp.float32)
            target[rows : 2 * rows, :] = own[side]
            row = CORNERS[tile, side]
            low, high = received("corners", corners, slice(row, row + rim))
            target[rows - rim : rows, :] = low
            target[2 * rows : 2 * rows + rim, :] = high
    for key, low, high, tile, at, _, _ in ENTRIES:
        low_side, high_side = packed[tile][0][...], packed[tile][1][...]
        lane = iota(low_side.shape, 1)
        home(key, *rims)[...] = jnp.where(
            lane < high,
            turned(high_side, -at, 1),
            jnp.where(lane >= LANES - low, turned(low_side, -(at + low), 1), 0.0),
        )
    rims[2][:, 8] = jnp.zeros(rims[2].shape[:1] + rims[2].shape[2:], jnp.float32)

    for k in range(5):
        slopes(fine, fine_x, fine_y, k, 16, 16, 2, 1.0)
    for k in (5, 6, 7):
        slopes(fine, fine_x, fine_y, k, 8, 32, 3, 1.0)

    def fine_plane(k):
        above = 1 if k == 0 else k - 1
        own = [slice(t * LANES, (t + 1) * LANES) for t in range(2)]
        shear = [named["fs"][k, :, lanes] for lanes in own]
        lame = [named["fl"][k, :, lanes] for lanes in own]
        accel = acceleration(fine, fine_x, fine_y, mixed, (above, k, k + 1), 16, 16, 2, 1.0, shear, lame)
        for c in range(3):
            for t in range(2):
                fine_rate[c, k, :, own[t]] = accel[c][t] / named["fd"][k, :, own[t]]

    for k in range(6):
        fine_plane(k)

    window = slice(8, 40)
    shear = [rest[slot[("fs", (6,))], t, window, :] for t in range(3)]
    lame = [rest[slot[("fl", (6,))], t, window, :] for t in range(3)]
    accel = acceleration(fine, fine_x, fine_y, mixed, (5, 6, 7), 8, 32, 3, 1.0, shear, lame)
    for t in range(3):
        density = rest[slot[("fd", (6,))], t, window, :]
        filled = density > 0.0
        density = jnp.where(filled, density, 1.0)
        for c in range(3):
            rate = jnp.where(filled, accel[c][t] / density, 0.0)
            planes[3 + c, t, :, :] = rate
            planes[c, t, :, :] = 2.0 * fine[c, 6, t, window, :] - rest[c, t, window, :]
            if t < 2:
                fine_rate[c, 6, :, t * LANES : (t + 1) * LANES] = rate[8:24, :]
        fine_shear = rest[slot[("fs", (7,))], t, window, :]
        planes[6, t, :, :] = fine_shear
        planes[7, t, :, :] = rest[slot[("fl", (7,))], t, window, :] + 2.0 * fine_shear

    stacked = jnp.concatenate(
        [
            jnp.concatenate([planes[p, t, pl.ds(odd, 16, stride=2), :] for t in range(3)], axis=1)
            for p in range(8)
            for odd in range(2)
        ],
        axis=0,
    )
    parted[...] = exact_dot(stacked, split_pick[...])

    def four(p):
        return tuple(
            [
                parted[p * 32 + odd_x * 16 : p * 32 + odd_x * 16 + 16, (odd_y * 2 + t) * LANES : (odd_y * 2 + t + 1) * LANES]
                for t in range(2)
            ]
            for odd_x in range(2)
            for odd_y in range(2)
        )

    for k in range(8):
        slopes(coarse, coarse_x, coarse_y, k, 4, 16, 2, 2.0)
    coarse_x[8] = jnp.zeros(coarse_x.shape[1:], jnp.float32)
    coarse_y[8] = jnp.zeros(coarse_y.shape[1:], jnp.float32)

    def coarse_plane(k):
        shear = [named["cs"][k]]
        lame = [named["cl"][k]]
        accel = acceleration(coarse, coarse_x, coarse_y, mixed, (k - 1, k, k + 1), 8, 8, 1, 2.0, shear, lame)
        for c in range(3):
            coarse_rate[c, k - 1] = accel[c][0] / named["cd"][k]

    for k in range(2, 8):
        coarse_plane(k)
    band = slice(4, 20)

    def coarse_pair(name, k):
        return [coarse_rest[coarse_slot[(name, (k,))], t, band, :] for t in range(2)]

    shear, lame, density = coarse_pair("cs", 1), coarse_pair("cl", 1), coarse_pair("cd", 1)
    accel = acceleration(coarse, coarse_x, coarse_y, mixed, (0, 1, 2), 4, 16, 2, 2.0, shear, lame)
    below_rate = [[], [], []]
    for c in range(3):
        for t in range(2):
            filled = density[t] > 0.0
            rate = jnp.where(filled, accel[c][t] / jnp.where(filled, density[t], 1.0), 0.0)
            below_rate[c].append(rate)
        coarse_rate[c, 0] = below_rate[c][0][4:12, :]

    shear, lame = coarse_pair("cs", 0), coarse_pair("cl", 0)
    row = iota((16, LANES), 0) + (lax.axis_index("gx") * 8 - 4)
    lane = iota((16, LANES), 1) + lax.axis_index("gy") * LANES
    column = [lane, jnp.where(iota((16, LANES), 1) < 64, lane + LANES, lane - LANES)]
    extent = (lax.axis_size("gx") * 8, lax.axis_size("gy") * LANES)
    fine_moduli = (four(6), four(6), four(7))
    coarse_moduli = (shear, shear, [l + 2.0 * s for l, s in zip(lame, shear)])
    for c in range(3):
        moduli = fine_moduli[c]
        half = [0.5 * m for m in coarse_moduli[c]]
        spread = restricted(moduli)
        inverse = []
        for t in range(2):
            diagonal = half[t] + 0.5625 * spread[t]
            x, y = row, column[t]
            inside = (x >= 0) & (x < extent[0]) & (y >= 0) & (y < extent[1]) & (diagonal > 0.0)
            inverse.append(jnp.where(inside, 1.0 / jnp.where(inside, diagonal, 1.0), 0.0))
        for part in range(2):
            if part == 0:
                now = [coarse[c, 0, t, band, :] for t in range(2)]
                before = [coarse_rest[coarse_slot[("cb", (c, 0))], t, band, :] for t in range(2)]
                iterate = [2.0 * a - b for a, b in zip(now, before)]
                now = [coarse[c, 1, t, band, :] for t in range(2)]
                before = [coarse_rest[coarse_slot[("cb", (c, 1))], t, band, :] for t in range(2)]
                below = [2.0 * a - b for a, b in zip(now, before)]
            else:
                iterate = [jnp.zeros((16, LANES), jnp.float32)] * 2
                below = below_rate[c]
            above = four(3 * part + c)
            fixed = restricted([[m * a for m, a in zip(ms, as_)] for ms, as_ in zip(moduli, above)])
            fixed = [h * b + f for h, b, f in zip(half, below, fixed)]

            def mismatch_of(iterate):
                stress = [[m * a for m, a in zip(ms, ps)] for ms, ps in zip(moduli, prolonged(iterate))]
                return [h * i + (s - f) for h, i, s, f in zip(half, iterate, restricted(stress), fixed)]

            mismatch = mismatch_of(iterate)
            ends[part, c] = mismatch[0]
            for _ in range(ITERS):
                iterate = [i - m * v for i, m, v in zip(iterate, mismatch, inverse)]
                mismatch = mismatch_of(iterate)
            ends[2 + part, c] = mismatch[0]
            ends[4 + part, c] = iterate[0]
            even_even, even_odd, odd_even, odd_odd = prolonged(iterate)
            at = (part * 3 + c) * 32
            woven[at : at + 16, 0:LANES] = even_even[0]
            woven[at : at + 16, LANES : 2 * LANES] = even_odd[0]
            woven[at + 16 : at + 32, 0:LANES] = odd_even[0]
            woven[at + 16 : at + 32, LANES : 2 * LANES] = odd_odd[0]

    woven[...] = exact_dot(woven[...], weave_pick[...])
    for part in range(2):
        for c in range(3):
            iterate_out[part, c] = ends[4 + part, c, 4:12, :]
            for odd in range(2):
                at = (part * 3 + c) * 32 + odd * 16 + 4
                for t in range(2):
                    plane_out[part, c, t, pl.ds(odd, 8, stride=2), :] = woven[
                        at : at + 8, t * LANES : (t + 1) * LANES
                    ]

    lines = []
    for which in range(2):
        found = []
        for c in range(3):
            begin, slope = ends[2 * which, c, 4:12, :], ends[2 * which + 1, c, 4:12, :]
            lines_out[2 * which, c] = begin
            lines_out[2 * which + 1, c] = slope
            found += [(begin, slope), (-begin, -slope)]
        lines.append(found)
    ratio = (named["fl"][...] + 2.0 * named["fs"][...]) / named["fd"][...]
    coarse_ratio = (named["cl"][...] + 2.0 * named["cs"][...]) / named["cd"][...]
    fine_peak = jnp.sqrt(jnp.full((8, LANES), jnp.max(ratio), jnp.float32))
    coarse_peak = jnp.sqrt(jnp.full((8, LANES), jnp.max(coarse_ratio), jnp.float32))
    peak = jnp.max(jnp.maximum(fine_peak, 0.5 * coarse_peak))
    message, flag = envelopes(lines[0], lines[1], peak)
    message_out[...] = jnp.broadcast_to(sealed(message, peak, flag), message_out.shape)


def merge_kernel(received, message_out):
    first, last, peak, flag = opened(received)
    message, full = envelopes(first, last, peak)
    message_out[...] = jnp.broadcast_to(sealed(message, peak, jnp.maximum(flag, full)), message_out.shape)


def final_kernel(
    received, fn, fb, cn, cb, fine_rate, coarse_rate, plane, iterate, fine_out, coarse_out, ratio_out, square_out, flag_out
):
    first, last, peak, flag = opened(received)
    step = 0.3 / jnp.full((8, LANES), peak, jnp.float32)
    square = step * step
    first_max = largest([a + square * b for a, b in first])
    last_max = largest([a + square * b for a, b in last])
    ratio = last_max / (jnp.full((8, LANES), first_max, jnp.float32) + 1e-06)
    ratio_out[0] = jnp.max(ratio)
    square_out[0] = jnp.max(square)
    flag_out[0] = jnp.where((flag > 0.0) | (jnp.max(square) < STEP_LOW), 1, 0)
    square = square[0:1, 0:1]
    for c in range(3):
        fine_out[c, 0:7] = 2.0 * fn[c, 0:7] - fb[c, 0:7] + square * fine_rate[c]
        coarse_out[c, 1:8] = 2.0 * cn[c, 1:8] - cb[c, 1:8] + square * coarse_rate[c]
        coarse_out[c, 0] = iterate[0, c] + square * iterate[1, c]
        for t in range(2):
            fine_out[c, 7, :, t * LANES : (t + 1) * LANES] = plane[0, c, t] + square * plane[1, c, t]


def exchange(first, second, what, count):
    axis, begin = FIRST_PAIRS[what]

    def swap(value, parity):
        ups = [(i, i + 1) for i in range(parity, count - 1, 2)]
        return lax.ppermute(value, axis, ups + [(j, i) for i, j in ups])

    return swap(first, begin), swap(second, 1 - begin)


def gather_groups(columns, rows):
    ring, plane = {}, {}
    for i in range(columns):
        for j in range(rows):
            chip_y, core, z, x = i // 2 % 4, i % 2, (i // 8, j % 4), j // 4
            ring.setdefault((x, chip_y), []).append(i * rows + j)
            plane.setdefault((z, core), []).append(i * rows + j)
    return list(ring.values()), list(plane.values())


def split_matrix():
    lane = np.arange(3 * LANES)
    fine_column = np.where(lane < 320, lane, lane - 384)[:, None]
    circle = np.arange(2 * LANES)
    coarse_column = np.where(circle < 192, circle, circle - 256)[None, :]
    return np.concatenate(
        [fine_column == 2 * coarse_column, fine_column == 2 * coarse_column + 1], axis=1
    ).astype(ml_dtypes.bfloat16)


def weave_matrix():
    lane = np.arange(2 * LANES)
    target = np.where(lane < LANES, 2 * lane, 2 * (lane - LANES) + 1)[:, None]
    return (target == lane[None, :]).astype(ml_dtypes.bfloat16)


def f32(*shape):
    return jax.ShapeDtypeStruct(shape, jnp.float32)


def vm(*shape):
    return pltpu.VMEM(shape, jnp.float32)


def make_shards(columns, rows):
    ring, plane_groups = gather_groups(columns, rows)
    axes = ("gx", "gy")

    def shards(*args):
        in_vmem = pl.BlockSpec(memory_space=pltpu.VMEM)
        in_smem = pl.BlockSpec(memory_space=pltpu.SMEM)
        in_hbm = pl.BlockSpec(memory_space=pltpu.HBM)

        def call(kernel, ins, outs, scratch=(), out_specs=None, cost=None, limit=16):
            return pl.pallas_call(
                kernel,
                out_shape=outs,
                in_specs=ins,
                out_specs=out_specs or ([in_vmem] * len(outs) if isinstance(outs, tuple) else in_vmem),
                scratch_shapes=list(scratch),
                compiler_params=pltpu.CompilerParams(vmem_limit_bytes=limit * 1024 * 1024),
                cost_estimate=cost,
            )

        fn, fb, _, _, _, cn, cb, _, _, _ = args
        first_side, second_side, first_rim, second_rim = call(
            pack,
            [in_hbm] * 10,
            (f32(PACKED_ROWS, LANES),) * 2 + (f32(RIM_ROWS, LANES),) * 2,
            [vm(PACKED_ROWS, LANES)] * 2
            + [vm(RIM_ROWS, LANES)] * 2
            + [vm(*a.shape) for a in args]
            + [pltpu.SemaphoreType.DMA((len(PACK_SOURCES),)), pltpu.SemaphoreType.DMA((4,))],
            out_specs=[in_hbm] * 4,
            limit=63,
        )(*args)
        sides = exchange(first_side, second_side, "columns", rows)
        rims = exchange(first_rim, second_rim, "rows", columns)
        first, second = call(
            pack_corners,
            [in_vmem] * 2,
            (f32(CORNER_ROWS, LANES),) * 2,
            cost=pl.CostEstimate(flops=10**12, bytes_accessed=10**9, transcendentals=0),
        )(*sides)
        corners = exchange(first, second, "corners", columns)
        ring_size, plane_size = len(ring[0]), len(plane_groups[0])
        own_shapes = ((3, 8, 2, 48, LANES), (8, 2, 48, LANES), (3, 9, 1, 24, LANES), (11, 1, 24, LANES))
        owns = call(place_kernel, [in_vmem] * 12, tuple(f32(*shape) for shape in own_shapes))(*args, *rims)
        outs = (
            f32(3, 7, 16, 256),
            f32(3, 7, 8, 128),
            f32(2, 3, 2, 16, 128),
            f32(2, 3, 8, 128),
            f32(4, 3, 8, 128),
            f32(ring_size, LANES),
        )
        scratch = [vm(*shape[:-3], *shape[-2:]) for shape in own_shapes] + [
            vm(8, 3, 48, LANES),
            vm(8, 3, 48, LANES),
            vm(9, 2, 24, LANES),
            vm(9, 2, 24, LANES),
            vm(3, 48, LANES),
            vm(8, 3, 32, LANES),
            vm(256, 512),
            vm(192, 256),
            vm(6, 3, 16, LANES),
        ]
        scratch += [vm(48, LANES), vm(48, LANES), vm(24, LANES), vm(24, LANES)] * 2
        fine_rate, coarse_rate, plane, iterate, lines, message = call(main_kernel, [in_vmem] * 16, outs, scratch)(
            *args[2:5],
            *args[7:],
            *sides,
            *corners,
            jnp.asarray(split_matrix()),
            jnp.asarray(weave_matrix()),
            *owns,
        )
        received = lax.all_to_all(message, axes, 0, 0, tiled=True, axis_index_groups=ring)
        message = call(merge_kernel, [in_vmem], f32(plane_size, LANES))(received)
        received = lax.all_to_all(message, axes, 0, 0, tiled=True, axis_index_groups=plane_groups)
        fine_next, coarse_next, ratio, square, flag = call(
            final_kernel,
            [in_vmem] * 9,
            (f32(*fn.shape), f32(*cn.shape), f32(1), f32(1), jax.ShapeDtypeStruct((1,), jnp.int32)),
            out_specs=[in_vmem] * 2 + [in_smem] * 3,
        )(received, fn, fb, cn, cb, fine_rate, coarse_rate, plane, iterate)

        def plain():
            values = jnp.abs(lines[0::2] + square[0] * lines[1::2])
            tops = lax.pmax(jnp.max(values, axis=(1, 2, 3)), axes)
            return tops[1] / (tops[0] + 1e-06)

        reduction = lax.cond(flag[0] > 0, plain, lambda: ratio[0])
        return fine_next, coarse_next, reduction

    return shards


def solution(mesh):
    placed = (
        P(None, None, "gx", "gy"),
        P(None, None, "gx", "gy"),
        P(None, "gx", "gy"),
        P(None, "gx", "gy"),
        P(None, "gx", "gy"),
        P(None, None, "gx", "gy"),
        P(None, None, "gx", "gy"),
        P(None, "gx", "gy"),
        P(None, "gx", "gy"),
        P(None, "gx", "gy"),
    )
    return jax.shard_map(
        make_shards(mesh.shape["gx"], mesh.shape["gy"]),
        mesh=mesh,
        in_specs=placed,
        out_specs=(P(None, None, "gx", "gy"), P(None, None, "gx", "gy"), P()),
        check_vma=False,
    )
```

```python
import jax
import jax.numpy as jnp
import ml_dtypes
import numpy as np
from jax import lax
from jax.experimental import pallas as pl
from jax.experimental.pallas import tpu as pltpu
from jax.sharding import PartitionSpec as P

ITERS = 3
LANES = 128
NAMES = ("fn", "fb", "fd", "fs", "fl", "cn", "cb", "cd", "cs", "cl")

DEEP_NOW = [("fn", (c, k)) for c in range(3) for k in (5, 6, 7)]
THIN_NOW = [("fn", (c, k)) for c in range(3) for k in range(5)]
DEEP_REST = [("fb", (c, 6)) for c in range(3)] + [("fd", (6,)), ("fs", (6,)), ("fl", (6,)), ("fs", (7,)), ("fl", (7,))]
COARSE_NOW = [("cn", (c, k)) for c in range(3) for k in range(3)]
COARSE_REST = [("cb", (c, k)) for c in range(3) for k in range(2)] + [
    ("cd", (1,)),
    ("cs", (0,)),
    ("cl", (0,)),
    ("cs", (1,)),
    ("cl", (1,)),
]
COARSE_THIN = [("cn", (c, k)) for c in range(3) for k in range(3, 8)]

TILE_ROWS = {"A": (0, 16), "B": (16, 16), "C": (16, 8), "D": (24, 8)}
TILE_RIM = {"A": 9, "B": 7, "C": 5, "D": 5}
PACKED_ROWS = 32


def plan():
    entries, lane, row = [], {"A": 0, "B": 0, "C": 7 * len(DEEP_REST), "D": 7 * len(DEEP_REST)}, 0
    for tile, keys, low, high in (
        ("A", DEEP_NOW, 9, 8),
        ("A", THIN_NOW, 2, 2),
        ("B", DEEP_REST, 7, 6),
        ("C", COARSE_NOW, 5, 5),
        ("D", COARSE_REST, 4, 4),
        ("C", COARSE_THIN[:13], 2, 2),
        ("D", COARSE_THIN[13:], 2, 2),
    ):
        for key in keys:
            own = 1 if tile in "CD" else 2
            entries.append((key, low, high, tile, lane[tile], row, own))
            lane[tile] += low
            row += own * low
    corners, corner_row = {}, 0
    for tile in TILE_ROWS:
        for side in range(2):
            corners[tile, side] = corner_row
            corner_row += TILE_RIM[tile]
    return entries, corners, -(-row // 8) * 8, -(-corner_row // 8) * 8


ENTRIES, CORNERS, RIM_ROWS, CORNER_ROWS = plan()

PACK_SOURCES = (
    ("fn", ()),
    ("fb", (slice(None), slice(6, 7))),
    ("fd", (slice(6, 7),)),
    ("fs", (slice(6, 8),)),
    ("fl", (slice(6, 8),)),
    ("cn", ()),
    ("cb", (slice(None), slice(0, 2))),
    ("cd", (slice(1, 2),)),
    ("cs", (slice(0, 2),)),
    ("cl", (slice(0, 2),)),
)

SLOTS = 31
PEAK_LANE = 31
FLAG_LANE = 63
STEP_LOW = 0.02
FAR = -1.0e30


def iota(shape, dim):
    return lax.broadcasted_iota(jnp.int32, shape, dim)


def turned(value, steps, axis):
    size = value.shape[axis]
    steps = steps % size
    return value if steps == 0 else pltpu.roll(value, steps, axis)


def own_tile(refs, key, tile):
    name, index = key
    return refs[name][index + (slice(None), slice(tile * LANES, (tile + 1) * LANES))]


FIRST_PAIRS = {"columns": ("gy", 1), "rows": ("gx", 1), "corners": ("gx", 1)}
TURN = 16


def begins(what, row):
    begin = FIRST_PAIRS[what][1]
    return jnp.where(row < TURN, begin, 1 - begin) if what == "columns" else begin


def pair(what, low, high):
    upward = lax.axis_index(FIRST_PAIRS[what][0]) % 2 == begins(what, lax.axis_index("gx"))
    return jnp.where(upward, low, high), jnp.where(upward, high, low)


def pack(*refs):
    sources = dict(zip(NAMES, refs[:10]))
    column_outs, row_outs = refs[10:12], refs[12:14]
    named = dict(zip(NAMES, refs[14:24]))
    sems = refs[24]
    copies = []
    for i, (name, part) in enumerate(PACK_SOURCES):
        source, target = sources[name], named[name]
        if part:
            source, target = source.at[part], target.at[part]
        copies.append(pltpu.make_async_copy(source, target, sems.at[i]))
    for copy in copies:
        copy.start()
    for copy in copies:
        copy.wait()
    for tile, (base, rows) in TILE_ROWS.items():
        lane = iota((rows, LANES), 1)
        low_sum = jnp.zeros((rows, LANES), jnp.float32)
        high_sum = low_sum
        for key, low, _, where, at, _, own in ENTRIES:
            if where != tile:
                continue
            inside = (lane >= at) & (lane < at + low)
            low_sum = jnp.where(inside, turned(own_tile(named, key, own - 1), at + low, 1), low_sum)
            high_sum = jnp.where(inside, turned(own_tile(named, key, 0), at, 1), high_sum)
        span = slice(base, base + rows)
        sums = pair("columns", low_sum, high_sum)
        for out, value in zip(column_outs, sums):
            out[span, :] = out[span, :] + value if tile in "CD" else value
    row_outs[0][RIM_ROWS - 8 :, :] = jnp.zeros((8, LANES), jnp.float32)
    row_outs[1][RIM_ROWS - 8 :, :] = jnp.zeros((8, LANES), jnp.float32)
    for (name, index), low, _, _, _, row, own in ENTRIES:
        ref = named[name]
        rows = ref.shape[-2]
        for tile in range(own):
            lanes = slice(tile * LANES, (tile + 1) * LANES)
            span = slice(row + tile * low, row + tile * low + low)
            row_outs[0][span, :], row_outs[1][span, :] = pair(
                "rows", ref[index + (slice(rows - low, rows), lanes)], ref[index + (slice(0, low), lanes)]
            )


def pack_corners(first, second, first_out, second_out):
    first_out[CORNER_ROWS - 8 :, :] = jnp.zeros((8, LANES), jnp.float32)
    second_out[CORNER_ROWS - 8 :, :] = jnp.zeros((8, LANES), jnp.float32)
    for tile, (base, rows) in TILE_ROWS.items():
        rim = TILE_RIM[tile]
        end, begin = slice(base + rows - rim, base + rows), slice(base, base + rim)
        ends = pair("columns", second[end, :], first[end, :])
        begins = pair("columns", second[begin, :], first[begin, :])
        for side in range(2):
            row = CORNERS[tile, side]
            first_out[row : row + rim, :], second_out[row : row + rim, :] = pair("corners", ends[side], begins[side])


def across(tiles, steps, wanted):
    count = len(tiles)
    lane = iota(tiles[0].shape, 1)
    rolled = [turned(tile, -steps, 1) for tile in tiles]
    if steps > 0:
        return [jnp.where(lane < LANES - steps, rolled[t], rolled[(t + 1) % count]) for t in range(wanted)]
    return [jnp.where(lane >= -steps, rolled[t], rolled[(t - 1) % count]) for t in range(wanted)]


def first_of(down2, down1, up1, up2, spacing):
    return (8.0 * (up1 - down1) - (up2 - down2)) * (1.0 / (12.0 * spacing))


def second_of(down2, down1, here, up1, up2, spacing):
    return (16.0 * (up1 + down1) - (up2 + down2) - 30.0 * here) * (1.0 / (12.0 * spacing * spacing))


def across_all(tiles, wanted):
    return [across(tiles, steps, wanted) for steps in (-2, -1, 1, 2)]


def slopes(field, along_x, along_y, plane, start, rows, wanted, spacing):
    count = field.count
    for t in range(count):
        down2, down1, up1, up2 = (field[0, plane, t, pl.ds(start + d, rows), :] for d in (-2, -1, 1, 2))
        along_x[plane, t, start : start + rows, :] = first_of(down2, down1, up1, up2, spacing)
    span = slice(start - 4, start + rows + 4)
    shifted = across_all([field[1, plane, t, span, :] for t in range(count)], wanted)
    for t in range(wanted):
        along_y[plane, t, span, :] = first_of(*(s[t] for s in shifted), spacing)


def acceleration(field, along_x, along_y, mixed, planes, start, rows, wanted, spacing, shear, lame):
    above, plane, under = planes
    count = field.count
    half = 1.0 / (2.0 * spacing)
    square = 1.0 / (spacing * spacing)
    span = slice(start, start + rows)
    wide = slice(start - 4, start + rows + 4)
    for t in range(wanted):
        mixed[t, wide, :] = along_y[plane, t, wide, :] + half * (
            field[2, under, t, wide, :] - field[2, above, t, wide, :]
        )
    twist = [
        along_x[plane, t, span, :] + half * (field[2, under, t, span, :] - field[2, above, t, span, :])
        for t in range(count)
    ]
    twist = across_all(twist, wanted)
    laps, seconds = [], []
    for c in range(3):
        shifted = across_all([field[c, plane, t, span, :] for t in range(count)], wanted)
        lap, second = [], []
        for t in range(wanted):
            here = field[c, plane, t, span, :]
            down2, down1, up1, up2 = (field[c, plane, t, pl.ds(start + d, rows), :] for d in (-2, -1, 1, 2))
            in_x = second_of(down2, down1, here, up1, up2, spacing)
            in_y = second_of(shifted[0][t], shifted[1][t], here, shifted[2][t], shifted[3][t], spacing)
            in_z = square * (field[c, under, t, span, :] - 2.0 * here + field[c, above, t, span, :])
            lap.append(in_x + in_y + in_z)
            second.append((in_x, in_y, in_z)[c])
        laps.append(lap)
        seconds.append(second)
    out = [[], [], []]
    for t in range(wanted):
        ends = (mixed[t, pl.ds(start + d, rows), :] for d in (-2, -1, 1, 2))
        div_x = seconds[0][t] + first_of(*ends, spacing)
        div_y = seconds[1][t] + first_of(*(s[t] for s in twist), spacing)
        lower = along_x[under, t, span, :] + along_y[under, t, span, :]
        upper = along_x[above, t, span, :] + along_y[above, t, span, :]
        div_z = seconds[2][t] + half * (lower - upper)
        bulk = lame[t] + shear[t]
        for c, div in enumerate((div_x, div_y, div_z)):
            out[c].append(shear[t] * laps[c][t] + bulk * div)
    return out


def exact_dot(value, pick):
    high = value.astype(jnp.bfloat16)
    rest = value - high.astype(jnp.float32)
    middle = rest.astype(jnp.bfloat16)
    low = (rest - middle.astype(jnp.float32)).astype(jnp.bfloat16)
    dot = lambda part: jnp.dot(part, pick, preferred_element_type=jnp.float32)
    return dot(high) + (dot(middle) + dot(low))


def prolonged(tiles):
    odd_x = [0.5 * (tile + turned(tile, -1, 0)) for tile in tiles]
    next_y = across(tiles, 1, 2)
    next_odd = across(odd_x, 1, 2)
    return (
        tiles,
        [0.5 * (a + b) for a, b in zip(tiles, next_y)],
        odd_x,
        [0.5 * (a + b) for a, b in zip(odd_x, next_odd)],
    )


def restricted(parts):
    even_even, even_odd, odd_even, odd_odd = parts
    even = [0.5 * a + 0.25 * (b + turned(b, 1, 0)) for a, b in zip(even_even, odd_even)]
    odd = [0.5 * a + 0.25 * (b + turned(b, 1, 0)) for a, b in zip(even_odd, odd_odd)]
    return [0.5 * a + 0.25 * (b + c) for a, b, c in zip(even, odd, across(odd, -1, 2))]


def largest(values):
    total = values[0]
    for value in values[1:]:
        total = jnp.maximum(total, value)
    return jnp.max(total)


def smallest(values):
    total = values[0]
    for value in values[1:]:
        total = jnp.minimum(total, value)
    return jnp.min(total)


def pick(lines, marks, wanted):
    begin = smallest([jnp.where(m == wanted, a, -FAR) for m, (a, _) in zip(marks, lines)])
    slope = largest([jnp.where(m == wanted, b, FAR) for m, (_, b) in zip(marks, lines)])
    return begin, slope


def top_line(lines, step):
    values = [a + step * b for a, b in lines]
    top = largest(values)
    return pick(lines, values, top)


def next_line(lines, begin, slope, limit):
    crossings = []
    for a, b in lines:
        steeper = b - slope
        crossings.append(jnp.where(steeper > 0.0, (begin - a) / steeper, -FAR))
    nearest = smallest(crossings)
    found = nearest <= limit
    new_begin, new_slope = pick(lines, crossings, nearest)
    return jnp.where(found, new_begin, begin), jnp.where(found, new_slope, slope), found


def envelopes(first, last, peak):
    lane = iota((1, LANES), 1)
    bound = 0.3 / jnp.full((8, LANES), peak, jnp.float32)
    bound = bound * bound * 1.00001
    limit = jnp.max(bound)
    first_begin, first_slope = top_line(first, STEP_LOW)
    last_begin, last_slope = top_line(last, STEP_LOW)
    first_top = largest([a + bound * b for a, b in first])
    last_top = largest([a + bound * b for a, b in last])
    single = (jnp.max(first_begin + bound * first_slope) >= first_top) & (
        jnp.max(last_begin + bound * last_slope) >= last_top
    )
    message = jnp.where(
        lane < 32,
        first_begin,
        jnp.where(lane < 64, first_slope, jnp.where(lane < 96, last_begin, last_slope)),
    )

    def more(state):
        return (state[0] < SLOTS) & (state[1] > 0)

    def step(state):
        n, _, fa, fb, la, lb, message = state
        fa, fb, found_first = next_line(first, fa, fb, limit)
        la, lb, found_last = next_line(last, la, lb, limit)
        message = jnp.where(lane == n, fa, message)
        message = jnp.where(lane == n + 32, fb, message)
        message = jnp.where(lane == n + 64, la, message)
        message = jnp.where(lane == n + 96, lb, message)
        found = (found_first | found_last).astype(jnp.int32)
        return n + 1, found, fa, fb, la, lb, message

    left = jnp.where(single, 0, 1).astype(jnp.int32)
    start = (jnp.int32(1), left, first_begin, first_slope, last_begin, last_slope, message)
    _, left, _, _, _, _, message = lax.while_loop(more, step, start)
    return message, left.astype(jnp.float32)


def sealed(message, peak, flag):
    lane = iota((1, LANES), 1)
    return jnp.where(lane == PEAK_LANE, peak, jnp.where(lane == FLAG_LANE, flag, message))


def opened(received):
    first, last = [], []
    rows = received.shape[0]
    lane = iota((8, LANES), 1)
    peak, flag = [], []
    for r in range(0, rows, 8):
        begin = received[r : r + 8, :]
        slope = turned(begin, -32, 1)
        in_first = lane < SLOTS
        in_last = (lane >= 64) & (lane < 64 + SLOTS)
        first.append((jnp.where(in_first, begin, FAR), jnp.where(in_first, slope, 0.0)))
        last.append((jnp.where(in_last, begin, FAR), jnp.where(in_last, slope, 0.0)))
        peak.append(jnp.where(lane == PEAK_LANE, begin, 0.0))
        flag.append(jnp.where(lane == FLAG_LANE, begin, 0.0))
    return first, last, largest(peak), largest(flag)


class Tiles:
    def __init__(self, own, rim):
        self.own, self.rim = own, rim
        self.count = own.shape[-3] + 1

    def __getitem__(self, index):
        *plane, tile, rows, lanes = index
        if tile < self.count - 1:
            return self.own[(*plane, tile, rows, lanes)]
        return self.rim[(*plane, rows, lanes)]


def home(key, fine, rest, coarse, coarse_rest):
    if key in DEEP_REST:
        return rest.at[DEEP_REST.index(key)]
    if key in COARSE_REST:
        return coarse_rest.at[COARSE_REST.index(key)]
    return (fine if key[0] == "fn" else coarse).at[key[1]]


def received(what, pieces, span):
    return pair(what, pieces[1][span, :], pieces[0][span, :])


def place_kernel(*refs):
    named = dict(zip(NAMES, refs[:10]))
    rims, targets = refs[10:12], refs[12:16]
    for key, low, _, tile, _, row, own in ENTRIES:
        target = home(key, *targets)
        rows = TILE_ROWS[tile][1]
        total = target.shape[1]
        for t in range(own):
            if low > 2:
                target[t, 0:rows, :] = jnp.zeros((rows, LANES), jnp.float32)
                target[t, 2 * rows : total, :] = jnp.zeros((total - 2 * rows, LANES), jnp.float32)
            target[t, rows : 2 * rows, :] = own_tile(named, key, t)
            below, beyond = received("rows", rims, slice(row + t * low, row + t * low + low))
            target[t, rows - low : rows, :] = below
            target[t, 2 * rows : 2 * rows + low, :] = beyond
    coarse = targets[2]
    coarse[:, 8] = jnp.zeros(coarse.shape[:1] + coarse.shape[2:], jnp.float32)


def main_kernel(*refs):
    named = dict(zip(("fd", "fs", "fl", "cd", "cs", "cl"), refs[:6]))
    sides, corners = refs[6:8], refs[8:10]
    split_pick, weave_pick = refs[10:12]
    owns = refs[12:16]
    fine_rate, coarse_rate, plane_out, iterate_out, lines_out, message_out = refs[16:22]
    rims = refs[22:26]
    fine_x, fine_y, coarse_x, coarse_y = refs[26:30]
    mixed, planes, parted, woven, ends = refs[30:35]
    packed = dict(zip(TILE_ROWS, zip(refs[35:39], refs[39:43])))
    fine, rest, coarse, coarse_rest = (Tiles(own, rim) for own, rim in zip(owns, rims))
    slot = {key: i for i, key in enumerate(DEEP_REST)}
    coarse_slot = {key: i for i, key in enumerate(COARSE_REST)}

    for tile, (base, rows) in TILE_ROWS.items():
        rim = TILE_RIM[tile]
        own = received("columns", sides, slice(base, base + rows))
        for side in range(2):
            target = packed[tile][side]
            target[...] = jnp.zeros(target.shape, jnp.float32)
            target[rows : 2 * rows, :] = own[side]
            row = CORNERS[tile, side]
            low, high = received("corners", corners, slice(row, row + rim))
            target[rows - rim : rows, :] = low
            target[2 * rows : 2 * rows + rim, :] = high
    for key, low, high, tile, at, _, _ in ENTRIES:
        low_side, high_side = packed[tile][0][...], packed[tile][1][...]
        lane = iota(low_side.shape, 1)
        home(key, *rims)[...] = jnp.where(
            lane < high,
            turned(high_side, -at, 1),
            jnp.where(lane >= LANES - low, turned(low_side, -(at + low), 1), 0.0),
        )
    rims[2][:, 8] = jnp.zeros(rims[2].shape[:1] + rims[2].shape[2:], jnp.float32)

    for k in range(5):
        slopes(fine, fine_x, fine_y, k, 16, 16, 2, 1.0)
    for k in (5, 6, 7):
        slopes(fine, fine_x, fine_y, k, 8, 32, 3, 1.0)

    def fine_plane(k):
        above = 1 if k == 0 else k - 1
        own = [slice(t * LANES, (t + 1) * LANES) for t in range(2)]
        shear = [named["fs"][k, :, lanes] for lanes in own]
        lame = [named["fl"][k, :, lanes] for lanes in own]
        accel = acceleration(fine, fine_x, fine_y, mixed, (above, k, k + 1), 16, 16, 2, 1.0, shear, lame)
        for c in range(3):
            for t in range(2):
                fine_rate[c, k, :, own[t]] = accel[c][t] / named["fd"][k, :, own[t]]

    for k in range(6):
        fine_plane(k)

    window = slice(8, 40)
    shear = [rest[slot[("fs", (6,))], t, window, :] for t in range(3)]
    lame = [rest[slot[("fl", (6,))], t, window, :] for t in range(3)]
    accel = acceleration(fine, fine_x, fine_y, mixed, (5, 6, 7), 8, 32, 3, 1.0, shear, lame)
    for t in range(3):
        density = rest[slot[("fd", (6,))], t, window, :]
        filled = density > 0.0
        density = jnp.where(filled, density, 1.0)
        for c in range(3):
            rate = jnp.where(filled, accel[c][t] / density, 0.0)
            planes[3 + c, t, :, :] = rate
            planes[c, t, :, :] = 2.0 * fine[c, 6, t, window, :] - rest[c, t, window, :]
            if t < 2:
                fine_rate[c, 6, :, t * LANES : (t + 1) * LANES] = rate[8:24, :]
        fine_shear = rest[slot[("fs", (7,))], t, window, :]
        planes[6, t, :, :] = fine_shear
        planes[7, t, :, :] = rest[slot[("fl", (7,))], t, window, :] + 2.0 * fine_shear

    stacked = jnp.concatenate(
        [
            jnp.concatenate([planes[p, t, pl.ds(odd, 16, stride=2), :] for t in range(3)], axis=1)
            for p in range(8)
            for odd in range(2)
        ],
        axis=0,
    )
    parted[...] = exact_dot(stacked, split_pick[...])

    def four(p):
        return tuple(
            [
                parted[p * 32 + odd_x * 16 : p * 32 + odd_x * 16 + 16, (odd_y * 2 + t) * LANES : (odd_y * 2 + t + 1) * LANES]
                for t in range(2)
            ]
            for odd_x in range(2)
            for odd_y in range(2)
        )

    for k in range(8):
        slopes(coarse, coarse_x, coarse_y, k, 4, 16, 2, 2.0)
    coarse_x[8] = jnp.zeros(coarse_x.shape[1:], jnp.float32)
    coarse_y[8] = jnp.zeros(coarse_y.shape[1:], jnp.float32)

    def coarse_plane(k):
        shear = [named["cs"][k]]
        lame = [named["cl"][k]]
        accel = acceleration(coarse, coarse_x, coarse_y, mixed, (k - 1, k, k + 1), 8, 8, 1, 2.0, shear, lame)
        for c in range(3):
            coarse_rate[c, k - 1] = accel[c][0] / named["cd"][k]

    for k in range(2, 8):
        coarse_plane(k)
    band = slice(4, 20)

    def coarse_pair(name, k):
        return [coarse_rest[coarse_slot[(name, (k,))], t, band, :] for t in range(2)]

    shear, lame, density = coarse_pair("cs", 1), coarse_pair("cl", 1), coarse_pair("cd", 1)
    accel = acceleration(coarse, coarse_x, coarse_y, mixed, (0, 1, 2), 4, 16, 2, 2.0, shear, lame)
    below_rate = [[], [], []]
    for c in range(3):
        for t in range(2):
            filled = density[t] > 0.0
            rate = jnp.where(filled, accel[c][t] / jnp.where(filled, density[t], 1.0), 0.0)
            below_rate[c].append(rate)
        coarse_rate[c, 0] = below_rate[c][0][4:12, :]

    shear, lame = coarse_pair("cs", 0), coarse_pair("cl", 0)
    row = iota((16, LANES), 0) + (lax.axis_index("gx") * 8 - 4)
    lane = iota((16, LANES), 1) + lax.axis_index("gy") * LANES
    column = [lane, jnp.where(iota((16, LANES), 1) < 64, lane + LANES, lane - LANES)]
    extent = (lax.axis_size("gx") * 8, lax.axis_size("gy") * LANES)
    fine_moduli = (four(6), four(6), four(7))
    coarse_moduli = (shear, shear, [l + 2.0 * s for l, s in zip(lame, shear)])
    for c in range(3):
        moduli = fine_moduli[c]
        half = [0.5 * m for m in coarse_moduli[c]]
        spread = restricted(moduli)
        inverse = []
        for t in range(2):
            diagonal = half[t] + 0.5625 * spread[t]
            x, y = row, column[t]
            inside = (x >= 0) & (x < extent[0]) & (y >= 0) & (y < extent[1]) & (diagonal > 0.0)
            inverse.append(jnp.where(inside, 1.0 / jnp.where(inside, diagonal, 1.0), 0.0))
        for part in range(2):
            if part == 0:
                now = [coarse[c, 0, t, band, :] for t in range(2)]
                before = [coarse_rest[coarse_slot[("cb", (c, 0))], t, band, :] for t in range(2)]
                iterate = [2.0 * a - b for a, b in zip(now, before)]
                now = [coarse[c, 1, t, band, :] for t in range(2)]
                before = [coarse_rest[coarse_slot[("cb", (c, 1))], t, band, :] for t in range(2)]
                below = [2.0 * a - b for a, b in zip(now, before)]
            else:
                iterate = [jnp.zeros((16, LANES), jnp.float32)] * 2
                below = below_rate[c]
            above = four(3 * part + c)
            fixed = restricted([[m * a for m, a in zip(ms, as_)] for ms, as_ in zip(moduli, above)])
            fixed = [h * b + f for h, b, f in zip(half, below, fixed)]

            def mismatch_of(iterate):
                stress = [[m * a for m, a in zip(ms, ps)] for ms, ps in zip(moduli, prolonged(iterate))]
                return [h * i + (s - f) for h, i, s, f in zip(half, iterate, restricted(stress), fixed)]

            mismatch = mismatch_of(iterate)
            ends[part, c] = mismatch[0]
            for _ in range(ITERS):
                iterate = [i - m * v for i, m, v in zip(iterate, mismatch, inverse)]
                mismatch = mismatch_of(iterate)
            ends[2 + part, c] = mismatch[0]
            ends[4 + part, c] = iterate[0]
            even_even, even_odd, odd_even, odd_odd = prolonged(iterate)
            at = (part * 3 + c) * 32
            woven[at : at + 16, 0:LANES] = even_even[0]
            woven[at : at + 16, LANES : 2 * LANES] = even_odd[0]
            woven[at + 16 : at + 32, 0:LANES] = odd_even[0]
            woven[at + 16 : at + 32, LANES : 2 * LANES] = odd_odd[0]

    woven[...] = exact_dot(woven[...], weave_pick[...])
    for part in range(2):
        for c in range(3):
            iterate_out[part, c] = ends[4 + part, c, 4:12, :]
            for odd in range(2):
                at = (part * 3 + c) * 32 + odd * 16 + 4
                for t in range(2):
                    plane_out[part, c, t, pl.ds(odd, 8, stride=2), :] = woven[
                        at : at + 8, t * LANES : (t + 1) * LANES
                    ]

    lines = []
    for which in range(2):
        found = []
        for c in range(3):
            begin, slope = ends[2 * which, c, 4:12, :], ends[2 * which + 1, c, 4:12, :]
            lines_out[2 * which, c] = begin
            lines_out[2 * which + 1, c] = slope
            found += [(begin, slope), (-begin, -slope)]
        lines.append(found)
    ratio = (named["fl"][...] + 2.0 * named["fs"][...]) / named["fd"][...]
    coarse_ratio = (named["cl"][...] + 2.0 * named["cs"][...]) / named["cd"][...]
    fine_peak = jnp.sqrt(jnp.full((8, LANES), jnp.max(ratio), jnp.float32))
    coarse_peak = jnp.sqrt(jnp.full((8, LANES), jnp.max(coarse_ratio), jnp.float32))
    peak = jnp.max(jnp.maximum(fine_peak, 0.5 * coarse_peak))
    message, flag = envelopes(lines[0], lines[1], peak)
    message_out[...] = jnp.broadcast_to(sealed(message, peak, flag), message_out.shape)


def merge_kernel(received, message_out):
    first, last, peak, flag = opened(received)
    message, full = envelopes(first, last, peak)
    message_out[...] = jnp.broadcast_to(sealed(message, peak, jnp.maximum(flag, full)), message_out.shape)


def final_kernel(
    received, fn, fb, cn, cb, fine_rate, coarse_rate, plane, iterate, fine_out, coarse_out, ratio_out, square_out, flag_out
):
    first, last, peak, flag = opened(received)
    step = 0.3 / jnp.full((8, LANES), peak, jnp.float32)
    square = step * step
    first_max = largest([a + square * b for a, b in first])
    last_max = largest([a + square * b for a, b in last])
    ratio = last_max / (jnp.full((8, LANES), first_max, jnp.float32) + 1e-06)
    ratio_out[0] = jnp.max(ratio)
    square_out[0] = jnp.max(square)
    flag_out[0] = jnp.where((flag > 0.0) | (jnp.max(square) < STEP_LOW), 1, 0)
    square = square[0:1, 0:1]
    for c in range(3):
        fine_out[c, 0:7] = 2.0 * fn[c, 0:7] - fb[c, 0:7] + square * fine_rate[c]
        coarse_out[c, 1:8] = 2.0 * cn[c, 1:8] - cb[c, 1:8] + square * coarse_rate[c]
        coarse_out[c, 0] = iterate[0, c] + square * iterate[1, c]
        for t in range(2):
            fine_out[c, 7, :, t * LANES : (t + 1) * LANES] = plane[0, c, t] + square * plane[1, c, t]


def exchange(first, second, what, columns, rows):
    axis, begin = FIRST_PAIRS[what]

    def swap(value, parity):
        ups = []
        for i in range(columns):
            for j in range(rows):
                turned_parity = 1 - parity if axis == "gy" and i >= TURN else parity
                place, count, step = (j, rows, 1) if axis == "gy" else (i, columns, rows)
                if place % 2 == turned_parity and place + 1 < count:
                    ups.append((i * rows + j, i * rows + j + step))
        return lax.ppermute(value, ("gx", "gy"), ups + [(j, i) for i, j in ups])

    return swap(first, begin), swap(second, 1 - begin)


def gather_groups(columns, rows):
    ring, plane = {}, {}
    for i in range(columns):
        for j in range(rows):
            chip_y, core, z, x = i // 2 % 4, i % 2, (i // 8, j % 4), j // 4
            ring.setdefault((x, chip_y), []).append(i * rows + j)
            plane.setdefault((z, core), []).append(i * rows + j)
    return list(ring.values()), list(plane.values())


def split_matrix():
    lane = np.arange(3 * LANES)
    fine_column = np.where(lane < 320, lane, lane - 384)[:, None]
    circle = np.arange(2 * LANES)
    coarse_column = np.where(circle < 192, circle, circle - 256)[None, :]
    return np.concatenate(
        [fine_column == 2 * coarse_column, fine_column == 2 * coarse_column + 1], axis=1
    ).astype(ml_dtypes.bfloat16)


def weave_matrix():
    lane = np.arange(2 * LANES)
    target = np.where(lane < LANES, 2 * lane, 2 * (lane - LANES) + 1)[:, None]
    return (target == lane[None, :]).astype(ml_dtypes.bfloat16)


def f32(*shape):
    return jax.ShapeDtypeStruct(shape, jnp.float32)


def vm(*shape):
    return pltpu.VMEM(shape, jnp.float32)


def make_shards(columns, rows):
    ring, plane_groups = gather_groups(columns, rows)
    axes = ("gx", "gy")

    def shards(*args):
        in_vmem = pl.BlockSpec(memory_space=pltpu.VMEM)
        in_smem = pl.BlockSpec(memory_space=pltpu.SMEM)
        in_hbm = pl.BlockSpec(memory_space=pltpu.HBM)

        def call(kernel, ins, outs, scratch=(), out_specs=None, cost=None, limit=16):
            return pl.pallas_call(
                kernel,
                out_shape=outs,
                in_specs=ins,
                out_specs=out_specs or ([in_vmem] * len(outs) if isinstance(outs, tuple) else in_vmem),
                scratch_shapes=list(scratch),
                compiler_params=pltpu.CompilerParams(vmem_limit_bytes=limit * 1024 * 1024),
                cost_estimate=cost,
            )

        fn, fb, _, _, _, cn, cb, _, _, _ = args
        first_side, second_side, first_rim, second_rim = call(
            pack,
            [in_hbm] * 10,
            (pltpu.VMEM((PACKED_ROWS, LANES), jnp.float32),) * 2 + (pltpu.VMEM((RIM_ROWS, LANES), jnp.float32),) * 2,
            [vm(*a.shape) for a in args] + [pltpu.SemaphoreType.DMA((len(PACK_SOURCES),))],
        )(*[pltpu.with_memory_space_constraint(a, pltpu.HBM) for a in args])
        sides = exchange(first_side, second_side, "columns", columns, rows)
        rims = exchange(first_rim, second_rim, "rows", columns, rows)
        first, second = call(
            pack_corners,
            [in_vmem] * 2,
            (f32(CORNER_ROWS, LANES),) * 2,
            cost=pl.CostEstimate(flops=10**12, bytes_accessed=10**9, transcendentals=0),
        )(*sides)
        corners = exchange(first, second, "corners", columns, rows)
        ring_size, plane_size = len(ring[0]), len(plane_groups[0])
        own_shapes = ((3, 8, 2, 48, LANES), (8, 2, 48, LANES), (3, 9, 1, 24, LANES), (11, 1, 24, LANES))
        owns = call(place_kernel, [in_vmem] * 12, tuple(f32(*shape) for shape in own_shapes))(
            *args, *[pltpu.with_memory_space_constraint(rim, pltpu.VMEM) for rim in rims]
        )
        outs = (
            f32(3, 7, 16, 256),
            f32(3, 7, 8, 128),
            f32(2, 3, 2, 16, 128),
            f32(2, 3, 8, 128),
            f32(4, 3, 8, 128),
            f32(ring_size, LANES),
        )
        scratch = [vm(*shape[:-3], *shape[-2:]) for shape in own_shapes] + [
            vm(8, 3, 48, LANES),
            vm(8, 3, 48, LANES),
            vm(9, 2, 24, LANES),
            vm(9, 2, 24, LANES),
            vm(3, 48, LANES),
            vm(8, 3, 32, LANES),
            vm(256, 512),
            vm(192, 256),
            vm(6, 3, 16, LANES),
        ]
        scratch += [vm(48, LANES), vm(48, LANES), vm(24, LANES), vm(24, LANES)] * 2
        fine_rate, coarse_rate, plane, iterate, lines, message = call(main_kernel, [in_vmem] * 16, outs, scratch)(
            *args[2:5],
            *args[7:],
            *sides,
            *corners,
            jnp.asarray(split_matrix()),
            jnp.asarray(weave_matrix()),
            *owns,
        )
        received = lax.all_to_all(message, axes, 0, 0, tiled=True, axis_index_groups=ring)
        message = call(merge_kernel, [in_vmem], f32(plane_size, LANES))(received)
        received = lax.all_to_all(message, axes, 0, 0, tiled=True, axis_index_groups=plane_groups)
        fine_next, coarse_next, ratio, square, flag = call(
            final_kernel,
            [in_vmem] * 9,
            (f32(*fn.shape), f32(*cn.shape), f32(1), f32(1), jax.ShapeDtypeStruct((1,), jnp.int32)),
            out_specs=[in_vmem] * 2 + [in_smem] * 3,
        )(received, fn, fb, cn, cb, fine_rate, coarse_rate, plane, iterate)

        def plain():
            values = jnp.abs(lines[0::2] + square[0] * lines[1::2])
            tops = lax.pmax(jnp.max(values, axis=(1, 2, 3)), axes)
            return tops[1] / (tops[0] + 1e-06)

        reduction = lax.cond(flag[0] > 0, plain, lambda: ratio[0])
        return fine_next, coarse_next, reduction

    return shards


def solution(mesh):
    placed = (
        P(None, None, "gx", "gy"),
        P(None, None, "gx", "gy"),
        P(None, "gx", "gy"),
        P(None, "gx", "gy"),
        P(None, "gx", "gy"),
        P(None, None, "gx", "gy"),
        P(None, None, "gx", "gy"),
        P(None, "gx", "gy"),
        P(None, "gx", "gy"),
        P(None, "gx", "gy"),
    )
    return jax.shard_map(
        make_shards(mesh.shape["gx"], mesh.shape["gy"]),
        mesh=mesh,
        in_specs=placed,
        out_specs=(P(None, None, "gx", "gy"), P(None, None, "gx", "gy"), P()),
        check_vma=False,
    )
```

```python
import jax
import jax.numpy as jnp
import ml_dtypes
import numpy as np
from jax import lax
from jax.experimental import pallas as pl
from jax.experimental.pallas import tpu as pltpu
from jax.sharding import PartitionSpec as P

ITERS = 3
LANES = 128
NAMES = ("fn", "fb", "fd", "fs", "fl", "cn", "cb", "cd", "cs", "cl")

DEEP_NOW = [("fn", (c, k)) for c in range(3) for k in (5, 6, 7)]
THIN_NOW = [("fn", (c, k)) for c in range(3) for k in range(5)]
DEEP_REST = [("fb", (c, 6)) for c in range(3)] + [("fd", (6,)), ("fs", (6,)), ("fl", (6,)), ("fs", (7,)), ("fl", (7,))]
COARSE_NOW = [("cn", (c, k)) for c in range(3) for k in range(3)]
COARSE_REST = [("cb", (c, k)) for c in range(3) for k in range(2)] + [
    ("cd", (1,)),
    ("cs", (0,)),
    ("cl", (0,)),
    ("cs", (1,)),
    ("cl", (1,)),
]
COARSE_THIN = [("cn", (c, k)) for c in range(3) for k in range(3, 8)]

TILE_ROWS = {"A": (0, 16), "B": (16, 16), "C": (16, 8), "D": (24, 8)}
TILE_RIM = {"A": 9, "B": 7, "C": 5, "D": 5}
PACKED_ROWS = 32


def plan():
    entries, lane, row = [], {"A": 0, "B": 0, "C": 7 * len(DEEP_REST), "D": 7 * len(DEEP_REST)}, 0
    for tile, keys, low, high in (
        ("A", DEEP_NOW, 9, 8),
        ("A", THIN_NOW, 2, 2),
        ("B", DEEP_REST, 7, 6),
        ("C", COARSE_NOW, 5, 5),
        ("D", COARSE_REST, 4, 4),
        ("C", COARSE_THIN[:13], 2, 2),
        ("D", COARSE_THIN[13:], 2, 2),
    ):
        for key in keys:
            own = 1 if tile in "CD" else 2
            entries.append((key, low, high, tile, lane[tile], row, own))
            lane[tile] += low
            row += own * low
    corners, corner_row = {}, 0
    for tile in TILE_ROWS:
        for side in range(2):
            corners[tile, side] = corner_row
            corner_row += TILE_RIM[tile]
    return entries, corners, -(-row // 8) * 8, -(-corner_row // 8) * 8


ENTRIES, CORNERS, RIM_ROWS, CORNER_ROWS = plan()

PACK_SOURCES = (
    ("fn", ()),
    ("fb", (slice(None), slice(6, 7))),
    ("fd", (slice(6, 7),)),
    ("fs", (slice(6, 8),)),
    ("fl", (slice(6, 8),)),
    ("cn", ()),
    ("cb", (slice(None), slice(0, 2))),
    ("cd", (slice(1, 2),)),
    ("cs", (slice(0, 2),)),
    ("cl", (slice(0, 2),)),
)

SLOTS = 31
PEAK_LANE = 31
FLAG_LANE = 63
STEP_LOW = 0.02
FAR = -1.0e30


def iota(shape, dim):
    return lax.broadcasted_iota(jnp.int32, shape, dim)


def turned(value, steps, axis):
    size = value.shape[axis]
    steps = steps % size
    return value if steps == 0 else pltpu.roll(value, steps, axis)


def own_tile(refs, key, tile):
    name, index = key
    return refs[name][index + (slice(None), slice(tile * LANES, (tile + 1) * LANES))]


FIRST_PAIRS = {"columns": ("gy", 1), "rows": ("gx", 1), "corners": ("gx", 1)}
TURN = 16


def begins(what, row):
    begin = FIRST_PAIRS[what][1]
    return jnp.where(row < TURN, begin, 1 - begin) if what == "columns" else begin


def pair(what, low, high):
    upward = lax.axis_index(FIRST_PAIRS[what][0]) % 2 == begins(what, lax.axis_index("gx"))
    return jnp.where(upward, low, high), jnp.where(upward, high, low)


def pack(*refs):
    sources = dict(zip(NAMES, refs[:10]))
    column_outs, row_outs = refs[10:12], refs[12:14]
    named = dict(zip(NAMES, refs[14:24]))
    sems = refs[24]
    copies = []
    for i, (name, part) in enumerate(PACK_SOURCES):
        source, target = sources[name], named[name]
        if part:
            source, target = source.at[part], target.at[part]
        copies.append(pltpu.make_async_copy(source, target, sems.at[i]))
    for copy in copies:
        copy.start()
    for copy in copies:
        copy.wait()
    for tile, (base, rows) in TILE_ROWS.items():
        lane = iota((rows, LANES), 1)
        low_sum = jnp.zeros((rows, LANES), jnp.float32)
        high_sum = low_sum
        for key, low, _, where, at, _, own in ENTRIES:
            if where != tile:
                continue
            inside = (lane >= at) & (lane < at + low)
            low_sum = jnp.where(inside, turned(own_tile(named, key, own - 1), at + low, 1), low_sum)
            high_sum = jnp.where(inside, turned(own_tile(named, key, 0), at, 1), high_sum)
        span = slice(base, base + rows)
        sums = pair("columns", low_sum, high_sum)
        for out, value in zip(column_outs, sums):
            out[span, :] = out[span, :] + value if tile in "CD" else value
    row_outs[0][RIM_ROWS - 8 :, :] = jnp.zeros((8, LANES), jnp.float32)
    row_outs[1][RIM_ROWS - 8 :, :] = jnp.zeros((8, LANES), jnp.float32)
    for (name, index), low, _, _, _, row, own in ENTRIES:
        ref = named[name]
        rows = ref.shape[-2]
        for tile in range(own):
            lanes = slice(tile * LANES, (tile + 1) * LANES)
            span = slice(row + tile * low, row + tile * low + low)
            row_outs[0][span, :], row_outs[1][span, :] = pair(
                "rows", ref[index + (slice(rows - low, rows), lanes)], ref[index + (slice(0, low), lanes)]
            )


def pack_corners(first, second, first_out, second_out):
    first_out[CORNER_ROWS - 8 :, :] = jnp.zeros((8, LANES), jnp.float32)
    second_out[CORNER_ROWS - 8 :, :] = jnp.zeros((8, LANES), jnp.float32)
    for tile, (base, rows) in TILE_ROWS.items():
        rim = TILE_RIM[tile]
        end, begin = slice(base + rows - rim, base + rows), slice(base, base + rim)
        ends = pair("columns", second[end, :], first[end, :])
        begins = pair("columns", second[begin, :], first[begin, :])
        for side in range(2):
            row = CORNERS[tile, side]
            first_out[row : row + rim, :], second_out[row : row + rim, :] = pair("corners", ends[side], begins[side])


def across(tiles, steps, wanted):
    count = len(tiles)
    lane = iota(tiles[0].shape, 1)
    rolled = [turned(tile, -steps, 1) for tile in tiles]
    if steps > 0:
        return [jnp.where(lane < LANES - steps, rolled[t], rolled[(t + 1) % count]) for t in range(wanted)]
    return [jnp.where(lane >= -steps, rolled[t], rolled[(t - 1) % count]) for t in range(wanted)]


def first_of(down2, down1, up1, up2, spacing):
    return (8.0 * (up1 - down1) - (up2 - down2)) * (1.0 / (12.0 * spacing))


def second_of(down2, down1, here, up1, up2, spacing):
    return (16.0 * (up1 + down1) - (up2 + down2) - 30.0 * here) * (1.0 / (12.0 * spacing * spacing))


def across_all(tiles, wanted):
    return [across(tiles, steps, wanted) for steps in (-2, -1, 1, 2)]


def slopes(field, along_x, along_y, plane, start, rows, wanted, spacing):
    count = field.count
    for t in range(count):
        down2, down1, up1, up2 = (field[0, plane, t, pl.ds(start + d, rows), :] for d in (-2, -1, 1, 2))
        along_x[plane, t, start : start + rows, :] = first_of(down2, down1, up1, up2, spacing)
    span = slice(start - 4, start + rows + 4)
    shifted = across_all([field[1, plane, t, span, :] for t in range(count)], wanted)
    for t in range(wanted):
        along_y[plane, t, span, :] = first_of(*(s[t] for s in shifted), spacing)


def acceleration(field, along_x, along_y, mixed, planes, start, rows, wanted, spacing, shear, lame):
    above, plane, under = planes
    count = field.count
    half = 1.0 / (2.0 * spacing)
    square = 1.0 / (spacing * spacing)
    span = slice(start, start + rows)
    wide = slice(start - 4, start + rows + 4)
    for t in range(wanted):
        mixed[t, wide, :] = along_y[plane, t, wide, :] + half * (
            field[2, under, t, wide, :] - field[2, above, t, wide, :]
        )
    twist = [
        along_x[plane, t, span, :] + half * (field[2, under, t, span, :] - field[2, above, t, span, :])
        for t in range(count)
    ]
    twist = across_all(twist, wanted)
    laps, seconds = [], []
    for c in range(3):
        shifted = across_all([field[c, plane, t, span, :] for t in range(count)], wanted)
        lap, second = [], []
        for t in range(wanted):
            here = field[c, plane, t, span, :]
            down2, down1, up1, up2 = (field[c, plane, t, pl.ds(start + d, rows), :] for d in (-2, -1, 1, 2))
            in_x = second_of(down2, down1, here, up1, up2, spacing)
            in_y = second_of(shifted[0][t], shifted[1][t], here, shifted[2][t], shifted[3][t], spacing)
            in_z = square * (field[c, under, t, span, :] - 2.0 * here + field[c, above, t, span, :])
            lap.append(in_x + in_y + in_z)
            second.append((in_x, in_y, in_z)[c])
        laps.append(lap)
        seconds.append(second)
    out = [[], [], []]
    for t in range(wanted):
        ends = (mixed[t, pl.ds(start + d, rows), :] for d in (-2, -1, 1, 2))
        div_x = seconds[0][t] + first_of(*ends, spacing)
        div_y = seconds[1][t] + first_of(*(s[t] for s in twist), spacing)
        lower = along_x[under, t, span, :] + along_y[under, t, span, :]
        upper = along_x[above, t, span, :] + along_y[above, t, span, :]
        div_z = seconds[2][t] + half * (lower - upper)
        bulk = lame[t] + shear[t]
        for c, div in enumerate((div_x, div_y, div_z)):
            out[c].append(shear[t] * laps[c][t] + bulk * div)
    return out


def exact_dot(value, pick):
    high = value.astype(jnp.bfloat16)
    rest = value - high.astype(jnp.float32)
    middle = rest.astype(jnp.bfloat16)
    low = (rest - middle.astype(jnp.float32)).astype(jnp.bfloat16)
    dot = lambda part: jnp.dot(part, pick, preferred_element_type=jnp.float32)
    return dot(high) + (dot(middle) + dot(low))


def prolonged(tiles):
    odd_x = [0.5 * (tile + turned(tile, -1, 0)) for tile in tiles]
    next_y = across(tiles, 1, 2)
    next_odd = across(odd_x, 1, 2)
    return (
        tiles,
        [0.5 * (a + b) for a, b in zip(tiles, next_y)],
        odd_x,
        [0.5 * (a + b) for a, b in zip(odd_x, next_odd)],
    )


def restricted(parts):
    even_even, even_odd, odd_even, odd_odd = parts
    even = [0.5 * a + 0.25 * (b + turned(b, 1, 0)) for a, b in zip(even_even, odd_even)]
    odd = [0.5 * a + 0.25 * (b + turned(b, 1, 0)) for a, b in zip(even_odd, odd_odd)]
    return [0.5 * a + 0.25 * (b + c) for a, b, c in zip(even, odd, across(odd, -1, 2))]


def largest(values):
    total = values[0]
    for value in values[1:]:
        total = jnp.maximum(total, value)
    return jnp.max(total)


def smallest(values):
    total = values[0]
    for value in values[1:]:
        total = jnp.minimum(total, value)
    return jnp.min(total)


def pick(lines, marks, wanted):
    begin = smallest([jnp.where(m == wanted, a, -FAR) for m, (a, _) in zip(marks, lines)])
    slope = largest([jnp.where(m == wanted, b, FAR) for m, (_, b) in zip(marks, lines)])
    return begin, slope


def top_line(lines, step):
    values = [a + step * b for a, b in lines]
    top = largest(values)
    return pick(lines, values, top)


def next_line(lines, begin, slope, limit):
    crossings = []
    for a, b in lines:
        steeper = b - slope
        crossings.append(jnp.where(steeper > 0.0, (begin - a) / steeper, -FAR))
    nearest = smallest(crossings)
    found = nearest <= limit
    new_begin, new_slope = pick(lines, crossings, nearest)
    return jnp.where(found, new_begin, begin), jnp.where(found, new_slope, slope), found


def envelopes(first, last, peak):
    lane = iota((1, LANES), 1)
    bound = 0.3 / jnp.full((8, LANES), peak, jnp.float32)
    bound = bound * bound * 1.00001
    limit = jnp.max(bound)
    first_begin, first_slope = top_line(first, STEP_LOW)
    last_begin, last_slope = top_line(last, STEP_LOW)
    first_top = largest([a + bound * b for a, b in first])
    last_top = largest([a + bound * b for a, b in last])
    single = (jnp.max(first_begin + bound * first_slope) >= first_top) & (
        jnp.max(last_begin + bound * last_slope) >= last_top
    )
    message = jnp.where(
        lane < 32,
        first_begin,
        jnp.where(lane < 64, first_slope, jnp.where(lane < 96, last_begin, last_slope)),
    )

    def more(state):
        return (state[0] < SLOTS) & (state[1] > 0)

    def step(state):
        n, _, fa, fb, la, lb, message = state
        fa, fb, found_first = next_line(first, fa, fb, limit)
        la, lb, found_last = next_line(last, la, lb, limit)
        message = jnp.where(lane == n, fa, message)
        message = jnp.where(lane == n + 32, fb, message)
        message = jnp.where(lane == n + 64, la, message)
        message = jnp.where(lane == n + 96, lb, message)
        found = (found_first | found_last).astype(jnp.int32)
        return n + 1, found, fa, fb, la, lb, message

    left = jnp.where(single, 0, 1).astype(jnp.int32)
    start = (jnp.int32(1), left, first_begin, first_slope, last_begin, last_slope, message)
    _, left, _, _, _, _, message = lax.while_loop(more, step, start)
    return message, left.astype(jnp.float32)


def sealed(message, peak, flag):
    lane = iota((1, LANES), 1)
    return jnp.where(lane == PEAK_LANE, peak, jnp.where(lane == FLAG_LANE, flag, message))


def opened(received):
    first, last = [], []
    rows = received.shape[0]
    lane = iota((8, LANES), 1)
    peak, flag = [], []
    for r in range(0, rows, 8):
        begin = received[r : r + 8, :]
        slope = turned(begin, -32, 1)
        in_first = lane < SLOTS
        in_last = (lane >= 64) & (lane < 64 + SLOTS)
        first.append((jnp.where(in_first, begin, FAR), jnp.where(in_first, slope, 0.0)))
        last.append((jnp.where(in_last, begin, FAR), jnp.where(in_last, slope, 0.0)))
        peak.append(jnp.where(lane == PEAK_LANE, begin, 0.0))
        flag.append(jnp.where(lane == FLAG_LANE, begin, 0.0))
    return first, last, largest(peak), largest(flag)


class Tiles:
    def __init__(self, own, rim):
        self.own, self.rim = own, rim
        self.count = own.shape[-3] + 1

    def __getitem__(self, index):
        *plane, tile, rows, lanes = index
        if tile < self.count - 1:
            return self.own[(*plane, tile, rows, lanes)]
        return self.rim[(*plane, rows, lanes)]


def home(key, fine, rest, coarse, coarse_rest):
    if key in DEEP_REST:
        return rest.at[DEEP_REST.index(key)]
    if key in COARSE_REST:
        return coarse_rest.at[COARSE_REST.index(key)]
    return (fine if key[0] == "fn" else coarse).at[key[1]]


def received(what, pieces, span):
    return pair(what, pieces[1][span, :], pieces[0][span, :])


def place_kernel(*refs):
    named = dict(zip(NAMES, refs[:10]))
    rims, targets = refs[10:12], refs[12:16]
    for key, low, _, tile, _, row, own in ENTRIES:
        target = home(key, *targets)
        rows = TILE_ROWS[tile][1]
        total = target.shape[1]
        for t in range(own):
            if low > 2:
                target[t, 0:rows, :] = jnp.zeros((rows, LANES), jnp.float32)
                target[t, 2 * rows : total, :] = jnp.zeros((total - 2 * rows, LANES), jnp.float32)
            target[t, rows : 2 * rows, :] = own_tile(named, key, t)
            below, beyond = received("rows", rims, slice(row + t * low, row + t * low + low))
            target[t, rows - low : rows, :] = below
            target[t, 2 * rows : 2 * rows + low, :] = beyond
    coarse = targets[2]
    coarse[:, 8] = jnp.zeros(coarse.shape[:1] + coarse.shape[2:], jnp.float32)


def main_kernel(*refs):
    named = dict(zip(("fd", "fs", "fl", "cd", "cs", "cl"), refs[:6]))
    sides, corners = refs[6:8], refs[8:10]
    split_pick, weave_pick = refs[10:12]
    owns = refs[12:16]
    fine_rate, coarse_rate, plane_out, iterate_out, lines_out, message_out = refs[16:22]
    rims = refs[22:26]
    fine_x, fine_y, coarse_x, coarse_y = refs[26:30]
    mixed, planes, parted, woven, ends = refs[30:35]
    packed = dict(zip(TILE_ROWS, zip(refs[35:39], refs[39:43])))
    fine, rest, coarse, coarse_rest = (Tiles(own, rim) for own, rim in zip(owns, rims))
    slot = {key: i for i, key in enumerate(DEEP_REST)}
    coarse_slot = {key: i for i, key in enumerate(COARSE_REST)}

    for tile, (base, rows) in TILE_ROWS.items():
        rim = TILE_RIM[tile]
        own = received("columns", sides, slice(base, base + rows))
        for side in range(2):
            target = packed[tile][side]
            target[...] = jnp.zeros(target.shape, jnp.float32)
            target[rows : 2 * rows, :] = own[side]
            row = CORNERS[tile, side]
            low, high = received("corners", corners, slice(row, row + rim))
            target[rows - rim : rows, :] = low
            target[2 * rows : 2 * rows + rim, :] = high
    for key, low, high, tile, at, _, _ in ENTRIES:
        low_side, high_side = packed[tile][0][...], packed[tile][1][...]
        lane = iota(low_side.shape, 1)
        home(key, *rims)[...] = jnp.where(
            lane < high,
            turned(high_side, -at, 1),
            jnp.where(lane >= LANES - low, turned(low_side, -(at + low), 1), 0.0),
        )
    rims[2][:, 8] = jnp.zeros(rims[2].shape[:1] + rims[2].shape[2:], jnp.float32)

    for k in range(5):
        slopes(fine, fine_x, fine_y, k, 16, 16, 2, 1.0)
    for k in (5, 6, 7):
        slopes(fine, fine_x, fine_y, k, 8, 32, 3, 1.0)

    def fine_plane(k):
        above = 1 if k == 0 else k - 1
        own = [slice(t * LANES, (t + 1) * LANES) for t in range(2)]
        shear = [named["fs"][k, :, lanes] for lanes in own]
        lame = [named["fl"][k, :, lanes] for lanes in own]
        accel = acceleration(fine, fine_x, fine_y, mixed, (above, k, k + 1), 16, 16, 2, 1.0, shear, lame)
        for c in range(3):
            for t in range(2):
                fine_rate[c, k, :, own[t]] = accel[c][t] / named["fd"][k, :, own[t]]

    for k in range(6):
        fine_plane(k)

    window = slice(8, 40)
    shear = [rest[slot[("fs", (6,))], t, window, :] for t in range(3)]
    lame = [rest[slot[("fl", (6,))], t, window, :] for t in range(3)]
    accel = acceleration(fine, fine_x, fine_y, mixed, (5, 6, 7), 8, 32, 3, 1.0, shear, lame)
    for t in range(3):
        density = rest[slot[("fd", (6,))], t, window, :]
        filled = density > 0.0
        density = jnp.where(filled, density, 1.0)
        for c in range(3):
            rate = jnp.where(filled, accel[c][t] / density, 0.0)
            planes[3 + c, t, :, :] = rate
            planes[c, t, :, :] = 2.0 * fine[c, 6, t, window, :] - rest[c, t, window, :]
            if t < 2:
                fine_rate[c, 6, :, t * LANES : (t + 1) * LANES] = rate[8:24, :]
        fine_shear = rest[slot[("fs", (7,))], t, window, :]
        planes[6, t, :, :] = fine_shear
        planes[7, t, :, :] = rest[slot[("fl", (7,))], t, window, :] + 2.0 * fine_shear

    stacked = jnp.concatenate(
        [
            jnp.concatenate([planes[p, t, pl.ds(odd, 16, stride=2), :] for t in range(3)], axis=1)
            for p in range(8)
            for odd in range(2)
        ],
        axis=0,
    )
    parted[...] = exact_dot(stacked, split_pick[...])

    def four(p):
        return tuple(
            [
                parted[p * 32 + odd_x * 16 : p * 32 + odd_x * 16 + 16, (odd_y * 2 + t) * LANES : (odd_y * 2 + t + 1) * LANES]
                for t in range(2)
            ]
            for odd_x in range(2)
            for odd_y in range(2)
        )

    for k in range(8):
        slopes(coarse, coarse_x, coarse_y, k, 4, 16, 2, 2.0)
    coarse_x[8] = jnp.zeros(coarse_x.shape[1:], jnp.float32)
    coarse_y[8] = jnp.zeros(coarse_y.shape[1:], jnp.float32)

    def coarse_plane(k):
        shear = [named["cs"][k]]
        lame = [named["cl"][k]]
        accel = acceleration(coarse, coarse_x, coarse_y, mixed, (k - 1, k, k + 1), 8, 8, 1, 2.0, shear, lame)
        for c in range(3):
            coarse_rate[c, k - 1] = accel[c][0] / named["cd"][k]

    for k in range(2, 8):
        coarse_plane(k)
    band = slice(4, 20)

    def coarse_pair(name, k):
        return [coarse_rest[coarse_slot[(name, (k,))], t, band, :] for t in range(2)]

    shear, lame, density = coarse_pair("cs", 1), coarse_pair("cl", 1), coarse_pair("cd", 1)
    accel = acceleration(coarse, coarse_x, coarse_y, mixed, (0, 1, 2), 4, 16, 2, 2.0, shear, lame)
    below_rate = [[], [], []]
    for c in range(3):
        for t in range(2):
            filled = density[t] > 0.0
            rate = jnp.where(filled, accel[c][t] / jnp.where(filled, density[t], 1.0), 0.0)
            below_rate[c].append(rate)
        coarse_rate[c, 0] = below_rate[c][0][4:12, :]

    shear, lame = coarse_pair("cs", 0), coarse_pair("cl", 0)
    row = iota((16, LANES), 0) + (lax.axis_index("gx") * 8 - 4)
    lane = iota((16, LANES), 1) + lax.axis_index("gy") * LANES
    column = [lane, jnp.where(iota((16, LANES), 1) < 64, lane + LANES, lane - LANES)]
    extent = (lax.axis_size("gx") * 8, lax.axis_size("gy") * LANES)
    fine_moduli = (four(6), four(6), four(7))
    coarse_moduli = (shear, shear, [l + 2.0 * s for l, s in zip(lame, shear)])
    for c in range(3):
        moduli = fine_moduli[c]
        half = [0.5 * m for m in coarse_moduli[c]]
        spread = restricted(moduli)
        inverse = []
        for t in range(2):
            diagonal = half[t] + 0.5625 * spread[t]
            x, y = row, column[t]
            inside = (x >= 0) & (x < extent[0]) & (y >= 0) & (y < extent[1]) & (diagonal > 0.0)
            inverse.append(jnp.where(inside, 1.0 / jnp.where(inside, diagonal, 1.0), 0.0))
        for part in range(2):
            if part == 0:
                now = [coarse[c, 0, t, band, :] for t in range(2)]
                before = [coarse_rest[coarse_slot[("cb", (c, 0))], t, band, :] for t in range(2)]
                iterate = [2.0 * a - b for a, b in zip(now, before)]
                now = [coarse[c, 1, t, band, :] for t in range(2)]
                before = [coarse_rest[coarse_slot[("cb", (c, 1))], t, band, :] for t in range(2)]
                below = [2.0 * a - b for a, b in zip(now, before)]
            else:
                iterate = [jnp.zeros((16, LANES), jnp.float32)] * 2
                below = below_rate[c]
            above = four(3 * part + c)
            fixed = restricted([[m * a for m, a in zip(ms, as_)] for ms, as_ in zip(moduli, above)])
            fixed = [h * b + f for h, b, f in zip(half, below, fixed)]

            def mismatch_of(iterate):
                stress = [[m * a for m, a in zip(ms, ps)] for ms, ps in zip(moduli, prolonged(iterate))]
                return [h * i + (s - f) for h, i, s, f in zip(half, iterate, restricted(stress), fixed)]

            mismatch = mismatch_of(iterate)
            ends[part, c] = mismatch[0]
            for _ in range(ITERS):
                iterate = [i - m * v for i, m, v in zip(iterate, mismatch, inverse)]
                mismatch = mismatch_of(iterate)
            ends[2 + part, c] = mismatch[0]
            ends[4 + part, c] = iterate[0]
            even_even, even_odd, odd_even, odd_odd = prolonged(iterate)
            at = (part * 3 + c) * 32
            woven[at : at + 16, 0:LANES] = even_even[0]
            woven[at : at + 16, LANES : 2 * LANES] = even_odd[0]
            woven[at + 16 : at + 32, 0:LANES] = odd_even[0]
            woven[at + 16 : at + 32, LANES : 2 * LANES] = odd_odd[0]

    woven[...] = exact_dot(woven[...], weave_pick[...])
    for part in range(2):
        for c in range(3):
            iterate_out[part, c] = ends[4 + part, c, 4:12, :]
            for odd in range(2):
                at = (part * 3 + c) * 32 + odd * 16 + 4
                for t in range(2):
                    plane_out[part, c, t, pl.ds(odd, 8, stride=2), :] = woven[
                        at : at + 8, t * LANES : (t + 1) * LANES
                    ]

    lines = []
    for which in range(2):
        found = []
        for c in range(3):
            begin, slope = ends[2 * which, c, 4:12, :], ends[2 * which + 1, c, 4:12, :]
            lines_out[2 * which, c] = begin
            lines_out[2 * which + 1, c] = slope
            found += [(begin, slope), (-begin, -slope)]
        lines.append(found)
    ratio = (named["fl"][...] + 2.0 * named["fs"][...]) / named["fd"][...]
    coarse_ratio = (named["cl"][...] + 2.0 * named["cs"][...]) / named["cd"][...]
    fine_peak = jnp.sqrt(jnp.full((8, LANES), jnp.max(ratio), jnp.float32))
    coarse_peak = jnp.sqrt(jnp.full((8, LANES), jnp.max(coarse_ratio), jnp.float32))
    peak = jnp.max(jnp.maximum(fine_peak, 0.5 * coarse_peak))
    message, flag = envelopes(lines[0], lines[1], peak)
    message_out[...] = jnp.broadcast_to(sealed(message, peak, flag), message_out.shape)


def merge_kernel(received, message_out):
    first, last, peak, flag = opened(received)
    message, full = envelopes(first, last, peak)
    message_out[...] = jnp.broadcast_to(sealed(message, peak, jnp.maximum(flag, full)), message_out.shape)


def final_kernel(
    received, fn, fb, cn, cb, fine_rate, coarse_rate, plane, iterate, fine_out, coarse_out, ratio_out, square_out, flag_out
):
    first, last, peak, flag = opened(received)
    step = 0.3 / jnp.full((8, LANES), peak, jnp.float32)
    square = step * step
    first_max = largest([a + square * b for a, b in first])
    last_max = largest([a + square * b for a, b in last])
    ratio = last_max / (jnp.full((8, LANES), first_max, jnp.float32) + 1e-06)
    ratio_out[0] = jnp.max(ratio)
    square_out[0] = jnp.max(square)
    flag_out[0] = jnp.where((flag > 0.0) | (jnp.max(square) < STEP_LOW), 1, 0)
    square = square[0:1, 0:1]
    for c in range(3):
        fine_out[c, 0:7] = 2.0 * fn[c, 0:7] - fb[c, 0:7] + square * fine_rate[c]
        coarse_out[c, 1:8] = 2.0 * cn[c, 1:8] - cb[c, 1:8] + square * coarse_rate[c]
        coarse_out[c, 0] = iterate[0, c] + square * iterate[1, c]
        for t in range(2):
            fine_out[c, 7, :, t * LANES : (t + 1) * LANES] = plane[0, c, t] + square * plane[1, c, t]


def exchange(first, second, what, columns, rows):
    axis, begin = FIRST_PAIRS[what]

    def swap(value, parity):
        ups = []
        for i in range(columns):
            for j in range(rows):
                turned_parity = 1 - parity if axis == "gy" and i >= TURN else parity
                place, count, step = (j, rows, 1) if axis == "gy" else (i, columns, rows)
                if place % 2 == turned_parity and place + 1 < count:
                    ups.append((i * rows + j, i * rows + j + step))
        return lax.ppermute(value, ("gx", "gy"), ups + [(j, i) for i, j in ups])

    return swap(first, begin), swap(second, 1 - begin)


def gather_groups(columns, rows):
    ring, plane = {}, {}
    for i in range(columns):
        for j in range(rows):
            chip_y, core, z, x = i // 2 % 4, i % 2, (i // 8, j % 4), j // 4
            ring.setdefault((x, chip_y), []).append(i * rows + j)
            plane.setdefault((z, core), []).append(i * rows + j)
    return list(ring.values()), list(plane.values())


def split_matrix():
    lane = np.arange(3 * LANES)
    fine_column = np.where(lane < 320, lane, lane - 384)[:, None]
    circle = np.arange(2 * LANES)
    coarse_column = np.where(circle < 192, circle, circle - 256)[None, :]
    return np.concatenate(
        [fine_column == 2 * coarse_column, fine_column == 2 * coarse_column + 1], axis=1
    ).astype(ml_dtypes.bfloat16)


def weave_matrix():
    lane = np.arange(2 * LANES)
    target = np.where(lane < LANES, 2 * lane, 2 * (lane - LANES) + 1)[:, None]
    return (target == lane[None, :]).astype(ml_dtypes.bfloat16)


def f32(*shape):
    return jax.ShapeDtypeStruct(shape, jnp.float32)


def vm(*shape):
    return pltpu.VMEM(shape, jnp.float32)


def make_shards(columns, rows):
    ring, plane_groups = gather_groups(columns, rows)
    axes = ("gx", "gy")

    def shards(*args):
        in_vmem = pl.BlockSpec(memory_space=pltpu.VMEM)
        in_smem = pl.BlockSpec(memory_space=pltpu.SMEM)
        in_hbm = pl.BlockSpec(memory_space=pltpu.HBM)

        def call(kernel, ins, outs, scratch=(), out_specs=None, cost=None, limit=8):
            return pl.pallas_call(
                kernel,
                out_shape=outs,
                in_specs=ins,
                out_specs=out_specs or ([in_vmem] * len(outs) if isinstance(outs, tuple) else in_vmem),
                scratch_shapes=list(scratch),
                compiler_params=pltpu.CompilerParams(vmem_limit_bytes=limit * 1024 * 1024),
                cost_estimate=cost,
            )

        fn, fb, _, _, _, cn, cb, _, _, _ = args
        first_side, second_side, first_rim, second_rim = call(
            pack,
            [in_hbm] * 10,
            (pltpu.VMEM((PACKED_ROWS, LANES), jnp.float32),) * 2 + (pltpu.VMEM((RIM_ROWS, LANES), jnp.float32),) * 2,
            [vm(*a.shape) for a in args] + [pltpu.SemaphoreType.DMA((len(PACK_SOURCES),))],
        )(*[pltpu.with_memory_space_constraint(a, pltpu.HBM) for a in args])
        sides = exchange(first_side, second_side, "columns", columns, rows)
        rims = exchange(first_rim, second_rim, "rows", columns, rows)
        first, second = call(
            pack_corners,
            [in_vmem] * 2,
            (f32(CORNER_ROWS, LANES),) * 2,
            cost=pl.CostEstimate(flops=10**12, bytes_accessed=10**9, transcendentals=0),
        )(*sides)
        corners = exchange(first, second, "corners", columns, rows)
        ring_size, plane_size = len(ring[0]), len(plane_groups[0])
        own_shapes = ((3, 8, 2, 48, LANES), (8, 2, 48, LANES), (3, 9, 1, 24, LANES), (11, 1, 24, LANES))
        owns = call(place_kernel, [in_vmem] * 12, tuple(f32(*shape) for shape in own_shapes))(
            *args, *[pltpu.with_memory_space_constraint(rim, pltpu.VMEM) for rim in rims]
        )
        outs = (
            f32(3, 7, 16, 256),
            f32(3, 7, 8, 128),
            f32(2, 3, 2, 16, 128),
            f32(2, 3, 8, 128),
            f32(4, 3, 8, 128),
            f32(ring_size, LANES),
        )
        scratch = [vm(*shape[:-3], *shape[-2:]) for shape in own_shapes] + [
            vm(8, 3, 48, LANES),
            vm(8, 3, 48, LANES),
            vm(9, 2, 24, LANES),
            vm(9, 2, 24, LANES),
            vm(3, 48, LANES),
            vm(8, 3, 32, LANES),
            vm(256, 512),
            vm(192, 256),
            vm(6, 3, 16, LANES),
        ]
        scratch += [vm(48, LANES), vm(48, LANES), vm(24, LANES), vm(24, LANES)] * 2
        fine_rate, coarse_rate, plane, iterate, lines, message = call(main_kernel, [in_vmem] * 16, outs, scratch)(
            *args[2:5],
            *args[7:],
            *sides,
            *corners,
            jnp.asarray(split_matrix()),
            jnp.asarray(weave_matrix()),
            *owns,
        )
        received = lax.all_to_all(message, axes, 0, 0, tiled=True, axis_index_groups=ring)
        message = call(merge_kernel, [in_vmem], f32(plane_size, LANES))(received)
        received = lax.all_to_all(message, axes, 0, 0, tiled=True, axis_index_groups=plane_groups)
        fine_next, coarse_next, ratio, square, flag = call(
            final_kernel,
            [in_vmem] * 9,
            (f32(*fn.shape), f32(*cn.shape), f32(1), f32(1), jax.ShapeDtypeStruct((1,), jnp.int32)),
            out_specs=[in_vmem] * 2 + [in_smem] * 3,
        )(received, fn, fb, cn, cb, fine_rate, coarse_rate, plane, iterate)

        def plain():
            values = jnp.abs(lines[0::2] + square[0] * lines[1::2])
            tops = lax.pmax(jnp.max(values, axis=(1, 2, 3)), axes)
            return tops[1] / (tops[0] + 1e-06)

        reduction = lax.cond(flag[0] > 0, plain, lambda: ratio[0])
        return fine_next, coarse_next, reduction

    return shards


def solution(mesh):
    placed = (
        P(None, None, "gx", "gy"),
        P(None, None, "gx", "gy"),
        P(None, "gx", "gy"),
        P(None, "gx", "gy"),
        P(None, "gx", "gy"),
        P(None, None, "gx", "gy"),
        P(None, None, "gx", "gy"),
        P(None, "gx", "gy"),
        P(None, "gx", "gy"),
        P(None, "gx", "gy"),
    )
    return jax.shard_map(
        make_shards(mesh.shape["gx"], mesh.shape["gy"]),
        mesh=mesh,
        in_specs=placed,
        out_specs=(P(None, None, "gx", "gy"), P(None, None, "gx", "gy"), P()),
        check_vma=False,
    )
```
